32 devices in a mesh: dp: 2 (over core), expert: 16 (over z, y, x).
Axes of the slice: x: 2, y: 2, z: 4, core: 2. Of those that a mesh axis runs over, the one named last changes fastest.
Arguments:
- hidden_saved: bfloat16 [2, 16, 448, 1024], P('dp', 'expert'), may hold values from -6 to 6
- down_weight: bfloat16 [16, 1024, 3584], P('expert', 'dp'), may hold values from -0.1875 to 0.1875
- route_device: int32 [4096, 4], P(('dp', 'expert')), may hold values from 0 to 15, all different within a row; in each aligned block of 128 rows (0 to 127, 128 to 255, ...) at most 40 rows name the same one
- replica_flag: int32 [4096, 4], P(('dp', 'expert')), may hold values 0 or 1
- gate_values: float32 [4096, 4], P(('dp', 'expert')), may hold values from 0.05 to 1
- grad_out: bfloat16 [4096, 3584], P(('dp', 'expert')), may hold values from -6 to 6
Outputs:
- layer_out: bfloat16 [4096, 3584], P(('dp', 'expert'))
- grad_hidden: bfloat16 [2, 16, 448, 1024], P('dp', 'expert')
- grad_weight: bfloat16 [16, 1024, 3584], P('expert', 'dp')
The draws below stay inside these ranges and needn't reach their ends.
Inputs may be any that keep to these rules, and one draw needn't show every extreme that they name: `route_device`: the 4 numbers of a row differ; the rows of one device name any one device at most 40 times, and some device exactly 40 times.
All inputs are finite; a program needn't handle non-finite values. No bound on the sum of `replica_flag` on one device may be relied on, other than what follows from the above.
Results may differ from the reference program's by a relative error of at most 0.012.
Values may be sent and summed in bfloat16 or wider, within the bound.
No kernel may reach another device: no remote copies, remote signals or barrier semaphores. Data moves between devices by JAX's collectives and lax.ppermute only.
A program may use at most 192 MiB of HBM per device.

```python
import math
import jax
import jax.numpy as jnp
import numpy as np
from jax import lax

D = 3584
HID = 1024
TOP = 4
TOK_DEV = 128
EXPERTS = 16
TOKENS = 4096
SEND_CAP = 40
CAP_MAIN = 384
CAP_SPARE = 64
SLOTS = 448
N_DP = 2
N_EXPERT = 16


def with_ends(result, stream_key, least, largest):
    spot = [jax.random.randint(jax.random.fold_in(stream_key, axis), (), 0, length) for axis, length in enumerate(result.shape)]
    widest = result.shape.index(max(result.shape))
    beside = spot[:widest] + [(spot[widest] + 1) % result.shape[widest]] + spot[widest + 1:]
    return result.at[tuple(spot)].set(least).at[tuple(beside)].set(largest)


def steps_of(rng, dims, split, low, top_value):
    gain, own = 1.0, jax.random.fold_in(rng, 6)
    for axis_at, blocks in split:
        steps = jnp.exp(jax.random.uniform(jax.random.fold_in(own, axis_at), (blocks,), jnp.float32, low / len(split), top_value / len(split)))
        gain = gain * jnp.repeat(steps, dims[axis_at] // blocks).reshape([-1 if axis == axis_at else 1 for axis in range(len(dims))])
    return gain


def shared_out(stream_key, own, number, rows, count, top, reach, lean):
    sequence = jax.random.permutation(stream_key, count)
    heavy_load, usual = load_shares(count, rows * top, reach, lean, True), load_shares(count, rows * top, reach, lean, False)
    places = jnp.arange(count)

    def named(sizes, rotation):
        used = int((sizes > 0).sum())
        fixed = max(1, used // 4)
        moved = fixed + (places - fixed + rotation * (used - fixed)) % max(1, count - fixed)
        return jnp.zeros((count,), jnp.int32).at[sequence[jnp.where(places < fixed, places, moved)]].set(jnp.asarray(sizes, jnp.int32))

    sizes = jnp.where(number % 4 == 0, named(heavy_load, number // 4), named(usual, number - number // 4 - 1))
    mixed = jax.random.permutation(jax.random.fold_in(own, 3), count)
    source_of, taker = mixed[0:count // 2 * 2:2], mixed[1:count // 2 * 2:2]
    slack = jnp.minimum(sizes[source_of] - 1, reach - sizes[taker]) // 2
    slack = jnp.where((source_of == sequence[0]) | (taker == sequence[0]) | (sizes[taker] == 0), 0, jnp.maximum(slack, 0))
    moved = jax.random.randint(jax.random.fold_in(own, 4), (count // 2,), 0, 1 << 20) % (slack + 1)
    sizes = sizes.at[source_of].add(-moved).at[taker].add(moved)
    items = jnp.searchsorted(jnp.cumsum(sizes), jnp.arange(rows * top), side="right").astype(jnp.int32)
    table = items.reshape(top, rows).T
    table = table[jax.random.permutation(jax.random.fold_in(own, 1), rows)]
    rotation = jax.random.randint(jax.random.fold_in(own, 2), (rows, 1), 0, top)
    return jnp.take_along_axis(table, (jnp.arange(top)[None, :] + rotation) % top, axis=1)


def load_shares(amount, total, limit, skew, full):
    loads = [(1 << 20) // math.isqrt(rank ** skew) + 1 for rank in range(1, amount + 1)]
    largest = limit if full else min(limit, max(-(-total // amount), total * loads[0] // sum(loads)))
    least = 1 if total - largest >= amount - 1 else 0
    counts, rest = [largest] + [least] * (amount - 1), total - largest - least * (amount - 1)
    while rest > 0:
        free = [i for i in range(1, amount) if counts[i] < largest] or [i for i in range(1, amount) if counts[i] < limit]
        whole, left = sum([loads[i] for i in free]), rest
        for i in free:
            addition = min(limit - counts[i], max(1, left * loads[i] // whole), rest)
            counts[i] = counts[i] + addition
            rest = rest - addition
    return np.array(counts)


def bell_draw(own_key, shape, spread, reach, cuts=(), kind=jnp.bfloat16):
    array = spread * jax.random.normal(own_key, shape, jnp.float32)
    if cuts:
        array = array * steps_of(own_key, shape, cuts, -0.22, 0.18)
    return jnp.clip(array, -reach, reach).astype(kind)


def setup_inputs(seed: int = 0) -> dict:
    streams_of = jax.random.split(jax.random.key(seed), 7)
    hidden_saved = bell_draw(streams_of[0], (N_DP, N_EXPERT, SLOTS, HID), 1.0, 6.0, ((0, 2), (1, 16)))
    down_weight = bell_draw(streams_of[1], (EXPERTS, HID, D), HID ** -0.5, 0.1875, ((0, 16), (1, 2)))
    route_device_keys = jax.random.split(jax.random.fold_in(streams_of[2], 1), TOKENS // TOK_DEV)
    route_device_turns = jax.random.permutation(jax.random.fold_in(streams_of[2], 3), TOKENS // TOK_DEV)
    route_device = jax.vmap(lambda own, number: shared_out(jax.random.fold_in(streams_of[2], 2), own, number, TOK_DEV, N_EXPERT, TOP, SEND_CAP, 1))(route_device_keys, route_device_turns).reshape((TOKENS, TOP))
    replica_flag = with_ends((jax.random.randint(streams_of[3], (TOKENS, TOP), 0, 4) < 1).astype(jnp.int32), jax.random.fold_in(streams_of[3], 1), 0, 1)
    gate_values = jnp.clip(jnp.exp(math.log(1.0) - 2.9957323 * jax.random.uniform(streams_of[4], (TOKENS, TOP), jnp.float32) ** steps_of(streams_of[4], (TOKENS, TOP), ((0, 32),), -0.2, 0.2)), 0.05, 1.0)
    grad_out = bell_draw(streams_of[5], (TOKENS, D), 1.0, 6.0, ((0, 32),))
    return {"hidden_saved": hidden_saved, "down_weight": down_weight, "route_device": route_device, "replica_flag": replica_flag, "gate_values": gate_values, "grad_out": grad_out}


def exclusive_rank(labels, classes):
    onehot = (labels[:, None] == jnp.arange(classes, dtype=jnp.int32)[None, :]).astype(jnp.int32)
    earlier = jnp.cumsum(onehot, axis=0) - onehot
    return lax.optimization_barrier(jnp.sum(earlier * onehot, axis=1)).astype(jnp.int32)

def spare_routes(route_device, replica_flag, axis_count):
    half_axis = axis_count // 2
    partner = (route_device + half_axis) % axis_count
    clash_mask = jnp.any(partner[:, :, None] == route_device[:, None, :], axis=2)
    return jnp.where((replica_flag == 1) & jnp.logical_not(clash_mask), 1, 0).astype(jnp.int32)

def reference(hidden_saved, down_weight, route_device, replica_flag, gate_values, grad_out):
    half_axis = N_EXPERT // 2
    slot_total = CAP_MAIN + CAP_SPARE
    owners = N_DP * N_EXPERT
    spare_mask = spare_routes(route_device, replica_flag, N_EXPERT)
    route_key = (route_device * 2 + spare_mask).reshape(N_DP, N_EXPERT * TOK_DEV * TOP)
    route_rank = lax.map(lambda key_list: exclusive_rank(key_list, 2 * N_EXPERT), route_key).reshape(TOKENS, TOP)
    cap_limit = jnp.where(spare_mask == 1, CAP_SPARE, CAP_MAIN)
    kept_mask = route_rank < cap_limit
    route_slot = route_rank + spare_mask * CAP_MAIN
    batch_ids = (jnp.arange(TOKENS, dtype=jnp.int32) // (N_EXPERT * TOK_DEV))[:, None]
    flat_index = ((batch_ids * N_EXPERT + route_device) * slot_total + route_slot).astype(jnp.int32)
    safe_index = jnp.where(kept_mask, flat_index, 0)
    drop_index = jnp.where(kept_mask, flat_index, owners * slot_total)

    def slot_weights(owner):
        device_id = owner % N_EXPERT
        return (down_weight[device_id], down_weight[(device_id + half_axis) % N_EXPERT])

    def forward_rows(owner):
        main_weight, side_weight = slot_weights(owner)
        saved_rows = hidden_saved[owner // N_EXPERT, owner % N_EXPERT]
        main_out = jnp.dot(saved_rows[:CAP_MAIN], main_weight, preferred_element_type=jnp.float32)
        side_out = jnp.dot(saved_rows[CAP_MAIN:], side_weight, preferred_element_type=jnp.float32)
        return jnp.concatenate([main_out, side_out], axis=0).astype(jnp.bfloat16)
    owner_ids = jnp.arange(owners, dtype=jnp.int32)
    out_rows = lax.map(forward_rows, owner_ids).reshape(owners * slot_total, D)
    gate_kept = jnp.where(kept_mask, gate_values, jnp.zeros_like(gate_values))

    def combine(block):
        index_block, gate_block = block
        picked = out_rows[index_block].astype(jnp.float32)
        return lax.optimization_barrier(jnp.sum(picked * gate_block[:, :, None], axis=1)).astype(jnp.bfloat16)
    layer_out = lax.map(combine, (safe_index.reshape(-1, TOK_DEV, TOP), gate_kept.reshape(-1, TOK_DEV, TOP))).reshape(TOKENS, D)
    route_grad = (gate_values[:, :, None] * grad_out.astype(jnp.float32)[:, None, :]).astype(jnp.bfloat16).reshape(TOKENS * TOP, D)
    slot_grad = jnp.zeros((owners * slot_total, D), jnp.bfloat16).at[drop_index.reshape(-1)].set(route_grad, mode='drop')
    slot_grad = slot_grad.reshape(owners, slot_total, D)

    def backward_rows(owner):
        main_weight, side_weight = slot_weights(owner)
        grad_rows = slot_grad[owner]
        contract = (((1,), (1,)), ((), ()))
        main_back = lax.dot_general(grad_rows[:CAP_MAIN], main_weight, contract, preferred_element_type=jnp.float32)
        side_back = lax.dot_general(grad_rows[CAP_MAIN:], side_weight, contract, preferred_element_type=jnp.float32)
        return jnp.concatenate([main_back, side_back], axis=0).astype(jnp.bfloat16)
    grad_hidden = lax.map(backward_rows, owner_ids).reshape(N_DP, N_EXPERT, slot_total, HID)

    def weight_grad(expert_id):
        partner = (expert_id + half_axis) % N_EXPERT
        contract = (((0,), (0,)), ((), ()))
        main_sum = jnp.zeros((HID, D), jnp.float32)
        spare_sum = jnp.zeros((HID, D), jnp.float32)
        for batch_pos in range(N_DP):
            own_slot = batch_pos * N_EXPERT + expert_id
            other_slot = batch_pos * N_EXPERT + partner
            main_part = lax.dot_general(hidden_saved[batch_pos, expert_id][:CAP_MAIN], slot_grad[own_slot][:CAP_MAIN], contract, preferred_element_type=jnp.float32)
            spare_part = lax.dot_general(hidden_saved[batch_pos, partner][CAP_MAIN:], slot_grad[other_slot][CAP_MAIN:], contract, preferred_element_type=jnp.float32)
            main_sum = main_sum + lax.optimization_barrier(main_part.astype(jnp.bfloat16)).astype(jnp.float32)
            spare_sum = spare_sum + lax.optimization_barrier(spare_part.astype(jnp.bfloat16)).astype(jnp.float32)
        spare_total = lax.optimization_barrier(spare_sum.astype(jnp.bfloat16)).astype(jnp.float32)
        return (main_sum + spare_total).astype(jnp.bfloat16)
    grad_weight = lax.map(weight_grad, jnp.arange(EXPERTS, dtype=jnp.int32))
    return (layer_out, grad_hidden, grad_weight)
```

```python
import jax
import jax.numpy as jnp
from jax import lax
from jax.sharding import PartitionSpec as P

F32, BF16, I32 = jnp.float32, jnp.bfloat16, jnp.int32


def swapped(value, axis, distance):
    count = lax.axis_size(axis)
    pairs = [(source, (source + distance) % count) for source in range(count)]
    return lax.ppermute(value, axis, pairs)


def earlier_in_row(flags):
    length = flags.shape[-1]
    before = jnp.arange(length)[:, None] < jnp.arange(length)[None, :]
    return jnp.dot(flags.astype(BF16), before.astype(BF16), preferred_element_type=F32).astype(I32)


def earlier_in_all(flags):
    rows = flags.shape[0]
    totals = jnp.sum(flags.astype(I32), axis=1)
    before = jnp.arange(rows)[None, :] < jnp.arange(rows)[:, None]
    offsets = jnp.sum(jnp.where(before, totals[None, :], 0), axis=1)
    return earlier_in_row(flags) + offsets[:, None]


def product(left, right, left_dim=1, right_dim=0):
    contract = (((left_dim,), (right_dim,)), ((), ()))
    return lax.dot_general(left, right, contract, preferred_element_type=F32)


def local(hidden_saved, down_weight, route_device, replica_flag, gate_values, grad_out):
    count = lax.axis_size("expert")
    half = count // 2
    tok, top = route_device.shape
    width = grad_out.shape[1]
    cap = 5 * tok * top // (4 * count)
    cap_main = 3 * tok * top // 4
    saved = hidden_saved[0, 0]
    slots, hid = saved.shape
    rows_half = hid // 2
    me = lax.axis_index("expert")
    core = lax.axis_index("dp")
    my_half = me // half
    first = my_half * half
    groups = [list(range(half)), list(range(half, count))]

    own_weight = down_weight[0]
    devices = route_device.T
    partner = (devices + half) % count
    clash = jnp.any(partner[:, None, :] == devices[None, :, :], axis=1)
    spare = (replica_flag.T == 1) & jnp.logical_not(clash)
    codes = devices * 2 + spare.astype(I32)
    meta = jnp.concatenate([codes.astype(F32), gate_values.T], axis=0)
    metas = lax.all_gather(meta, "expert", axis=0, tiled=False)
    mirror_grad = swapped(grad_out, "expert", half)
    other_weight = swapped(own_weight, "dp", 1)
    spare_hidden = swapped(saved[cap_main:], "expert", half)

    codes_all = metas[:, :top].astype(I32)
    gates_all = metas[:, top:]

    def outgoing_places(codes_of):
        dests = first + jnp.arange(half, dtype=I32)
        hits = (codes_of[None] >> 1) == dests[:, None, None]
        hit = jnp.any(hits, axis=1)
        place = earlier_in_row(hit)
        chosen = hit[:, None, :] & (place[:, None, :] == jnp.arange(cap, dtype=I32)[None, :, None])
        return hits, chosen

    mirror_at = (me + half) % count
    mirror_codes = lax.dynamic_index_in_dim(codes_all, mirror_at, 0, False)
    mirror_gates = lax.dynamic_index_in_dim(gates_all, mirror_at, 0, False)
    own_gates = gate_values.T
    hits_own, chosen_own = outgoing_places(codes)
    hits_mir, chosen_mir = outgoing_places(mirror_codes)

    def dispatch(chosen, rows):
        packed = product(chosen.reshape(half * cap, tok).astype(BF16), rows).astype(BF16)
        return lax.all_to_all(
            packed.reshape(half, cap, width), "expert", 0, 0, axis_index_groups=groups, tiled=True
        ).reshape(half * cap, width)

    arrived_own = dispatch(chosen_own, grad_out)
    arrived_mir = dispatch(chosen_mir, mirror_grad)

    at_main = jnp.any(codes_all == 2 * me, axis=1)
    at_spare = jnp.any(codes_all == 2 * me + 1, axis=1)
    here = at_main | at_spare
    rank_main = earlier_in_all(at_main)
    rank_spare = earlier_in_all(at_spare)
    slot = jnp.where(
        at_main & (rank_main < cap_main),
        rank_main,
        jnp.where(at_spare & (rank_spare < slots - cap_main), rank_spare + cap_main, slots),
    )
    place_here = earlier_in_row(here)
    gate_here = jnp.sum(jnp.where((codes_all >> 1) == me, gates_all, 0.0), axis=1)
    is_place = here[:, None, :] & (place_here[:, None, :] == jnp.arange(cap, dtype=I32)[None, :, None])
    slot_row = slots - jnp.sum(jnp.where(is_place, slots - slot[:, None, :], 0), axis=2)
    gate_row = jnp.sum(jnp.where(is_place, gate_here[:, None, :], 0.0), axis=2)
    by_half = lambda table: table.reshape(2, half * cap)
    slot_row, gate_row = by_half(slot_row), by_half(gate_row)
    flip = lambda table: jnp.where(my_half == 0, table, table[::-1])
    slot_row, gate_row = flip(slot_row), flip(gate_row)
    slot_ids = jnp.arange(slots, dtype=I32)
    place_own = slot_row[0][None, :] == slot_ids[:, None]
    place_mir = slot_row[1][None, :] == slot_ids[:, None]
    gate_slot = jnp.sum(jnp.where(place_own, gate_row[0][None, :], 0.0), axis=1) + jnp.sum(
        jnp.where(place_mir, gate_row[1][None, :], 0.0), axis=1
    )
    place_own = place_own.astype(BF16)
    place_mir = place_mir.astype(BF16)

    weight = jnp.concatenate([own_weight, other_weight], axis=0)
    hidden = jnp.concatenate([saved[:cap_main], spare_hidden], axis=0)
    swap = jnp.concatenate([hidden[:, rows_half:], hidden[:, :rows_half]], axis=1)
    hidden = jnp.where(core == 0, hidden, swap)
    out_main = product(hidden[:cap_main], weight).astype(BF16)
    out_spare = product(hidden[cap_main:], weight).astype(BF16)
    out_spare = swapped(out_spare, "expert", half)
    out_slots = jnp.concatenate([out_main, out_spare], axis=0)

    def give_back(place):
        packed = product(place, out_slots, 0, 0).astype(BF16)
        return lax.all_to_all(
            packed.reshape(half, cap, width), "expert", 0, 0, axis_index_groups=groups, tiled=True
        ).reshape(half * cap, width)

    returned_mir = give_back(place_mir)
    returned_own = give_back(place_own)

    def combine(hits, chosen, gates, rows):
        gate_of = jnp.sum(jnp.where(hits, gates[None], 0.0), axis=1)
        mix = jnp.where(chosen, gate_of[:, None, :], 0.0).reshape(half * cap, tok)
        high = mix.astype(BF16)
        low = (mix - high.astype(F32)).astype(BF16)
        return product(high, rows, 0, 0) + product(low, rows, 0, 0)

    part_mir = combine(hits_mir, chosen_mir, mirror_gates, returned_mir).astype(BF16)
    part_back = swapped(part_mir, "expert", half)
    part_own = combine(hits_own, chosen_own, own_gates, returned_own)
    layer_out = (part_own + part_back.astype(F32)).astype(BF16)

    slot_grad = product(place_own, arrived_own) + product(place_mir, arrived_mir)
    slot_grad = (slot_grad * gate_slot[:, None]).astype(BF16)
    spare_grad = swapped(slot_grad[cap_main:], "expert", half)
    grads = jnp.concatenate([slot_grad[:cap_main], spare_grad], axis=0)
    far_part = product(hidden[:, rows_half:], grads, 0, 0).astype(BF16)
    far_part = swapped(far_part, "dp", 1)
    back = product(grads, weight, 1, 1).astype(BF16)
    swap_back = jnp.concatenate([back[:, rows_half:], back[:, :rows_half]], axis=1)
    back = jnp.where(core == 0, back, swap_back)
    back_spare = swapped(back[cap_main:], "expert", half)
    grad_hidden = jnp.concatenate([back[:cap_main], back_spare], axis=0)
    near_part = product(hidden[:, :rows_half], grads, 0, 0)
    grad_weight = (near_part + far_part.astype(F32)).astype(BF16)
    return (layer_out, grad_hidden[None, None], grad_weight[None])


def solution(mesh):
    in_specs = (
        P("dp", "expert", None, None),
        P("expert", "dp", None),
        P(("dp", "expert"), None),
        P(("dp", "expert"), None),
        P(("dp", "expert"), None),
        P(("dp", "expert"), None),
    )
    out_specs = (P(("dp", "expert"), None), P("dp", "expert", None, None), P("expert", "dp", None))
    return jax.shard_map(local, mesh=mesh, in_specs=in_specs, out_specs=out_specs, check_vma=False)
```

```python
import functools
import jax
import jax.numpy as jnp
from jax import lax
from jax.experimental import pallas as pl
from jax.experimental.pallas import tpu as pltpu
from jax.sharding import PartitionSpec as P

F32, BF16, I32 = jnp.float32, jnp.bfloat16, jnp.int32
LANES = 128
VMEM_LIMIT = 40 * 1024 * 1024


def swapped(value, axis, distance):
    count = lax.axis_size(axis)
    pairs = [(source, (source + distance) % count) for source in range(count)]
    return lax.ppermute(value, axis, pairs)


def dot(left, right, left_dim=1, right_dim=0):
    contract = (((left_dim,), (right_dim,)), ((), ()))
    return lax.dot_general(left, right, contract, preferred_element_type=F32)


def iota(shape, dim):
    return lax.broadcasted_iota(I32, shape, dim).astype(F32)


def row_of(rows, cap, lanes):
    row = iota((rows, lanes), 0)
    group = jnp.floor((row + 0.5) * (1.0 / cap))
    return group, row - group * cap


def before_mask(size):
    return (iota((size, size), 0) < iota((size, size), 1)).astype(BF16)


def call(body, grid, in_specs, out_specs, out_shape, scratch, *operands):
    return pl.pallas_call(
        body,
        grid=(grid,),
        in_specs=in_specs,
        out_specs=out_specs,
        out_shape=out_shape,
        scratch_shapes=scratch,
        compiler_params=pltpu.CompilerParams(vmem_limit_bytes=VMEM_LIMIT),
        cost_estimate=pl.CostEstimate(flops=0, bytes_accessed=0, transcendentals=0),
    )(*operands)


def whole_block(shape):
    return pl.BlockSpec(shape, lambda step: (0,) * len(shape))


def columns(rows, tile):
    return pl.BlockSpec((rows, tile), lambda step: (0, step))


def pack_kernel(cap, top, half, mirrored, meta_ref, tokens_ref, packed_ref, mix_ref, sel_ref, gate_ref):
    rows, tok = sel_ref.shape

    @pl.when(pl.program_id(0) == 0)
    def _():
        me = lax.axis_index("expert")
        source = lax.rem(me + half, 2 * half) if mirrored else 0
        first = (lax.div(me, half) * half).astype(F32)
        row = meta_ref[pl.ds(source, 1), :]
        dest = iota((LANES, tok), 0)
        inside = dest < half
        dest = dest + first
        hit = jnp.zeros((LANES, tok), F32)
        gate = jnp.zeros((LANES, tok), F32)
        for k in range(top):
            device = jnp.floor(row[:, k * tok : (k + 1) * tok] * 0.5)
            named = (dest == device) & inside
            hit = jnp.where(named, 1.0, hit)
            gate = jnp.where(named, row[:, (top + k) * tok : (top + k + 1) * tok], gate)
        place = dot(hit.astype(BF16), before_mask(tok))
        place = jnp.where(hit > 0.5, place, -1.0).astype(BF16)
        group, at = row_of(rows, cap, LANES)
        spread = (iota((rows, LANES), 1) == group).astype(BF16)
        chosen = dot(spread, place) == at
        high = gate.astype(BF16)
        rest = gate - high.astype(F32)
        mid = rest.astype(BF16)
        low = (rest - mid.astype(F32)).astype(BF16)
        high, mid, low = dot(spread, high), dot(spread, mid), dot(spread, low)
        none = jnp.zeros((rows, tok), F32)
        sel_ref[...] = jnp.where(chosen, 1.0, none).astype(BF16)
        scale = jnp.sum(jnp.where(chosen, high + mid + low, none), axis=1, keepdims=True)
        gate_ref[...] = jnp.broadcast_to(scale, (rows, LANES))
        mix_ref[:, :tok] = jnp.where(chosen, high, none).astype(BF16)
        mix_ref[:, tok:] = jnp.where(chosen, mid, none).astype(BF16)

    packed = dot(sel_ref[...], tokens_ref[...]) * gate_ref[:, :1]
    packed_ref[...] = packed.astype(BF16)


def pack(meta, tokens, cap, top, half, mirrored, tile):
    tok, width = tokens.shape
    rows = half * cap
    return call(
        functools.partial(pack_kernel, cap, top, half, mirrored),
        width // tile,
        [whole_block(meta.shape), columns(tok, tile)],
        [columns(rows, tile), whole_block((rows, 2 * tok))],
        [jax.ShapeDtypeStruct((rows, width), BF16), jax.ShapeDtypeStruct((rows, 2 * tok), BF16)],
        [pltpu.VMEM((rows, tok), BF16), pltpu.VMEM((rows, LANES), F32)],
        meta,
        tokens,
    )


def stack_hidden(hidden_ref, spare_ref, out_ref, order):
    main = hidden_ref.shape[0] - spare_ref.shape[0]
    half = hidden_ref.shape[1] // 2
    core = lax.axis_index("dp")
    for at, flip in enumerate(order):
        start = pl.multiple_of((1 - core if flip else core) * half, LANES)
        out_ref[:main, at * half : (at + 1) * half] = hidden_ref[:main, pl.ds(start, half)]
        out_ref[main:, at * half : (at + 1) * half] = spare_ref[:, pl.ds(start, half)]


def out_kernel(hidden_ref, spare_ref, near_ref, far_ref, main_out, spare_out, stack_ref):
    @pl.when(pl.program_id(0) == 0)
    def _():
        stack_hidden(hidden_ref, spare_ref, stack_ref, (False, True))

    main, half = main_out.shape[0], near_ref.shape[0]
    total = dot(stack_ref[:, :half], near_ref[...]) + dot(stack_ref[:, half:], far_ref[...])
    total = total.astype(BF16)
    main_out[...] = total[:main]
    spare_out[...] = total[main:]


def project(hidden, spare_hidden, near, far, tile):
    half, width = near.shape
    slots, hid = hidden.shape
    spare = spare_hidden.shape[0]
    return call(
        out_kernel,
        width // tile,
        [whole_block(hidden.shape), whole_block(spare_hidden.shape), columns(half, tile), columns(half, tile)],
        [columns(slots - spare, tile), columns(spare, tile)],
        [jax.ShapeDtypeStruct((slots - spare, width), BF16), jax.ShapeDtypeStruct((spare, width), BF16)],
        [pltpu.VMEM((slots, hid), BF16)],
        hidden,
        spare_hidden,
        near,
        far,
    )


def give_kernel(cap, top, half, mirrored, metas_ref, main_ref, spare_ref, packed_ref, slot_ref):
    rows, slots = slot_ref.shape
    count = 2 * half
    tok = metas_ref.shape[1] // (2 * top)
    main, spare = main_ref.shape[0], spare_ref.shape[0]

    @pl.when(pl.program_id(0) == 0)
    def _():
        me = lax.axis_index("expert")
        base = lax.div(me, half) * half
        base = (lax.rem(base + half, count) if mirrored else base).astype(F32)
        mine = me.astype(F32)
        other = lax.rem(me + half, count).astype(F32)
        none = jnp.zeros((count, tok), F32)
        here, flag, clash = none, none, none
        for k in range(top):
            code = metas_ref[:, k * tok : (k + 1) * tok]
            device = jnp.floor(code * 0.5)
            here = jnp.where(device == mine, 1.0, here)
            flag = jnp.where(device == mine, code - 2.0 * device, flag)
            clash = jnp.where(device == other, 1.0, clash)
        at_spare = here * flag * (1.0 - clash)
        at_main = here - at_spare
        before = before_mask(tok)
        ones = jnp.ones((tok, LANES), BF16)
        lower = (iota((count, count), 1) < iota((count, count), 0)).astype(BF16)

        def rank(flags):
            flags = flags.astype(BF16)
            return dot(flags, before) + dot(lower, dot(flags, ones).astype(BF16))

        rank_main, rank_spare = rank(at_main), rank(at_spare)
        slot = jnp.where((at_main > 0.5) & (rank_main < main), rank_main + 1.0, none)
        slot = jnp.where((at_spare > 0.5) & (rank_spare < spare), rank_spare + (main + 1.0), slot)
        place = jnp.where(here > 0.5, dot(here.astype(BF16), before), -1.0).astype(BF16)
        group, _ = row_of(rows, cap, count)
        _, at = row_of(rows, cap, tok)
        spread = (iota((rows, count), 1) == group + base).astype(BF16)
        chosen = dot(spread, place) == at
        tens = jnp.floor(slot * (1.0 / 32.0))
        units = slot - tens * 32.0
        slot = dot(spread, tens.astype(BF16)) * 32.0 + dot(spread, units.astype(BF16))
        slot = jnp.sum(jnp.where(chosen, slot, 0.0), axis=1, keepdims=True)
        slot_ref[...] = (iota((rows, slots), 1) + 1.0 == slot).astype(BF16)

    packed = dot(slot_ref[:, :main], main_ref[...]) + dot(slot_ref[:, main:], spare_ref[...])
    packed_ref[...] = packed.astype(BF16)


def give(metas, out_main, out_spare, cap, top, half, mirrored, tile):
    main, width = out_main.shape
    spare = out_spare.shape[0]
    rows = half * cap
    return call(
        functools.partial(give_kernel, cap, top, half, mirrored),
        width // tile,
        [whole_block(metas.shape), columns(main, tile), columns(spare, tile)],
        [columns(rows, tile), whole_block((rows, main + spare))],
        [jax.ShapeDtypeStruct((rows, width), BF16), jax.ShapeDtypeStruct((rows, main + spare), BF16)],
        [],
        metas,
        out_main,
        out_spare,
    )


def mixed(mix_ref, rows_ref):
    both = dot(mix_ref[...], rows_ref[...], 0, 0)
    tok = both.shape[0] // 2
    return both[:tok] + both[tok:]


def part_kernel(mix_ref, rows_ref, part_ref):
    part_ref[...] = mixed(mix_ref, rows_ref).astype(BF16)


def total_kernel(mix_ref, rows_ref, other_ref, total_ref):
    total_ref[...] = (mixed(mix_ref, rows_ref) + other_ref[...].astype(F32)).astype(BF16)


def combine(mix, rows, other, tile):
    count, width = rows.shape
    tok = mix.shape[1] // 2
    more = [] if other is None else [other]
    return call(
        part_kernel if other is None else total_kernel,
        width // tile,
        [whole_block(mix.shape), columns(count, tile)] + [columns(tok, tile)] * len(more),
        columns(tok, tile),
        jax.ShapeDtypeStruct((tok, width), BF16),
        [],
        mix,
        rows,
        *more,
    )


def slot_kernel(own_slot, mirror_slot, own_ref, mirror_ref, main_ref, spare_ref):
    total = dot(own_slot[...], own_ref[...], 0, 0) + dot(mirror_slot[...], mirror_ref[...], 0, 0)
    total = total.astype(BF16)
    main = main_ref.shape[0]
    main_ref[...] = total[:main]
    spare_ref[...] = total[main:]


def to_slots(own_slot, mirror_slot, own, mirror, main, tile):
    rows, width = own.shape
    slots = own_slot.shape[1]
    return call(
        slot_kernel,
        width // tile,
        [whole_block(own_slot.shape), whole_block(own_slot.shape), columns(rows, tile), columns(rows, tile)],
        [columns(main, tile), columns(slots - main, tile)],
        [jax.ShapeDtypeStruct((main, width), BF16), jax.ShapeDtypeStruct((slots - main, width), BF16)],
        [],
        own_slot,
        mirror_slot,
        own,
        mirror,
    )


def weight_kernel(flip, with_other, hidden_ref, spare_ref, main_ref, grad_ref, *rest):
    out_ref, stack_ref, grads_ref = rest[-3:]
    main = main_ref.shape[0]

    @pl.when(pl.program_id(0) == 0)
    def _():
        stack_hidden(hidden_ref, spare_ref, stack_ref, (flip,))

    grads_ref[:main] = main_ref[...]
    grads_ref[main:] = grad_ref[...]
    total = dot(stack_ref[...], grads_ref[...], 0, 0)
    if with_other:
        total = total + rest[0][...].astype(F32)
    out_ref[...] = total.astype(BF16)


def weight_part(hidden, spare_hidden, grads_main, grads_spare, other, flip, tile):
    slots, hid = hidden.shape
    main, width = grads_main.shape
    spare = slots - main
    more = [] if other is None else [other]
    return call(
        functools.partial(weight_kernel, flip, bool(more)),
        width // tile,
        [whole_block(hidden.shape), whole_block(spare_hidden.shape), columns(main, tile), columns(spare, tile)]
        + [columns(hid // 2, tile)] * len(more),
        columns(hid // 2, tile),
        jax.ShapeDtypeStruct((hid // 2, width), BF16),
        [pltpu.VMEM((slots, hid // 2), BF16), pltpu.VMEM((slots, tile), BF16)],
        hidden,
        spare_hidden,
        grads_main,
        grads_spare,
        *more,
    )


def back_kernel(main_ref, spare_ref, near_ref, far_ref, main_out, spare_out, sum_ref):
    step = pl.program_id(0)
    core = lax.axis_index("dp")
    half = near_ref.shape[0]

    @pl.when(step == 0)
    def _():
        sum_ref[...] = jnp.zeros_like(sum_ref)

    main = main_ref.shape[0]
    for at, weight in ((0, near_ref), (half, far_ref)):
        sum_ref[:main, at : at + half] += dot(main_ref[...], weight[...], 1, 1)
        sum_ref[main:, at : at + half] += dot(spare_ref[...], weight[...], 1, 1)

    @pl.when(step == pl.num_programs(0) - 1)
    def _():
        near = pl.multiple_of(core * half, LANES)
        far = pl.multiple_of((1 - core) * half, LANES)
        for start, at in ((near, 0), (far, half)):
            total = sum_ref[:, at : at + half].astype(BF16)
            main_out[:, pl.ds(start, half)] = total[:main]
            spare_out[:, pl.ds(start, half)] = total[main:]


def project_back(grads_main, grads_spare, near, far, tile):
    main, width = grads_main.shape
    spare = grads_spare.shape[0]
    half = near.shape[0]
    return call(
        back_kernel,
        width // tile,
        [columns(main, tile), columns(spare, tile), columns(half, tile), columns(half, tile)],
        [whole_block((main, 2 * half)), whole_block((spare, 2 * half))],
        [jax.ShapeDtypeStruct((main, 2 * half), BF16), jax.ShapeDtypeStruct((spare, 2 * half), BF16)],
        [pltpu.VMEM((main + spare, 2 * half), F32)],
        grads_main,
        grads_spare,
        near,
        far,
    )


def local(hidden_saved, down_weight, route_device, replica_flag, gate_values, grad_out):
    count = lax.axis_size("expert")
    half = count // 2
    tok, top = route_device.shape
    width = grad_out.shape[1]
    cap = 5 * tok * top // (4 * count)
    main = 3 * tok * top // 4
    hidden = hidden_saved[0, 0]
    near = down_weight[0]
    tile = width // 4
    groups = [list(range(half)), list(range(half, count))]

    def to_half(rows):
        return lax.all_to_all(
            rows.reshape(half, cap, width), "expert", 0, 0, axis_index_groups=groups, tiled=True
        ).reshape(half * cap, width)

    mirror_grad = swapped(grad_out, "expert", half)
    far = swapped(near, "dp", 1)
    spare_hidden = swapped(hidden[main:], "expert", half)
    codes = (route_device * 2 + replica_flag).T.reshape(1, tok * top).astype(F32)
    meta = jnp.concatenate([codes, gate_values.T.reshape(1, tok * top)], axis=1)
    metas = lax.all_to_all(
        jnp.broadcast_to(meta, (count, 2 * tok * top)), "expert", 0, 0, tiled=True
    )

    packed_own, mix_own = pack(meta, grad_out, cap, top, half, False, tile)
    arrived_own = to_half(packed_own)
    out_main, out_spare = project(hidden, spare_hidden, near, far, tile)
    out_spare = swapped(out_spare, "expert", half)
    packed_mirror, mix_mirror = pack(metas, mirror_grad, cap, top, half, True, tile)
    arrived_mirror = to_half(packed_mirror)
    given_mirror, slot_mirror = give(metas, out_main, out_spare, cap, top, half, True, tile)
    returned_mirror = to_half(given_mirror)
    given_own, slot_own = give(metas, out_main, out_spare, cap, top, half, False, tile)
    returned_own = to_half(given_own)
    grads_main, grads_spare = to_slots(slot_own, slot_mirror, arrived_own, arrived_mirror, main, tile)
    grads_spare = swapped(grads_spare, "expert", half)
    part = combine(mix_mirror, returned_mirror, None, tile)
    part = swapped(part, "expert", half)
    far_part = weight_part(hidden, spare_hidden, grads_main, grads_spare, None, True, tile)
    far_part = swapped(far_part, "dp", 1)
    back_main, back_spare = project_back(grads_main, grads_spare, near, far, tile)
    back_spare = swapped(back_spare, "expert", half)
    layer_out = combine(mix_own, returned_own, part, tile)
    grad_weight = weight_part(hidden, spare_hidden, grads_main, grads_spare, far_part, False, tile)
    grad_hidden = jnp.concatenate([back_main, back_spare], axis=0)
    return (layer_out, grad_hidden[None, None], grad_weight[None])


def solution(mesh):
    in_specs = (
        P("dp", "expert", None, None),
        P("expert", "dp", None),
        P(("dp", "expert"), None),
        P(("dp", "expert"), None),
        P(("dp", "expert"), None),
        P(("dp", "expert"), None),
    )
    out_specs = (P(("dp", "expert"), None), P("dp", "expert", None, None), P("expert", "dp", None))
    return jax.shard_map(local, mesh=mesh, in_specs=in_specs, out_specs=out_specs, check_vma=False)
```

```python
import functools
import jax
import jax.numpy as jnp
from jax import lax
from jax.experimental import pallas as pl
from jax.experimental.pallas import tpu as pltpu
from jax.sharding import PartitionSpec as P

F32, BF16, I32 = jnp.float32, jnp.bfloat16, jnp.int32
LANES = 128
LONG = 400_000_000
VMEM_LIMIT = 60 * 1024 * 1024


def swapped(value, axis, distance):
    count = lax.axis_size(axis)
    pairs = [(source, (source + distance) % count) for source in range(count)]
    return lax.ppermute(value, axis, pairs)


def dot(left, right, left_dim=1, right_dim=0):
    contract = (((left_dim,), (right_dim,)), ((), ()))
    return lax.dot_general(left, right, contract, preferred_element_type=F32)


def iota(shape, dim):
    return lax.broadcasted_iota(I32, shape, dim).astype(F32)


def row_of(rows, cap, lanes):
    row = iota((rows, lanes), 0)
    group = jnp.floor((row + 0.5) * (1.0 / cap))
    return group, row - group * cap


def before_mask(size):
    return (iota((size, size), 0) < iota((size, size), 1)).astype(BF16)


def call(body, grid, in_specs, out_specs, out_shape, scratch, *operands, cost=0):
    return pl.pallas_call(
        body,
        grid=(grid,),
        in_specs=in_specs,
        out_specs=out_specs,
        out_shape=out_shape,
        scratch_shapes=scratch,
        compiler_params=pltpu.CompilerParams(vmem_limit_bytes=VMEM_LIMIT),
        cost_estimate=pl.CostEstimate(flops=0, bytes_accessed=cost, transcendentals=0),
    )(*operands)


def anywhere():
    return pl.BlockSpec(memory_space=pl.ANY)


def whole_block(shape):
    return pl.BlockSpec(shape, lambda step: (0,) * len(shape))


def columns(rows, tile):
    return pl.BlockSpec((rows, tile), lambda step: (0, step))


def head_kernel(device_ref, flag_ref, gate_ref, tokens_ref, hidden_ref, payload_ref, spare_ref):
    top, tok = device_ref.shape
    width = tokens_ref.shape[1]
    gate = gate_ref[...]
    high = gate.astype(BF16).astype(F32)
    mid = (gate - high).astype(BF16).astype(F32)
    low = gate - high - mid
    parts = [device_ref[...].astype(F32), flag_ref[...].astype(F32), high, mid, low]
    filler = jnp.zeros((LANES - len(parts) * top, tok), F32)
    payload_ref[:, :width] = tokens_ref[...]
    payload_ref[:, width:] = jnp.concatenate(parts + [filler], axis=0).T.astype(BF16)
    spare_ref[...] = hidden_ref[...]


def head(devices, flags, gates, tokens, hidden, spare):
    top = devices.shape[0]
    tok, width = tokens.shape
    slots, hid = hidden.shape
    return call(
        head_kernel,
        1,
        [whole_block((top, tok))] * 3
        + [whole_block((tok, width)), pl.BlockSpec((spare, hid), lambda step: (slots // spare - 1, 0))],
        [whole_block((tok, width + LANES)), whole_block((spare, hid))],
        [jax.ShapeDtypeStruct((tok, width + LANES), BF16), jax.ShapeDtypeStruct((spare, hid), BF16)],
        [],
        devices,
        flags,
        gates,
        tokens,
        hidden,
    )


def pack_kernel(cap, top, half, tiles, meta_ref, tokens_ref, *rest):
    packed_ref, mix_ref, sel_ref, gate_ref, kind_ref = rest[-5:]
    rows, tok = sel_ref.shape
    step = pl.program_id(0)

    @pl.when(step == 0)
    def _():
        me = lax.axis_index("expert")
        first = (lax.div(me, half) * half).astype(F32)
        meta = meta_ref[...].astype(F32).T
        part = lambda which, k: meta[which * top + k : which * top + k + 1]
        devices = [part(0, k) for k in range(top)]
        dest = iota((LANES, tok), 0)
        inside = dest < half
        dest = dest + first
        none = jnp.zeros((LANES, tok), F32)
        hit, spare, high, mid, low = none, none, none, none, none
        for k in range(top):
            partner = devices[k] + jnp.where(devices[k] < half, 1.0 * half, -1.0 * half)
            wants = part(1, k)
            for other in devices:
                wants = jnp.where(other == partner, 0.0, wants)
            named = (dest == devices[k]) & inside
            hit = jnp.where(named, 1.0, hit)
            spare = jnp.where(named, wants, spare)
            high = jnp.where(named, part(2, k), high)
            mid = jnp.where(named, part(3, k), mid)
            low = jnp.where(named, part(4, k), low)
        place = dot(hit.astype(BF16), before_mask(tok))
        place = jnp.where(hit > 0.5, place, -1.0)
        group, at = row_of(rows, cap, LANES)
        spread = (iota((rows, LANES), 1) == group).astype(BF16)
        to_rows = lambda table: dot(spread, table.astype(BF16))
        chosen = to_rows(place) == at
        of_row = lambda table: jnp.sum(jnp.where(chosen, table, 0.0), axis=1, keepdims=True)
        high, mid, low = to_rows(high), to_rows(mid), to_rows(low)
        sel = jnp.where(chosen, 1.0, jnp.zeros((rows, tok), F32))
        sel_ref[...] = sel.astype(BF16)
        gate_ref[...] = jnp.broadcast_to(of_row(high + mid + low), (rows, LANES))
        mix_ref[:tok] = (sel * high).T.astype(BF16)
        mix_ref[tok:] = (sel * mid).T.astype(BF16)
        is_spare = of_row(to_rows(spare))
        is_main = of_row(sel) - is_spare
        lane = iota((rows, LANES), 1)
        kind = jnp.where(lane == 0.0, is_main, jnp.where(lane == 1.0, is_spare, 0.0))
        kind_ref[...] = kind.astype(BF16)

    @pl.when(step < tiles)
    def _():
        packed = dot(sel_ref[...], tokens_ref[...]) * gate_ref[:, :1]
        packed_ref[...] = packed.astype(BF16)

    @pl.when(step == tiles)
    def _():
        packed_ref[:, :LANES] = kind_ref[...]


def pack(payload, cap, top, half, tile, cost, *after):
    tok, wide = payload.shape
    rows = half * cap
    tiles = (wide - LANES) // tile
    return call(
        functools.partial(pack_kernel, cap, top, half, tiles),
        tiles + 1,
        [
            pl.BlockSpec((tok, LANES), lambda step: (0, wide // LANES - 1)),
            pl.BlockSpec((tok, tile), lambda step: (0, jnp.minimum(step, tiles - 1))),
        ]
        + [anywhere()] * len(after),
        [columns(rows, tile), whole_block((2 * tok, rows))],
        [jax.ShapeDtypeStruct((rows, wide), BF16), jax.ShapeDtypeStruct((2 * tok, rows), BF16)],
        [pltpu.VMEM((rows, tok), BF16), pltpu.VMEM((rows, LANES), F32), pltpu.VMEM((rows, LANES), BF16)],
        payload,
        payload,
        *after,
        cost=cost,
    )


def stack_hidden(hidden_ref, spare_ref, out_ref, order):
    main = hidden_ref.shape[0] - spare_ref.shape[0]
    half = hidden_ref.shape[1] // 2
    core = lax.axis_index("dp")
    for at, flip in enumerate(order):
        start = pl.multiple_of((1 - core if flip else core) * half, LANES)
        out_ref[:main, at * half : (at + 1) * half] = hidden_ref[:main, pl.ds(start, half)]
        out_ref[main:, at * half : (at + 1) * half] = spare_ref[:, pl.ds(start, half)]


def out_kernel(hidden_ref, spare_ref, near_ref, far_ref, *rest):
    main_out, spare_out, stack_ref = rest[-3:]

    @pl.when(pl.program_id(0) == 0)
    def _():
        stack_hidden(hidden_ref, spare_ref, stack_ref, (False, True))

    main, half = main_out.shape[0], near_ref.shape[0]
    total = dot(stack_ref[:, :half], near_ref[...]) + dot(stack_ref[:, half:], far_ref[...])
    total = total.astype(BF16)
    main_out[...] = total[:main]
    spare_out[...] = total[main:]


def project(hidden, spare_hidden, near, far, tile, *after):
    half, width = near.shape
    slots, hid = hidden.shape
    spare = spare_hidden.shape[0]
    return call(
        out_kernel,
        width // tile,
        [whole_block(hidden.shape), whole_block(spare_hidden.shape), columns(half, tile), columns(half, tile)]
        + [anywhere()] * len(after),
        [columns(slots - spare, tile), columns(spare, tile)],
        [jax.ShapeDtypeStruct((slots - spare, width), BF16), jax.ShapeDtypeStruct((spare, width), BF16)],
        [pltpu.VMEM((slots, hid), BF16)],
        hidden,
        spare_hidden,
        near,
        far,
        *after,
    )


def slots_of(kind_ref, other_ref, second, main, spare):
    rows = kind_ref.shape[0]
    kind = kind_ref[...]
    lower = (iota((rows, rows), 1) < iota((rows, rows), 0)).astype(BF16)
    ahead = jnp.sum(other_ref[...].astype(F32), axis=0, keepdims=True)
    rank = dot(lower, kind) + jnp.where(second, ahead, 0.0)
    kind = kind.astype(F32)
    fits = lambda lane, limit: (kind[:, lane : lane + 1] > 0.5) & (rank[:, lane : lane + 1] < limit)
    slot = jnp.where(fits(1, spare), rank[:, 1:2] + (main + 1.0), 0.0)
    return jnp.where(fits(0, main), rank[:, 0:1] + 1.0, slot)


def upper_half(half):
    return lax.axis_index("expert") >= half


def give_kernel(half, mirrored, kind_ref, other_ref, main_ref, spare_ref, *rest):
    packed_ref, slot_ref = rest[-2:]
    rows, slots = slot_ref.shape
    main, spare = main_ref.shape[0], spare_ref.shape[0]

    @pl.when(pl.program_id(0) == 0)
    def _():
        second = upper_half(half) != mirrored
        slot = slots_of(kind_ref, other_ref, second, main, spare)
        slot_ref[...] = (iota((rows, slots), 1) + 1.0 == slot).astype(BF16)

    packed = dot(slot_ref[:, :main], main_ref[...]) + dot(slot_ref[:, main:], spare_ref[...])
    packed_ref[...] = packed.astype(BF16)


def kinds(arrived):
    rows, wide = arrived.shape
    return pl.BlockSpec((rows, LANES), lambda step: (0, wide // LANES - 1))


def give(arrived, other, out_main, out_spare, half, mirrored, tile, *after):
    main, width = out_main.shape
    spare = out_spare.shape[0]
    rows = arrived.shape[0]
    return call(
        functools.partial(give_kernel, half, mirrored),
        width // tile,
        [kinds(arrived), kinds(other), columns(main, tile), columns(spare, tile)]
        + [anywhere()] * len(after),
        columns(rows, tile),
        jax.ShapeDtypeStruct((rows, width), BF16),
        [pltpu.VMEM((rows, main + spare), BF16)],
        arrived,
        other,
        out_main,
        out_spare,
        *after,
    )


def mixed(mix_ref, rows_ref):
    both = dot(mix_ref[...], rows_ref[...])
    tok = both.shape[0] // 2
    return both[:tok] + both[tok:]


def part_kernel(mix_ref, rows_ref, part_ref):
    part_ref[...] = mixed(mix_ref, rows_ref).astype(BF16)


def total_kernel(mix_ref, rows_ref, other_ref, *rest):
    rest[-1][...] = (mixed(mix_ref, rows_ref) + other_ref[...].astype(F32)).astype(BF16)


def combine(mix, rows, other, tile, *after):
    count, width = rows.shape
    tok = mix.shape[0] // 2
    more = [] if other is None else [other]
    return call(
        part_kernel if other is None else total_kernel,
        width // tile,
        [whole_block(mix.shape), columns(count, tile)]
        + [columns(tok, tile)] * len(more)
        + [anywhere()] * len(after),
        columns(tok, tile),
        jax.ShapeDtypeStruct((tok, width), BF16),
        [],
        mix,
        rows,
        *more,
        *after,
    )


def slot_kernel(half, own_kind, mirror_kind, own_ref, mirror_ref, *rest):
    main_ref, spare_ref, own_slot, mirror_slot = rest[-4:]
    main, spare = main_ref.shape[0], spare_ref.shape[0]
    slots, rows = own_slot.shape

    @pl.when(pl.program_id(0) == 0)
    def _():
        upper = upper_half(half)
        pairs = (
            (own_kind, mirror_kind, upper, own_slot),
            (mirror_kind, own_kind, jnp.logical_not(upper), mirror_slot),
        )
        for kind, other, second, out_ref in pairs:
            slot = slots_of(kind, other, second, main, spare)
            slot = jnp.broadcast_to(slot, (rows, LANES)).T[0:1]
            out_ref[...] = (iota((slots, rows), 0) + 1.0 == slot).astype(BF16)

    total = dot(own_slot[...], own_ref[...]) + dot(mirror_slot[...], mirror_ref[...])
    total = total.astype(BF16)
    main_ref[...] = total[:main]
    spare_ref[...] = total[main:]


def to_slots(own, mirror, main, spare, half, tile, *after):
    rows, wide = own.shape
    width = wide - LANES
    return call(
        functools.partial(slot_kernel, half),
        width // tile,
        [kinds(own), kinds(mirror), columns(rows, tile), columns(rows, tile)] + [anywhere()] * len(after),
        [columns(main, tile), columns(spare, tile)],
        [jax.ShapeDtypeStruct((main, width), BF16), jax.ShapeDtypeStruct((spare, width), BF16)],
        [pltpu.VMEM((main + spare, rows), BF16), pltpu.VMEM((main + spare, rows), BF16)],
        own,
        mirror,
        own,
        mirror,
        *after,
    )


def weight_kernel(flip, with_other, hidden_ref, spare_ref, main_ref, grad_ref, *rest):
    out_ref, turned_ref, grads_ref = rest[-3:]
    main, half = main_ref.shape[0], turned_ref.shape[0]

    @pl.when(pl.program_id(0) == 0)
    def _():
        core = lax.axis_index("dp")
        start = pl.multiple_of((1 - core if flip else core) * half, LANES)
        turned_ref[:, :main] = hidden_ref[:main, pl.ds(start, half)].T
        turned_ref[:, main:] = spare_ref[:, pl.ds(start, half)].T

    grads_ref[:main] = main_ref[...]
    grads_ref[main:] = grad_ref[...]
    total = dot(turned_ref[...], grads_ref[...])
    if with_other:
        total = total + rest[0][...].astype(F32)
    out_ref[...] = total.astype(BF16)


def weight_part(hidden, spare_hidden, grads_main, grads_spare, other, flip, tile, *after):
    slots, hid = hidden.shape
    main, width = grads_main.shape
    spare = slots - main
    more = [] if other is None else [other]
    return call(
        functools.partial(weight_kernel, flip, bool(more)),
        width // tile,
        [whole_block(hidden.shape), whole_block(spare_hidden.shape), columns(main, tile), columns(spare, tile)]
        + [columns(hid // 2, tile)] * len(more)
        + [anywhere()] * len(after),
        columns(hid // 2, tile),
        jax.ShapeDtypeStruct((hid // 2, width), BF16),
        [pltpu.VMEM((hid // 2, slots), BF16), pltpu.VMEM((slots, tile), BF16)],
        hidden,
        spare_hidden,
        grads_main,
        grads_spare,
        *more,
        *after,
    )


def back_kernel(main_ref, spare_ref, near_ref, far_ref, main_out, spare_out, sum_ref):
    step = pl.program_id(0)
    core = lax.axis_index("dp")
    half = near_ref.shape[0]

    @pl.when(step == 0)
    def _():
        sum_ref[...] = jnp.zeros_like(sum_ref)

    main = main_ref.shape[0]
    for at, weight in ((0, near_ref), (half, far_ref)):
        sum_ref[:main, at : at + half] += dot(main_ref[...], weight[...], 1, 1)
        sum_ref[main:, at : at + half] += dot(spare_ref[...], weight[...], 1, 1)

    @pl.when(step == pl.num_programs(0) - 1)
    def _():
        near = pl.multiple_of(core * half, LANES)
        far = pl.multiple_of((1 - core) * half, LANES)
        for start, at in ((near, 0), (far, half)):
            total = sum_ref[:, at : at + half].astype(BF16)
            main_out[:, pl.ds(start, half)] = total[:main]
            spare_out[:, pl.ds(start, half)] = total[main:]


def project_back(grads_main, grads_spare, near, far, tile):
    main, width = grads_main.shape
    spare = grads_spare.shape[0]
    half = near.shape[0]
    return call(
        back_kernel,
        width // tile,
        [columns(main, tile), columns(spare, tile), columns(half, tile), columns(half, tile)],
        [whole_block((main, 2 * half)), whole_block((spare, 2 * half))],
        [jax.ShapeDtypeStruct((main, 2 * half), BF16), jax.ShapeDtypeStruct((spare, 2 * half), BF16)],
        [pltpu.VMEM((main + spare, 2 * half), F32)],
        grads_main,
        grads_spare,
        near,
        far,
    )


def local(hidden_saved, down_weight, route_device, replica_flag, gate_values, grad_out):
    count = lax.axis_size("expert")
    half = count // 2
    tok, top = route_device.shape
    width = grad_out.shape[1]
    cap = 5 * tok * top // (4 * count)
    main = 3 * tok * top // 4
    hidden = hidden_saved[0, 0]
    near = down_weight[0]
    tile = width // 4
    groups = [list(range(half)), list(range(half, count))]

    def to_half(rows):
        return lax.all_to_all(
            rows.reshape(half, cap, -1), "expert", 0, 0, axis_index_groups=groups, tiled=True
        ).reshape(half * cap, -1)

    payload, spare_hidden = head(
        route_device.T, replica_flag.T, gate_values.T, grad_out, hidden, hidden.shape[0] - main
    )
    mirror = swapped(payload, "expert", half)
    far = swapped(near, "dp", 1)
    spare_hidden = swapped(spare_hidden, "expert", half)
    packed_own, mix_own = pack(payload, cap, top, half, tile, 0)
    arrived_own = to_half(packed_own)
    out_main, out_spare = project(hidden, spare_hidden, near, far, tile, mix_own)
    packed_mirror, mix_mirror = pack(mirror, cap, top, half, tile, LONG, out_spare)
    out_spare = swapped(out_spare, "expert", half)
    arrived_mirror = to_half(packed_mirror)
    given_mirror = give(arrived_mirror, arrived_own, out_main, out_spare, half, True, tile)
    returned_mirror = to_half(given_mirror)
    grads_main, grads_spare = to_slots(
        arrived_own, arrived_mirror, main, hidden.shape[0] - main, half, tile, given_mirror
    )
    given_own = give(arrived_own, arrived_mirror, out_main, out_spare, half, False, tile, grads_spare)
    returned_own = to_half(given_own)
    grads_spare = swapped(grads_spare, "expert", half)
    part = combine(mix_mirror, returned_mirror, None, tile)
    far_part = weight_part(hidden, spare_hidden, grads_main, grads_spare, None, True, tile, part)
    part = swapped(part, "expert", half)
    far_part = swapped(far_part, "dp", 1)
    back_main, back_spare = project_back(grads_main, grads_spare, near, far, tile)
    back_spare = swapped(back_spare, "expert", half)
    grad_weight = weight_part(hidden, spare_hidden, grads_main, grads_spare, far_part, False, tile)
    layer_out = combine(mix_own, returned_own, part, tile, grad_weight)
    grad_hidden = jnp.concatenate([back_main, back_spare], axis=0)
    return (layer_out, grad_hidden[None, None], grad_weight[None])


def solution(mesh):
    in_specs = (
        P("dp", "expert", None, None),
        P("expert", "dp", None),
        P(("dp", "expert"), None),
        P(("dp", "expert"), None),
        P(("dp", "expert"), None),
        P(("dp", "expert"), None),
    )
    out_specs = (P(("dp", "expert"), None), P("dp", "expert", None, None), P("expert", "dp", None))
    return jax.shard_map(local, mesh=mesh, in_specs=in_specs, out_specs=out_specs, check_vma=False)
```

```python
import functools
import jax
import jax.numpy as jnp
from jax import lax
from jax.experimental import pallas as pl
from jax.experimental.pallas import tpu as pltpu
from jax.sharding import PartitionSpec as P

F32, BF16, I32 = jnp.float32, jnp.bfloat16, jnp.int32
LANES = 128
VMEM_LIMIT = 60 * 1024 * 1024


def swapped(value, axis, distance):
    count = lax.axis_size(axis)
    pairs = [(source, (source + distance) % count) for source in range(count)]
    return lax.ppermute(value, axis, pairs)


def dot(left, right, left_dim=1, right_dim=0):
    contract = (((left_dim,), (right_dim,)), ((), ()))
    return lax.dot_general(left, right, contract, preferred_element_type=F32)


def iota(shape, dim):
    return lax.broadcasted_iota(I32, shape, dim).astype(F32)


def row_of(rows, cap, lanes):
    row = iota((rows, lanes), 0)
    group = jnp.floor((row + 0.5) * (1.0 / cap))
    return group, row - group * cap


def before_mask(size):
    return (iota((size, size), 0) < iota((size, size), 1)).astype(BF16)


def bf16(*shape):
    return jax.ShapeDtypeStruct(shape, BF16)


def f32(*shape):
    return jax.ShapeDtypeStruct(shape, F32)


def call(body, grid, ins, outs, scratch=(), after=(), alias=None):
    single = not isinstance(outs, list)
    pairs = [outs] if single else outs
    specs = [spec for _, spec in pairs]
    shapes = [shape for shape, _ in pairs]
    count = len(ins)

    def kernel(*refs):
        body(*refs[:count], *refs[count + len(after) :])

    return pl.pallas_call(
        kernel,
        grid=(grid,),
        in_specs=[spec for _, spec in ins] + [anywhere()] * len(after),
        out_specs=specs[0] if single else specs,
        out_shape=shapes[0] if single else shapes,
        scratch_shapes=list(scratch),
        input_output_aliases=alias or {},
        compiler_params=pltpu.CompilerParams(vmem_limit_bytes=VMEM_LIMIT),
        cost_estimate=pl.CostEstimate(flops=0, bytes_accessed=0, transcendentals=0),
    )(*[array for array, _ in ins], *after)


def anywhere():
    return pl.BlockSpec(memory_space=pl.ANY)


def whole(array):
    return pl.BlockSpec(array.shape, lambda step: (0,) * len(array.shape))


def columns(array, tile):
    return pl.BlockSpec((array.shape[0], tile), lambda step: (0, step))


def entire(*arrays):
    return [(array, whole(array)) for array in arrays]


def by_columns(tile, *arrays):
    return [(array, columns(array, tile)) for array in arrays]


def head_kernel(device_ref, flag_ref, gate_ref, hidden_ref, meta_ref, spare_ref):
    top = device_ref.shape[0]
    codes = (device_ref[...] * 2 + flag_ref[...]).astype(F32)
    count = meta_ref.shape[0]
    meta_ref[:, :top, :] = jnp.broadcast_to(codes[None], (count, *codes.shape))
    meta_ref[:, top:, :] = jnp.broadcast_to(gate_ref[...][None], (count, *codes.shape))
    spare_ref[...] = hidden_ref[...]


def head(devices, flags, gates, hidden, spare, count):
    top, tok = devices.shape
    slots, hid = hidden.shape
    last = pl.BlockSpec((spare, hid), lambda step: (slots // spare - 1, 0))
    outs = entire(f32(count, 2 * top, tok), bf16(spare, hid))
    return call(head_kernel, 1, entire(devices, flags, gates) + [(hidden, last)], outs)


def copy_kernel(source_ref, target_ref, done):
    copy = pltpu.make_async_copy(source_ref, target_ref, done)
    copy.start()
    copy.wait()


def copied(array, *after):
    shape = jax.ShapeDtypeStruct(array.shape, array.dtype)
    return call(
        copy_kernel, 1, [(array, anywhere())], (shape, anywhere()), [pltpu.SemaphoreType.DMA], after
    )


def plan_rows(meta, cap, half, sel_ref, gate_ref, mix_ref):
    rows, tok = sel_ref.shape
    top = meta.shape[0] // 2
    me = lax.axis_index("expert")
    first = (lax.div(me, half) * half).astype(F32)
    dest = iota((LANES, tok), 0)
    inside = dest < half
    dest = dest + first
    hit = jnp.zeros((LANES, tok), F32)
    gate = jnp.zeros((LANES, tok), F32)
    for k in range(top):
        device = jnp.floor(meta[k : k + 1] * 0.5)
        named = (dest == device) & inside
        hit = jnp.where(named, 1.0, hit)
        gate = jnp.where(named, meta[top + k : top + k + 1], gate)
    place = dot(hit.astype(BF16), before_mask(tok))
    place = jnp.where(hit > 0.5, place, -1.0)
    group, at = row_of(rows, cap, LANES)
    spread = (iota((rows, LANES), 1) == group).astype(BF16)
    to_rows = lambda table: dot(spread, table.astype(BF16))
    chosen = jnp.where(to_rows(place) == at, 1.0, jnp.zeros((rows, tok), F32))
    high = gate.astype(BF16).astype(F32)
    mid = (gate - high).astype(BF16).astype(F32)
    low = gate - high - mid
    high, mid, low = to_rows(high), to_rows(mid), to_rows(low)
    scale = jnp.sum(chosen * (high + mid + low), axis=1, keepdims=True)
    sel_ref[...] = chosen.astype(BF16)
    gate_ref[...] = jnp.broadcast_to(scale, (rows, LANES))
    mix_ref[:tok] = (chosen * high).T.astype(BF16)
    mix_ref[tok:] = (chosen * mid).T.astype(BF16)


def packed_rows(sel_ref, gate_ref, tokens_ref, packed_ref):
    packed_ref[...] = (dot(sel_ref[...], tokens_ref[...]) * gate_ref[:, :1]).astype(BF16)


def pack_own_kernel(cap, half, meta_ref, tokens_ref, packed_ref, mix_ref, sel_ref, gate_ref):
    @pl.when(pl.program_id(0) == 0)
    def _():
        plan_rows(meta_ref[0], cap, half, sel_ref, gate_ref, mix_ref)

    packed_rows(sel_ref, gate_ref, tokens_ref, packed_ref)


def pack_own(meta, tokens, cap, half, tile, *after):
    tok, width = tokens.shape
    rows = half * cap
    first = pl.BlockSpec((1, *meta.shape[1:]), lambda step: (0, 0, 0))
    return call(
        functools.partial(pack_own_kernel, cap, half),
        width // tile,
        [(meta, first)] + by_columns(tile, tokens),
        by_columns(tile, bf16(rows, width)) + entire(bf16(2 * tok, rows)),
        [pltpu.VMEM((rows, tok), BF16), pltpu.VMEM((rows, LANES), F32)],
        after,
    )


def pack(sel, gate, tokens, tile, *after):
    rows, width = sel.shape[0], tokens.shape[1]
    return call(
        packed_rows,
        width // tile,
        entire(sel, gate) + by_columns(tile, tokens),
        by_columns(tile, bf16(rows, width))[0],
        after=after,
    )


def plan_kernel(cap, half, main, metas_ref, sel_ref, gate_ref, mix_ref, *slot_refs):
    count, tops, tok = metas_ref.shape
    top = tops // 2
    rows, slots = slot_refs[0].shape
    spare = slots - main
    me = lax.axis_index("expert")
    mirror = lax.rem(me + half, count)
    plan_rows(metas_ref[mirror], cap, half, sel_ref, gate_ref, mix_ref)

    mine, other = me.astype(F32), mirror.astype(F32)
    none = jnp.zeros((count, tok), F32)
    here, flag, clash = none, none, none
    for k in range(top):
        code = metas_ref[:, k, :]
        device = jnp.floor(code * 0.5)
        here = jnp.where(device == mine, 1.0, here)
        flag = jnp.where(device == mine, code - 2.0 * device, flag)
        clash = jnp.where(device == other, 1.0, clash)
    at_spare = here * flag * (1.0 - clash)
    at_main = here - at_spare
    before = before_mask(tok)
    ones = jnp.ones((tok, LANES), BF16)
    lower = (iota((count, count), 1) < iota((count, count), 0)).astype(BF16)

    def rank(flags):
        flags = flags.astype(BF16)
        return dot(flags, before) + dot(lower, dot(flags, ones).astype(BF16))

    rank_main, rank_spare = rank(at_main), rank(at_spare)
    slot = jnp.where((at_main > 0.5) & (rank_main < main), rank_main + 1.0, none)
    slot = jnp.where((at_spare > 0.5) & (rank_spare < spare), rank_spare + (main + 1.0), slot)
    place = jnp.where(here > 0.5, dot(here.astype(BF16), before), -1.0).astype(BF16)
    tens = jnp.floor(slot * (1.0 / 32.0))
    units = (slot - tens * 32.0).astype(BF16)
    tens = tens.astype(BF16)
    group, _ = row_of(rows, cap, count)
    _, at = row_of(rows, cap, tok)
    start = lax.div(me, half) * half
    for side, base in enumerate((start, lax.rem(start + half, count))):
        spread = (iota((rows, count), 1) == group + base.astype(F32)).astype(BF16)
        chosen = dot(spread, place) == at
        number = dot(spread, tens) * 32.0 + dot(spread, units)
        number = jnp.sum(jnp.where(chosen, number, 0.0), axis=1, keepdims=True)
        give_ref, take_ref = slot_refs[2 * side : 2 * side + 2]
        give_ref[...] = (iota((rows, slots), 1) + 1.0 == number).astype(BF16)
        number = jnp.broadcast_to(number, (rows, LANES)).T[0:1]
        take_ref[...] = (iota((slots, rows), 0) + 1.0 == number).astype(BF16)


def plan(metas, cap, half, main, slots):
    tok = metas.shape[2]
    rows = half * cap
    sides = [bf16(rows, slots), bf16(slots, rows)] * 2
    outs = entire(bf16(rows, tok), f32(rows, LANES), bf16(2 * tok, rows), *sides)
    return call(functools.partial(plan_kernel, cap, half, main), 1, entire(metas), outs)


def project_kernel(hidden_ref, spare_ref, near_ref, far_ref, main_out, spare_out, near_turned, far_turned, stack_ref):
    main, half = main_out.shape[0], near_ref.shape[0]

    @pl.when(pl.program_id(0) == 0)
    def _():
        core = lax.axis_index("dp")
        for at, which, turned_ref in ((0, core, near_turned), (half, 1 - core, far_turned)):
            start = pl.multiple_of(which * half, LANES)
            stack_ref[:main, at : at + half] = hidden_ref[:main, pl.ds(start, half)]
            stack_ref[main:, at : at + half] = spare_ref[:, pl.ds(start, half)]
            turned_ref[...] = stack_ref[:, at : at + half].T

    total = dot(stack_ref[:, :half], near_ref[...]) + dot(stack_ref[:, half:], far_ref[...])
    total = total.astype(BF16)
    main_out[...] = total[:main]
    spare_out[...] = total[main:]


def project(hidden, spare_hidden, near, far, tile, *after):
    half, width = near.shape
    spare = spare_hidden.shape[0]
    slots = hidden.shape[0]
    turned = [bf16(half, slots), bf16(half, slots)]
    return call(
        project_kernel,
        width // tile,
        entire(hidden, spare_hidden) + by_columns(tile, near, far),
        by_columns(tile, bf16(slots - spare, width), bf16(spare, width)) + entire(*turned),
        [pltpu.VMEM(hidden.shape, BF16)],
        after,
    )


def give_kernel(own_slot, mirror_slot, main_ref, spare_ref, own_ref, mirror_ref):
    main = main_ref.shape[0]
    for slot_ref, out_ref in ((own_slot, own_ref), (mirror_slot, mirror_ref)):
        packed = dot(slot_ref[:, :main], main_ref[...]) + dot(slot_ref[:, main:], spare_ref[...])
        out_ref[...] = packed.astype(BF16)


def give(own_slot, mirror_slot, out_main, out_spare, tile):
    rows, width = own_slot.shape[0], out_main.shape[1]
    return call(
        give_kernel,
        width // tile,
        entire(own_slot, mirror_slot) + by_columns(tile, out_main, out_spare),
        by_columns(tile, bf16(rows, width), bf16(rows, width)),
    )


def take_kernel(own_slot, mirror_slot, own_ref, mirror_ref, main_ref, spare_ref):
    total = dot(own_slot[...], own_ref[...]) + dot(mirror_slot[...], mirror_ref[...])
    total = total.astype(BF16)
    main = main_ref.shape[0]
    main_ref[...] = total[:main]
    spare_ref[...] = total[main:]


def take(own_slot, mirror_slot, own, mirror, main, tile, *after):
    slots, width = own_slot.shape[0], own.shape[1]
    return call(
        take_kernel,
        width // tile,
        entire(own_slot, mirror_slot) + by_columns(tile, own, mirror),
        by_columns(tile, bf16(main, width), bf16(slots - main, width)),
        after=after,
    )


def mixed(mix_ref, rows_ref):
    both = dot(mix_ref[...], rows_ref[...])
    tok = both.shape[0] // 2
    return both[:tok] + both[tok:]


def part_kernel(mix_ref, rows_ref, part_ref):
    part_ref[...] = mixed(mix_ref, rows_ref).astype(BF16)


def total_kernel(mix_ref, rows_ref, other_ref, total_ref):
    total_ref[...] = (mixed(mix_ref, rows_ref) + other_ref[...].astype(F32)).astype(BF16)


def combine(mix, rows, others, tile, *after):
    width = rows.shape[1]
    return call(
        total_kernel if others else part_kernel,
        width // tile,
        entire(mix) + by_columns(tile, rows, *others),
        by_columns(tile, bf16(mix.shape[0] // 2, width))[0],
        after=after,
    )


def stack_grads(main_ref, spare_ref, grads_ref):
    main = main_ref.shape[0]
    grads_ref[:main] = main_ref[...]
    grads_ref[main:] = spare_ref[...]


def weight_kernel(turned, other_turned, main_ref, spare_ref, other_main, other_spare, out_ref, grads_ref):
    stack_grads(main_ref, spare_ref, grads_ref)
    total = dot(turned[...], grads_ref[...])
    stack_grads(other_main, other_spare, grads_ref)
    out_ref[...] = (total + dot(other_turned[...], grads_ref[...])).astype(BF16)


def weight_grad(turned, other_turned, grads, other_grads, tile, *after):
    half, slots = turned.shape
    width = grads[0].shape[1]
    return call(
        weight_kernel,
        width // tile,
        entire(turned, other_turned) + by_columns(tile, *grads, *other_grads),
        by_columns(tile, bf16(half, width))[0],
        [pltpu.VMEM((slots, tile), BF16)],
        after,
    )


def back_kernel(main_ref, grad_ref, near_ref, far_ref, back_ref, spare_ref, sum_ref, grads_ref):
    step = pl.program_id(0)
    half = near_ref.shape[0]
    main = main_ref.shape[0]

    @pl.when(step == 0)
    def _():
        sum_ref[...] = jnp.zeros_like(sum_ref)

    stack_grads(main_ref, grad_ref, grads_ref)
    sum_ref[:, :half] += dot(grads_ref[...], near_ref[...], 1, 1)
    sum_ref[:, half:] += dot(grads_ref[...], far_ref[...], 1, 1)

    @pl.when(step == pl.num_programs(0) - 1)
    def _():
        core = lax.axis_index("dp")
        for at, which in ((0, core), (half, 1 - core)):
            start = pl.multiple_of(which * half, LANES)
            total = sum_ref[:, at : at + half].astype(BF16)
            back_ref[:, pl.ds(start, half)] = total
            spare_ref[:, pl.ds(start, half)] = total[main:]


def project_back(grads_main, grads_spare, near, far, tile, *after):
    main, width = grads_main.shape
    spare = grads_spare.shape[0]
    half = near.shape[0]
    slots = main + spare
    return call(
        back_kernel,
        width // tile,
        by_columns(tile, grads_main, grads_spare, near, far),
        entire(bf16(slots, 2 * half), bf16(spare, 2 * half)),
        [pltpu.VMEM((slots, 2 * half), F32), pltpu.VMEM((slots, tile), BF16)],
        after,
    )


def place_kernel(back_ref, spare_ref, out_ref):
    out_ref[...] = spare_ref[...]


def with_spare(back, back_spare, *after):
    slots, hid = back.shape
    spare = back_spare.shape[0]
    last = pl.BlockSpec((spare, hid), lambda step: (slots // spare - 1, 0))
    ins = [(back, anywhere())] + entire(back_spare)
    return call(place_kernel, 1, ins, (bf16(slots, hid), last), (), after, {0: 0})


def local(hidden_saved, down_weight, route_device, replica_flag, gate_values, grad_out):
    count = lax.axis_size("expert")
    half = count // 2
    tok, top = route_device.shape
    width = grad_out.shape[1]
    cap = 5 * tok * top // (4 * count)
    main = 3 * tok * top // 4
    hidden = hidden_saved[0, 0]
    near = down_weight[0]
    slots = hidden.shape[0]
    tile = width // 4
    groups = [list(range(half)), list(range(half, count))]

    def to_half(rows):
        return lax.all_to_all(
            rows.reshape(half, cap, width), "expert", 0, 0, axis_index_groups=groups, tiled=True
        ).reshape(half * cap, width)

    far = swapped(near, "dp", 1)
    meta, spare_hidden = head(
        route_device.T, replica_flag.T, gate_values.T, hidden, slots - main, count
    )
    spare_hidden = swapped(spare_hidden, "expert", half)
    metas = lax.all_to_all(meta, "expert", 0, 0, tiled=True)
    mirror = swapped(copied(grad_out, metas, spare_hidden), "expert", half)
    packed_own, mix_own = pack_own(meta, grad_out, cap, half, tile)
    arrived_own = to_half(packed_own)
    sel, gate, mix_mirror, give_own, take_own, give_mirror, take_mirror = plan(
        metas, cap, half, main, slots
    )
    out_main, out_spare, turned, far_turned = project(
        hidden, spare_hidden, near, far, tile, mix_own
    )
    other_turned = swapped(far_turned, "dp", 1)
    packed_mirror = pack(sel, gate, mirror, tile, out_spare)
    out_spare = swapped(out_spare, "expert", half)
    arrived_mirror = to_half(packed_mirror)
    given_own, given_mirror = give(give_own, give_mirror, out_main, out_spare, tile)
    returned_mirror = to_half(given_mirror)
    grads_main, grads_spare = take(
        take_own, take_mirror, arrived_own, arrived_mirror, main, tile, given_mirror
    )
    returned_own = to_half(given_own)
    other_main = swapped(grads_main, "dp", 1)
    grads_spare = swapped(grads_spare, "expert", half)
    other_spare = swapped(grads_spare, "dp", 1)
    part = combine(mix_mirror, returned_mirror, [], tile)
    back, back_spare = project_back(grads_main, grads_spare, near, far, tile, part)
    grad_weight = weight_grad(
        turned, other_turned, (grads_main, grads_spare), (other_main, other_spare), tile, back
    )
    part = swapped(part, "expert", half)
    back_spare = swapped(back_spare, "expert", half)
    layer_out = combine(mix_own, returned_own, [part], tile, grad_weight)
    grad_hidden = with_spare(back, back_spare, layer_out)
    return (layer_out, grad_hidden[None, None], grad_weight[None])


def solution(mesh):
    in_specs = (
        P("dp", "expert", None, None),
        P("expert", "dp", None),
        P(("dp", "expert"), None),
        P(("dp", "expert"), None),
        P(("dp", "expert"), None),
        P(("dp", "expert"), None),
    )
    out_specs = (P(("dp", "expert"), None), P("dp", "expert", None, None), P("expert", "dp", None))
    return jax.shard_map(local, mesh=mesh, in_specs=in_specs, out_specs=out_specs, check_vma=False)
```

```python
import functools
import jax
import jax.numpy as jnp
from jax import lax
from jax.experimental import pallas as pl
from jax.experimental.pallas import tpu as pltpu
from jax.sharding import PartitionSpec as P

F32, BF16, I32 = jnp.float32, jnp.bfloat16, jnp.int32
LANES = 128
VMEM_LIMIT = 60 * 1024 * 1024


def swapped(value, axis, distance):
    count = lax.axis_size(axis)
    pairs = [(source, (source + distance) % count) for source in range(count)]
    return lax.ppermute(value, axis, pairs)


def dot(left, right, left_dim=1, right_dim=0):
    contract = (((left_dim,), (right_dim,)), ((), ()))
    return lax.dot_general(left, right, contract, preferred_element_type=F32)


def iota(shape, dim):
    return lax.broadcasted_iota(I32, shape, dim).astype(F32)


def row_of(rows, cap, lanes):
    row = iota((rows, lanes), 0)
    group = jnp.floor((row + 0.5) * (1.0 / cap))
    return group, row - group * cap


def before_mask(size):
    return (iota((size, size), 0) < iota((size, size), 1)).astype(BF16)


def bf16(*shape):
    return jax.ShapeDtypeStruct(shape, BF16)


def f32(*shape):
    return jax.ShapeDtypeStruct(shape, F32)


def call(body, grid, ins, outs, scratch=(), after=(), alias=None):
    single = not isinstance(outs, list)
    pairs = [outs] if single else outs
    specs = [spec for _, spec in pairs]
    shapes = [shape for shape, _ in pairs]
    count = len(ins)

    def kernel(*refs):
        body(*refs[:count], *refs[count + len(after) :])

    return pl.pallas_call(
        kernel,
        grid=(grid,),
        in_specs=[spec for _, spec in ins] + [anywhere()] * len(after),
        out_specs=specs[0] if single else specs,
        out_shape=shapes[0] if single else shapes,
        scratch_shapes=list(scratch),
        input_output_aliases=alias or {},
        compiler_params=pltpu.CompilerParams(vmem_limit_bytes=VMEM_LIMIT),
        cost_estimate=pl.CostEstimate(flops=0, bytes_accessed=0, transcendentals=0),
    )(*[array for array, _ in ins], *after)


def anywhere():
    return pl.BlockSpec(memory_space=pl.ANY)


def whole(array):
    return pl.BlockSpec(array.shape, lambda step: (0,) * len(array.shape))


def columns(array, tile):
    return pl.BlockSpec((array.shape[0], tile), lambda step: (0, step))


def entire(*arrays):
    return [(array, whole(array)) for array in arrays]


def by_columns(tile, *arrays):
    return [(array, columns(array, tile)) for array in arrays]


def slice_kernel(source_ref, target_ref):
    target_ref[...] = source_ref[...]


def last_rows(array, rows):
    return pl.BlockSpec((rows, array.shape[1]), lambda step: (array.shape[0] // rows - 1, 0))


def tail_of(array, rows):
    return call(slice_kernel, 1, [(array, last_rows(array, rows))], entire(bf16(rows, array.shape[1]))[0])


def touch_kernel(source_ref, target_ref):
    pass


def touched(array, *after):
    shape = jax.ShapeDtypeStruct(array.shape, array.dtype)
    return call(touch_kernel, 1, [(array, anywhere())], (shape, anywhere()), (), after, {0: 0})


def payload_kernel(device_ref, flag_ref, gate_ref, tokens_ref, first_ref, second_ref):
    top, tok = device_ref.shape
    cut = second_ref.shape[1]
    gate = gate_ref[...]
    high = gate.astype(BF16).astype(F32)
    mid = (gate - high).astype(BF16).astype(F32)
    low = gate - high - mid
    parts = [device_ref[...].astype(F32), flag_ref[...].astype(F32), high, mid, low]
    filler = jnp.zeros((LANES - len(parts) * top, tok), F32)
    first_ref[:, :cut] = tokens_ref[:, :cut]
    first_ref[:, cut:] = jnp.concatenate(parts + [filler], axis=0).T.astype(BF16)
    second_ref[...] = tokens_ref[:, cut:]


def payloads(routes, tokens, *after):
    tok, width = tokens.shape
    outs = entire(bf16(tok, width // 2 + LANES), bf16(tok, width // 2))
    return call(payload_kernel, 1, entire(*routes, tokens), outs, (), after)


def plan_rows(part, top, cap, half, sel_ref, gate_ref, kind_ref, mix_ref):
    rows, tok = sel_ref.shape
    me = lax.axis_index("expert")
    first = (lax.div(me, half) * half).astype(F32)
    devices = [part(0, k) for k in range(top)]
    dest = iota((LANES, tok), 0)
    inside = dest < half
    dest = dest + first
    none = jnp.zeros((LANES, tok), F32)
    hit, spare, high, mid, low = none, none, none, none, none
    for k in range(top):
        partner = devices[k] + jnp.where(devices[k] < half, 1.0 * half, -1.0 * half)
        wants = part(1, k)
        for other in devices:
            wants = jnp.where(other == partner, 0.0, wants)
        named = (dest == devices[k]) & inside
        hit = jnp.where(named, 1.0, hit)
        spare = jnp.where(named, wants, spare)
        high = jnp.where(named, part(2, k), high)
        mid = jnp.where(named, part(3, k), mid)
        low = jnp.where(named, part(4, k), low)
    place = dot(hit.astype(BF16), before_mask(tok))
    place = jnp.where(hit > 0.5, place, -1.0)
    group, at = row_of(rows, cap, LANES)
    spread = (iota((rows, LANES), 1) == group).astype(BF16)
    to_rows = lambda table: dot(spread, table.astype(BF16))
    chosen = jnp.where(to_rows(place) == at, 1.0, jnp.zeros((rows, tok), F32))
    of_row = lambda table: jnp.sum(chosen * table, axis=1, keepdims=True)
    high, mid, low = to_rows(high), to_rows(mid), to_rows(low)
    sel_ref[...] = chosen.astype(BF16)
    gate_ref[...] = jnp.broadcast_to(of_row(high + mid + low), (rows, LANES))
    mix_ref[:tok] = (chosen * high).T.astype(BF16)
    mix_ref[tok:] = (chosen * mid).T.astype(BF16)
    is_spare = of_row(to_rows(spare))
    is_main = of_row(1.0) - is_spare
    lane = iota((rows, LANES), 1)
    kind = jnp.where(lane == 0.0, is_main, jnp.where(lane == 1.0, is_spare, 0.0))
    kind_ref[...] = kind.astype(BF16)


def packed_rows(sel_ref, gate_ref, tokens_ref, packed_ref):
    packed_ref[...] = (dot(sel_ref[...], tokens_ref[...]) * gate_ref[:, :1]).astype(BF16)


def pack_steps(tiles, sel_ref, gate_ref, kind_ref, tokens_ref, packed_ref):
    step = pl.program_id(0)

    @pl.when(step < tiles)
    def _():
        packed_rows(sel_ref, gate_ref, tokens_ref, packed_ref)

    @pl.when(step == tiles)
    def _():
        packed_ref[:, :LANES] = kind_ref[...]


def pack_own_kernel(cap, half, tiles, device_ref, flag_ref, gates_ref, tokens_ref, packed_ref, mix_ref, *plan):
    sel_ref, gate_ref, kind_ref = plan
    top = device_ref.shape[0]

    @pl.when(pl.program_id(0) == 0)
    def _():
        gate = gates_ref[...]
        high = gate.astype(BF16).astype(F32)
        mid = (gate - high).astype(BF16).astype(F32)
        tables = (device_ref[...].astype(F32), flag_ref[...].astype(F32), high, mid, gate - high - mid)
        part = lambda which, k: tables[which][k : k + 1]
        plan_rows(part, top, cap, half, sel_ref, gate_ref, kind_ref, mix_ref)

    pack_steps(tiles, sel_ref, gate_ref, kind_ref, tokens_ref, packed_ref)


def up_to(array, tile, tiles):
    return pl.BlockSpec((array.shape[0], tile), lambda step: (0, jnp.minimum(step, tiles - 1)))


def pack_own(routes, tokens, cap, half, tile):
    tok, width = tokens.shape
    rows, tiles = half * cap, width // tile
    return call(
        functools.partial(pack_own_kernel, cap, half, tiles),
        tiles + 1,
        entire(*routes) + [(tokens, up_to(tokens, tile, tiles))],
        by_columns(tile, bf16(rows, width + LANES)) + entire(bf16(2 * tok, rows)),
        [pltpu.VMEM((rows, tok), BF16), pltpu.VMEM((rows, LANES), F32), pltpu.VMEM((rows, LANES), BF16)],
    )


def pack_first_kernel(cap, top, half, tiles, meta_ref, tokens_ref, packed_ref, sel_ref, gate_ref, mix_ref, kind_ref):
    @pl.when(pl.program_id(0) == 0)
    def _():
        meta = meta_ref[...].astype(F32).T
        part = lambda which, k: meta[which * top + k : which * top + k + 1]
        plan_rows(part, top, cap, half, sel_ref, gate_ref, kind_ref, mix_ref)

    pack_steps(tiles, sel_ref, gate_ref, kind_ref, tokens_ref, packed_ref)


def last_columns(array):
    return pl.BlockSpec((array.shape[0], LANES), lambda step: (0, array.shape[1] // LANES - 1))


def pack_first(payload, cap, top, half, tile, *after):
    tok, wide = payload.shape
    rows, tiles = half * cap, (wide - LANES) // tile
    return call(
        functools.partial(pack_first_kernel, cap, top, half, tiles),
        tiles + 1,
        [(payload, last_columns(payload)), (payload, up_to(payload, tile, tiles))],
        by_columns(tile, bf16(rows, wide)) + entire(bf16(rows, tok), f32(rows, LANES), bf16(2 * tok, rows)),
        [pltpu.VMEM((rows, LANES), BF16)],
        after,
    )


def pack(sel, gate, tokens, tile, *after):
    rows, width = sel.shape[0], tokens.shape[1]
    return call(
        packed_rows,
        width // tile,
        entire(sel, gate) + by_columns(tile, tokens),
        by_columns(tile, bf16(rows, width))[0],
        after=after,
    )


def slots_of(kind_ref, other_ref, second, main, spare):
    rows = kind_ref.shape[0]
    kind = kind_ref[...]
    lower = (iota((rows, rows), 1) < iota((rows, rows), 0)).astype(BF16)
    ahead = jnp.sum(other_ref[...].astype(F32), axis=0, keepdims=True)
    rank = dot(lower, kind) + jnp.where(second, ahead, 0.0)
    kind = kind.astype(F32)
    fits = lambda lane, limit: (kind[:, lane : lane + 1] > 0.5) & (rank[:, lane : lane + 1] < limit)
    slot = jnp.where(fits(1, spare), rank[:, 1:2] + (main + 1.0), 0.0)
    return jnp.where(fits(0, main), rank[:, 0:1] + 1.0, slot)


def upper_half(half):
    return lax.axis_index("expert") >= half


def project_kernel(hidden_ref, spare_ref, near_ref, far_ref, main_out, spare_out, near_turned, far_turned, stack_ref):
    main, half = main_out.shape[0], near_ref.shape[0]

    @pl.when(pl.program_id(0) == 0)
    def _():
        core = lax.axis_index("dp")
        for at, which, turned_ref in ((0, core, near_turned), (half, 1 - core, far_turned)):
            start = pl.multiple_of(which * half, LANES)
            stack_ref[:main, at : at + half] = hidden_ref[:main, pl.ds(start, half)]
            stack_ref[main:, at : at + half] = spare_ref[:, pl.ds(start, half)]
            turned_ref[...] = stack_ref[:, at : at + half].T

    total = dot(stack_ref[:, :half], near_ref[...]) + dot(stack_ref[:, half:], far_ref[...])
    total = total.astype(BF16)
    main_out[...] = total[:main]
    spare_out[...] = total[main:]


def project(hidden, spare_hidden, near, far, tile, *after):
    half, width = near.shape
    spare = spare_hidden.shape[0]
    slots = hidden.shape[0]
    turned = [bf16(half, slots), bf16(half, slots)]
    return call(
        project_kernel,
        width // tile,
        entire(hidden, spare_hidden) + by_columns(tile, near, far),
        by_columns(tile, bf16(slots - spare, width), bf16(spare, width)) + entire(*turned),
        [pltpu.VMEM(hidden.shape, BF16)],
        after,
    )


def given_rows(slot_ref, main_ref, spare_ref, out_ref):
    main = main_ref.shape[0]
    packed = dot(slot_ref[:, :main], main_ref[...]) + dot(slot_ref[:, main:], spare_ref[...])
    out_ref[...] = packed.astype(BF16)


def give_plan_kernel(half, mirrored, kind_ref, other_ref, main_ref, spare_ref, out_ref, slot_ref):
    rows, slots = slot_ref.shape
    main, spare = main_ref.shape[0], spare_ref.shape[0]

    @pl.when(pl.program_id(0) == 0)
    def _():
        slot = slots_of(kind_ref, other_ref, upper_half(half) != mirrored, main, spare)
        slot_ref[...] = (iota((rows, slots), 1) + 1.0 == slot).astype(BF16)

    given_rows(slot_ref, main_ref, spare_ref, out_ref)


def give_plan(kind, other, out_main, out_spare, half, mirrored, width, tile, *after):
    main, spare, rows = out_main.shape[0], out_spare.shape[0], kind.shape[0]
    ins = [(kind, last_columns(kind)), (other, last_columns(other))]
    return call(
        functools.partial(give_plan_kernel, half, mirrored),
        width // tile,
        ins + by_columns(tile, out_main, out_spare),
        by_columns(tile, bf16(rows, width)) + entire(bf16(rows, main + spare)),
        after=after,
    )


def later(array, tile, first):
    return pl.BlockSpec((array.shape[0], tile), lambda step: (0, step + first))


def give(slot, out_main, out_spare, first, tile, *after):
    width = out_main.shape[1] - first * tile
    return call(
        given_rows,
        width // tile,
        entire(slot) + [(array, later(array, tile, first)) for array in (out_main, out_spare)],
        by_columns(tile, bf16(slot.shape[0], width))[0],
        after=after,
    )


def take_kernel(half, cut, own_kind, mirror_kind, own_ref, first_ref, second_ref, *rest):
    main_ref, spare_ref, own_slot, mirror_slot = rest
    main, spare = main_ref.shape[0], spare_ref.shape[0]
    slots, rows = own_slot.shape
    step = pl.program_id(0)

    @pl.when(step == 0)
    def _():
        upper = upper_half(half)
        pairs = (
            (own_kind, mirror_kind, upper, own_slot),
            (mirror_kind, own_kind, jnp.logical_not(upper), mirror_slot),
        )
        for kind, other, second, out_ref in pairs:
            slot = slots_of(kind, other, second, main, spare)
            slot = jnp.broadcast_to(slot, (rows, LANES)).T[0:1]
            out_ref[...] = (iota((slots, rows), 0) + 1.0 == slot).astype(BF16)

    mirror = jnp.where(step < cut, first_ref[...], second_ref[...])
    total = dot(own_slot[...], own_ref[...]) + dot(mirror_slot[...], mirror)
    total = total.astype(BF16)
    main_ref[...] = total[:main]
    spare_ref[...] = total[main:]


def from_step(array, tile, first):
    return pl.BlockSpec((array.shape[0], tile), lambda step: (0, jnp.maximum(step - first, 0)))


def take(own, first, second, main, spare, half, tile, *after):
    rows = own.shape[0]
    width = own.shape[1] - LANES
    cut = second.shape[1] // tile
    ins = [(own, last_columns(own)), (first, last_columns(first))] + by_columns(tile, own)
    ins += [(first, up_to(first, tile, cut)), (second, from_step(second, tile, cut))]
    return call(
        functools.partial(take_kernel, half, cut),
        width // tile,
        ins,
        by_columns(tile, bf16(main, width), bf16(spare, width)),
        [pltpu.VMEM((main + spare, rows), BF16), pltpu.VMEM((main + spare, rows), BF16)],
        after,
    )


def mixed(mix_ref, rows_ref):
    both = dot(mix_ref[...], rows_ref[...])
    tok = both.shape[0] // 2
    return both[:tok] + both[tok:]


def part_kernel(mix_ref, rows_ref, part_ref):
    part_ref[...] = mixed(mix_ref, rows_ref).astype(BF16)


def total_kernel(cut, mix_ref, rows_ref, first_ref, second_ref, total_ref):
    other = jnp.where(pl.program_id(0) < cut, first_ref[...], second_ref[...]).astype(F32)
    total_ref[...] = (mixed(mix_ref, rows_ref) + other).astype(BF16)


def combine(mix, rows, others, tile, *after):
    width = rows.shape[1]
    body, more = part_kernel, []
    if others:
        cut = others[1].shape[1] // tile
        body = functools.partial(total_kernel, cut)
        more = [(others[0], up_to(others[0], tile, cut)), (others[1], from_step(others[1], tile, cut))]
    return call(
        body,
        width // tile,
        entire(mix) + by_columns(tile, rows) + more,
        by_columns(tile, bf16(mix.shape[0] // 2, width))[0],
        after=after,
    )


def stack_grads(main_ref, spare_ref, grads_ref):
    main = main_ref.shape[0]
    grads_ref[:main] = main_ref[...]
    grads_ref[main:] = spare_ref[...]


def weight_kernel(turned, other_turned, main_ref, spare_ref, other_main, other_spare, out_ref, grads_ref):
    stack_grads(main_ref, spare_ref, grads_ref)
    total = dot(turned[...], grads_ref[...])
    stack_grads(other_main, other_spare, grads_ref)
    out_ref[...] = (total + dot(other_turned[...], grads_ref[...])).astype(BF16)


def weight_grad(turned, other_turned, grads, other_grads, tile, *after):
    half, slots = turned.shape
    width = grads[0].shape[1]
    return call(
        weight_kernel,
        width // tile,
        entire(turned, other_turned) + by_columns(tile, *grads, *other_grads),
        by_columns(tile, bf16(half, width))[0],
        [pltpu.VMEM((slots, tile), BF16)],
        after,
    )


def back_kernel(main_ref, grad_ref, near_ref, far_ref, back_ref, spare_ref, sum_ref, grads_ref):
    step = pl.program_id(0)
    half = near_ref.shape[0]
    main = main_ref.shape[0]

    @pl.when(step == 0)
    def _():
        sum_ref[...] = jnp.zeros_like(sum_ref)

    stack_grads(main_ref, grad_ref, grads_ref)
    sum_ref[:, :half] += dot(grads_ref[...], near_ref[...], 1, 1)
    sum_ref[:, half:] += dot(grads_ref[...], far_ref[...], 1, 1)

    @pl.when(step == pl.num_programs(0) - 1)
    def _():
        core = lax.axis_index("dp")
        for at, which in ((0, core), (half, 1 - core)):
            start = pl.multiple_of(which * half, LANES)
            total = sum_ref[:, at : at + half].astype(BF16)
            back_ref[:, pl.ds(start, half)] = total
            spare_ref[:, pl.ds(start, half)] = total[main:]


def project_back(grads_main, grads_spare, near, far, tile, *after):
    main, width = grads_main.shape
    spare = grads_spare.shape[0]
    half = near.shape[0]
    slots = main + spare
    return call(
        back_kernel,
        width // tile,
        by_columns(tile, grads_main, grads_spare, near, far),
        entire(bf16(slots, 2 * half), bf16(spare, 2 * half)),
        [pltpu.VMEM((slots, 2 * half), F32), pltpu.VMEM((slots, tile), BF16)],
        after,
    )


def place_kernel(back_ref, spare_ref, out_ref):
    out_ref[...] = spare_ref[...]


def with_spare(back, back_spare, *after):
    slots, hid = back.shape
    spare = back_spare.shape[0]
    last = pl.BlockSpec((spare, hid), lambda step: (slots // spare - 1, 0))
    ins = [(back, anywhere())] + entire(back_spare)
    return call(place_kernel, 1, ins, (bf16(slots, hid), last), (), after, {0: 0})


def local(hidden_saved, down_weight, route_device, replica_flag, gate_values, grad_out):
    count = lax.axis_size("expert")
    half = count // 2
    tok, top = route_device.shape
    width = grad_out.shape[1]
    cap = 5 * tok * top // (4 * count)
    main = 3 * tok * top // 4
    hidden = hidden_saved[0, 0]
    near = down_weight[0]
    slots = hidden.shape[0]
    tile = width // 4
    groups = [list(range(half)), list(range(half, count))]

    def to_half(rows):
        return lax.all_to_all(
            rows.reshape(half, cap, -1), "expert", 0, 0, axis_index_groups=groups, tiled=True
        ).reshape(half * cap, -1)

    spare = slots - main
    routes = (route_device.T, replica_flag.T, gate_values.T)
    spare_hidden = swapped(tail_of(hidden, spare), "expert", half)
    far = swapped(near, "dp", 1)
    packed_own, mix_own = pack_own(routes, grad_out, cap, half, tile)
    arrived_own = to_half(touched(packed_own, spare_hidden))
    mirrors = [swapped(part, "expert", half) for part in payloads(routes, grad_out, spare_hidden)]
    out_main, out_spare, turned, far_turned = project(
        hidden, spare_hidden, near, far, tile, mix_own
    )
    other_turned = swapped(far_turned, "dp", 1)
    packed_first, sel, gate, mix_mirror = pack_first(mirrors[0], cap, top, half, tile, out_spare)
    arrived_first = to_half(packed_first)
    packed_second = pack(sel, gate, mirrors[1], tile)
    out_spare = swapped(out_spare, "expert", half)
    arrived_second = to_half(packed_second)
    given_first, slot_mirror = give_plan(
        arrived_first, arrived_own, out_main, out_spare, half, True, width // 2, tile
    )
    returned_first = to_half(given_first)
    given_second = give(slot_mirror, out_main, out_spare, width // 2 // tile, tile)
    returned_second = to_half(given_second)
    grads_main, grads_spare = take(
        arrived_own, arrived_first, arrived_second, main, spare, half, tile, given_second
    )
    given_own, _ = give_plan(
        arrived_own, arrived_first, out_main, out_spare, half, False, width, tile, grads_spare
    )
    returned_own = to_half(given_own)
    other_main = swapped(grads_main, "dp", 1)
    grads_spare = swapped(grads_spare, "expert", half)
    other_spare = swapped(grads_spare, "dp", 1)
    part_first = combine(mix_mirror, returned_first, [], tile, given_own)
    part_second = combine(mix_mirror, returned_second, [], tile, part_first)
    back, back_spare = project_back(grads_main, grads_spare, near, far, tile, part_second)
    grad_weight = weight_grad(
        turned, other_turned, (grads_main, grads_spare), (other_main, other_spare), tile, back
    )
    parts = [swapped(part, "expert", half) for part in (part_first, part_second)]
    back_spare = swapped(back_spare, "expert", half)
    layer_out = combine(mix_own, returned_own, parts, tile, grad_weight)
    grad_hidden = with_spare(back, back_spare, layer_out)
    return (layer_out, grad_hidden[None, None], grad_weight[None])


def solution(mesh):
    in_specs = (
        P("dp", "expert", None, None),
        P("expert", "dp", None),
        P(("dp", "expert"), None),
        P(("dp", "expert"), None),
        P(("dp", "expert"), None),
        P(("dp", "expert"), None),
    )
    out_specs = (P(("dp", "expert"), None), P("dp", "expert", None, None), P("expert", "dp", None))
    return jax.shard_map(local, mesh=mesh, in_specs=in_specs, out_specs=out_specs, check_vma=False)
```

```python
import functools
import jax
import jax.numpy as jnp
from jax import lax
from jax.experimental import pallas as pl
from jax.experimental.pallas import tpu as pltpu
from jax.sharding import PartitionSpec as P

F32, BF16, I32 = jnp.float32, jnp.bfloat16, jnp.int32
LANES = 128
LONG = 4_000_000_000_000
VMEM_LIMIT = 60 * 1024 * 1024


def swapped(value, axis, distance):
    count = lax.axis_size(axis)
    pairs = [(source, (source + distance) % count) for source in range(count)]
    return lax.ppermute(value, axis, pairs)


def dot(left, right, left_dim=1, right_dim=0):
    contract = (((left_dim,), (right_dim,)), ((), ()))
    return lax.dot_general(left, right, contract, preferred_element_type=F32)


def iota(shape, dim):
    return lax.broadcasted_iota(I32, shape, dim).astype(F32)


def row_of(rows, cap, lanes):
    row = iota((rows, lanes), 0)
    group = jnp.floor((row + 0.5) * (1.0 / cap))
    return group, row - group * cap


def before_mask(size):
    return (iota((size, size), 0) < iota((size, size), 1)).astype(BF16)


def bf16(*shape):
    return jax.ShapeDtypeStruct(shape, BF16)


def f32(*shape):
    return jax.ShapeDtypeStruct(shape, F32)


def call(body, grid, ins, outs, scratch=(), after=(), alias=None, cost=0):
    single = not isinstance(outs, list)
    pairs = [outs] if single else outs
    specs = [spec for _, spec in pairs]
    shapes = [shape for shape, _ in pairs]
    count = len(ins)

    def kernel(*refs):
        body(*refs[:count], *refs[count + len(after) :])

    return pl.pallas_call(
        kernel,
        grid=(grid,),
        in_specs=[spec for _, spec in ins] + [anywhere()] * len(after),
        out_specs=specs[0] if single else specs,
        out_shape=shapes[0] if single else shapes,
        scratch_shapes=list(scratch),
        input_output_aliases=alias or {},
        compiler_params=pltpu.CompilerParams(vmem_limit_bytes=VMEM_LIMIT),
        cost_estimate=pl.CostEstimate(flops=cost, bytes_accessed=0, transcendentals=0),
    )(*[array for array, _ in ins], *after)


def anywhere():
    return pl.BlockSpec(memory_space=pl.ANY)


def whole(array):
    return pl.BlockSpec(array.shape, lambda step: (0,) * len(array.shape))


def columns(array, tile):
    return pl.BlockSpec((array.shape[0], tile), lambda step: (0, step))


def entire(*arrays):
    return [(array, whole(array)) for array in arrays]


def by_columns(tile, *arrays):
    return [(array, columns(array, tile)) for array in arrays]


def slice_kernel(source_ref, target_ref):
    target_ref[...] = source_ref[...]


def last_rows(array, rows):
    return pl.BlockSpec((rows, array.shape[1]), lambda step: (array.shape[0] // rows - 1, 0))


def tail_of(array, rows):
    return call(slice_kernel, 1, [(array, last_rows(array, rows))], entire(bf16(rows, array.shape[1]))[0])


def touch_kernel(source_ref, target_ref):
    pass


def touched(array, *after):
    shape = jax.ShapeDtypeStruct(array.shape, array.dtype)
    return call(touch_kernel, 1, [(array, anywhere())], (shape, anywhere()), (), after, {0: 0})


def payload_kernel(device_ref, flag_ref, gate_ref, tokens_ref, first_ref, second_ref):
    top, tok = device_ref.shape
    cut = second_ref.shape[1]
    gate = gate_ref[...]
    high = gate.astype(BF16).astype(F32)
    mid = (gate - high).astype(BF16).astype(F32)
    low = gate - high - mid
    parts = [device_ref[...].astype(F32), flag_ref[...].astype(F32), high, mid, low]
    filler = jnp.zeros((LANES - len(parts) * top, tok), F32)
    first_ref[:, :cut] = tokens_ref[:, :cut]
    first_ref[:, cut:] = jnp.concatenate(parts + [filler], axis=0).T.astype(BF16)
    second_ref[...] = tokens_ref[:, cut:]


def payloads(routes, tokens, *after):
    tok, width = tokens.shape
    outs = entire(bf16(tok, width // 2 + LANES), bf16(tok, width // 2))
    return call(payload_kernel, 1, entire(*routes, tokens), outs, (), after)


def plan_rows(part, top, cap, half, sel_ref, gate_ref, kind_ref, mix_ref):
    rows, tok = sel_ref.shape
    me = lax.axis_index("expert")
    first = (lax.div(me, half) * half).astype(F32)
    devices = [part(0, k) for k in range(top)]
    dest = iota((LANES, tok), 0)
    inside = dest < half
    dest = dest + first
    none = jnp.zeros((LANES, tok), F32)
    hit, spare, high, mid, low = none, none, none, none, none
    for k in range(top):
        partner = devices[k] + jnp.where(devices[k] < half, 1.0 * half, -1.0 * half)
        wants = part(1, k)
        for other in devices:
            wants = jnp.where(other == partner, 0.0, wants)
        named = (dest == devices[k]) & inside
        hit = jnp.where(named, 1.0, hit)
        spare = jnp.where(named, wants, spare)
        high = jnp.where(named, part(2, k), high)
        mid = jnp.where(named, part(3, k), mid)
        low = jnp.where(named, part(4, k), low)
    place = dot(hit.astype(BF16), before_mask(tok))
    place = jnp.where(hit > 0.5, place, -1.0)
    group, at = row_of(rows, cap, LANES)
    spread = (iota((rows, LANES), 1) == group).astype(BF16)
    to_rows = lambda table: dot(spread, table.astype(BF16))
    chosen = jnp.where(to_rows(place) == at, 1.0, jnp.zeros((rows, tok), F32))
    of_row = lambda table: jnp.sum(chosen * table, axis=1, keepdims=True)
    high, mid, low = to_rows(high), to_rows(mid), to_rows(low)
    sel_ref[...] = chosen.astype(BF16)
    gate_ref[...] = jnp.broadcast_to(of_row(high + mid + low), (rows, LANES))
    mix_ref[:tok] = (chosen * high).T.astype(BF16)
    mix_ref[tok:] = (chosen * mid).T.astype(BF16)
    is_spare = of_row(to_rows(spare))
    is_main = of_row(1.0) - is_spare
    lane = iota((rows, LANES), 1)
    kind = jnp.where(lane == 0.0, is_main, jnp.where(lane == 1.0, is_spare, 0.0))
    kind_ref[...] = kind.astype(BF16)


def packed_rows(sel_ref, gate_ref, tokens_ref, packed_ref):
    packed_ref[...] = (dot(sel_ref[...], tokens_ref[...]) * gate_ref[:, :1]).astype(BF16)


def pack_steps(tiles, sel_ref, gate_ref, kind_ref, tokens_ref, packed_ref):
    step = pl.program_id(0)

    @pl.when(step < tiles)
    def _():
        packed_rows(sel_ref, gate_ref, tokens_ref, packed_ref)

    @pl.when(step == tiles)
    def _():
        packed_ref[:, :LANES] = kind_ref[...]


def pack_own_kernel(cap, half, tiles, device_ref, flag_ref, gates_ref, tokens_ref, packed_ref, mix_ref, *plan):
    sel_ref, gate_ref, kind_ref = plan
    top = device_ref.shape[0]

    @pl.when(pl.program_id(0) == 0)
    def _():
        gate = gates_ref[...]
        high = gate.astype(BF16).astype(F32)
        mid = (gate - high).astype(BF16).astype(F32)
        tables = (device_ref[...].astype(F32), flag_ref[...].astype(F32), high, mid, gate - high - mid)
        part = lambda which, k: tables[which][k : k + 1]
        plan_rows(part, top, cap, half, sel_ref, gate_ref, kind_ref, mix_ref)

    pack_steps(tiles, sel_ref, gate_ref, kind_ref, tokens_ref, packed_ref)


def up_to(array, tile, tiles):
    return pl.BlockSpec((array.shape[0], tile), lambda step: (0, jnp.minimum(step, tiles - 1)))


def pack_own(routes, tokens, cap, half, tile):
    tok, width = tokens.shape
    rows, tiles = half * cap, width // tile
    return call(
        functools.partial(pack_own_kernel, cap, half, tiles),
        tiles + 1,
        entire(*routes) + [(tokens, up_to(tokens, tile, tiles))],
        by_columns(tile, bf16(rows, width + LANES)) + entire(bf16(2 * tok, rows)),
        [pltpu.VMEM((rows, tok), BF16), pltpu.VMEM((rows, LANES), F32), pltpu.VMEM((rows, LANES), BF16)],
    )


def pack_first_kernel(cap, top, half, tiles, meta_ref, tokens_ref, packed_ref, sel_ref, gate_ref, mix_ref, kind_ref):
    @pl.when(pl.program_id(0) == 0)
    def _():
        meta = meta_ref[...].astype(F32).T
        part = lambda which, k: meta[which * top + k : which * top + k + 1]
        plan_rows(part, top, cap, half, sel_ref, gate_ref, kind_ref, mix_ref)

    pack_steps(tiles, sel_ref, gate_ref, kind_ref, tokens_ref, packed_ref)


def last_columns(array):
    return pl.BlockSpec((array.shape[0], LANES), lambda step: (0, array.shape[1] // LANES - 1))


def pack_first(payload, cap, top, half, tile, *after):
    tok, wide = payload.shape
    rows, tiles = half * cap, (wide - LANES) // tile
    return call(
        functools.partial(pack_first_kernel, cap, top, half, tiles),
        tiles + 1,
        [(payload, last_columns(payload)), (payload, up_to(payload, tile, tiles))],
        by_columns(tile, bf16(rows, wide)) + entire(bf16(rows, tok), f32(rows, LANES), bf16(2 * tok, rows)),
        [pltpu.VMEM((rows, LANES), BF16)],
        after,
    )


def pack(sel, gate, tokens, tile, *after):
    rows, width = sel.shape[0], tokens.shape[1]
    return call(
        packed_rows,
        width // tile,
        entire(sel, gate) + by_columns(tile, tokens),
        by_columns(tile, bf16(rows, width))[0],
        after=after,
        cost=LONG,
    )


def slots_of(kind_ref, other_ref, second, main, spare):
    rows = kind_ref.shape[0]
    kind = kind_ref[...]
    lower = (iota((rows, rows), 1) < iota((rows, rows), 0)).astype(BF16)
    ahead = jnp.sum(other_ref[...].astype(F32), axis=0, keepdims=True)
    rank = dot(lower, kind) + jnp.where(second, ahead, 0.0)
    kind = kind.astype(F32)
    fits = lambda lane, limit: (kind[:, lane : lane + 1] > 0.5) & (rank[:, lane : lane + 1] < limit)
    slot = jnp.where(fits(1, spare), rank[:, 1:2] + (main + 1.0), 0.0)
    return jnp.where(fits(0, main), rank[:, 0:1] + 1.0, slot)


def upper_half(half):
    return lax.axis_index("expert") >= half


def project_kernel(hidden_ref, spare_ref, near_ref, far_ref, main_out, spare_out, near_turned, far_turned, stack_ref):
    main, half = main_out.shape[0], near_ref.shape[0]

    @pl.when(pl.program_id(0) == 0)
    def _():
        core = lax.axis_index("dp")
        for at, which, turned_ref in ((0, core, near_turned), (half, 1 - core, far_turned)):
            start = pl.multiple_of(which * half, LANES)
            stack_ref[:main, at : at + half] = hidden_ref[:main, pl.ds(start, half)]
            stack_ref[main:, at : at + half] = spare_ref[:, pl.ds(start, half)]
            turned_ref[...] = stack_ref[:, at : at + half].T

    total = dot(stack_ref[:, :half], near_ref[...]) + dot(stack_ref[:, half:], far_ref[...])
    total = total.astype(BF16)
    main_out[...] = total[:main]
    spare_out[...] = total[main:]


def project(hidden, spare_hidden, near, far, tile, *after):
    half, width = near.shape
    spare = spare_hidden.shape[0]
    slots = hidden.shape[0]
    turned = [bf16(half, slots), bf16(half, slots)]
    return call(
        project_kernel,
        width // tile,
        entire(hidden, spare_hidden) + by_columns(tile, near, far),
        by_columns(tile, bf16(slots - spare, width), bf16(spare, width)) + entire(*turned),
        [pltpu.VMEM(hidden.shape, BF16)],
        after,
    )


def given_rows(slot_ref, main_ref, spare_ref, out_ref):
    main = main_ref.shape[0]
    packed = dot(slot_ref[:, :main], main_ref[...]) + dot(slot_ref[:, main:], spare_ref[...])
    out_ref[...] = packed.astype(BF16)


def give_plan_kernel(half, mirrored, kind_ref, other_ref, main_ref, spare_ref, out_ref, slot_ref):
    rows, slots = slot_ref.shape
    main, spare = main_ref.shape[0], spare_ref.shape[0]

    @pl.when(pl.program_id(0) == 0)
    def _():
        slot = slots_of(kind_ref, other_ref, upper_half(half) != mirrored, main, spare)
        slot_ref[...] = (iota((rows, slots), 1) + 1.0 == slot).astype(BF16)

    given_rows(slot_ref, main_ref, spare_ref, out_ref)


def give_plan(kind, other, out_main, out_spare, half, mirrored, width, tile, cost, *after):
    main, spare, rows = out_main.shape[0], out_spare.shape[0], kind.shape[0]
    ins = [(kind, last_columns(kind)), (other, last_columns(other))]
    return call(
        functools.partial(give_plan_kernel, half, mirrored),
        width // tile,
        ins + by_columns(tile, out_main, out_spare),
        by_columns(tile, bf16(rows, width)) + entire(bf16(rows, main + spare)),
        after=after,
        cost=cost,
    )


def later(array, tile, first):
    return pl.BlockSpec((array.shape[0], tile), lambda step: (0, step + first))


def give(slot, out_main, out_spare, first, tile, *after):
    width = out_main.shape[1] - first * tile
    return call(
        given_rows,
        width // tile,
        entire(slot) + [(array, later(array, tile, first)) for array in (out_main, out_spare)],
        by_columns(tile, bf16(slot.shape[0], width))[0],
        after=after,
    )


def take_kernel(half, cut, own_kind, mirror_kind, own_ref, first_ref, second_ref, *rest):
    main_ref, spare_ref, own_slot, mirror_slot = rest
    main, spare = main_ref.shape[0], spare_ref.shape[0]
    slots, rows = own_slot.shape
    step = pl.program_id(0)

    @pl.when(step == 0)
    def _():
        upper = upper_half(half)
        pairs = (
            (own_kind, mirror_kind, upper, own_slot),
            (mirror_kind, own_kind, jnp.logical_not(upper), mirror_slot),
        )
        for kind, other, second, out_ref in pairs:
            slot = slots_of(kind, other, second, main, spare)
            slot = jnp.broadcast_to(slot, (rows, LANES)).T[0:1]
            out_ref[...] = (iota((slots, rows), 0) + 1.0 == slot).astype(BF16)

    mirror = jnp.where(step < cut, first_ref[...], second_ref[...])
    total = dot(own_slot[...], own_ref[...]) + dot(mirror_slot[...], mirror)
    total = total.astype(BF16)
    main_ref[...] = total[:main]
    spare_ref[...] = total[main:]


def from_step(array, tile, first):
    return pl.BlockSpec((array.shape[0], tile), lambda step: (0, jnp.maximum(step - first, 0)))


def take(own, first, second, main, spare, half, tile, *after):
    rows = own.shape[0]
    width = own.shape[1] - LANES
    cut = second.shape[1] // tile
    ins = [(own, last_columns(own)), (first, last_columns(first))] + by_columns(tile, own)
    ins += [(first, up_to(first, tile, cut)), (second, from_step(second, tile, cut))]
    return call(
        functools.partial(take_kernel, half, cut),
        width // tile,
        ins,
        by_columns(tile, bf16(main, width), bf16(spare, width)),
        [pltpu.VMEM((main + spare, rows), BF16), pltpu.VMEM((main + spare, rows), BF16)],
        after,
    )


def mixed(mix_ref, rows_ref):
    both = dot(mix_ref[...], rows_ref[...])
    tok = both.shape[0] // 2
    return both[:tok] + both[tok:]


def part_kernel(mix_ref, rows_ref, part_ref):
    part_ref[...] = mixed(mix_ref, rows_ref).astype(BF16)


def total_kernel(cut, mix_ref, rows_ref, first_ref, second_ref, total_ref):
    other = jnp.where(pl.program_id(0) < cut, first_ref[...], second_ref[...]).astype(F32)
    total_ref[...] = (mixed(mix_ref, rows_ref) + other).astype(BF16)


def combine(mix, rows, others, tile, *after):
    width = rows.shape[1]
    body, more = part_kernel, []
    if others:
        cut = others[1].shape[1] // tile
        body = functools.partial(total_kernel, cut)
        more = [(others[0], up_to(others[0], tile, cut)), (others[1], from_step(others[1], tile, cut))]
    return call(
        body,
        width // tile,
        entire(mix) + by_columns(tile, rows) + more,
        by_columns(tile, bf16(mix.shape[0] // 2, width))[0],
        after=after,
    )


def stack_grads(main_ref, spare_ref, grads_ref):
    main = main_ref.shape[0]
    grads_ref[:main] = main_ref[...]
    grads_ref[main:] = spare_ref[...]


def weight_kernel(turned, other_turned, main_ref, spare_ref, other_main, other_spare, out_ref, grads_ref):
    stack_grads(main_ref, spare_ref, grads_ref)
    total = dot(turned[...], grads_ref[...])
    stack_grads(other_main, other_spare, grads_ref)
    out_ref[...] = (total + dot(other_turned[...], grads_ref[...])).astype(BF16)


def weight_grad(turned, other_turned, grads, other_grads, tile, *after):
    half, slots = turned.shape
    width = grads[0].shape[1]
    return call(
        weight_kernel,
        width // tile,
        entire(turned, other_turned) + by_columns(tile, *grads, *other_grads),
        by_columns(tile, bf16(half, width))[0],
        [pltpu.VMEM((slots, tile), BF16)],
        after,
    )


def back_kernel(main_ref, grad_ref, near_ref, far_ref, back_ref, spare_ref, sum_ref, grads_ref):
    step = pl.program_id(0)
    half = near_ref.shape[0]
    main = main_ref.shape[0]

    @pl.when(step == 0)
    def _():
        sum_ref[...] = jnp.zeros_like(sum_ref)

    stack_grads(main_ref, grad_ref, grads_ref)
    sum_ref[:, :half] += dot(grads_ref[...], near_ref[...], 1, 1)
    sum_ref[:, half:] += dot(grads_ref[...], far_ref[...], 1, 1)

    @pl.when(step == pl.num_programs(0) - 1)
    def _():
        core = lax.axis_index("dp")
        for at, which in ((0, core), (half, 1 - core)):
            start = pl.multiple_of(which * half, LANES)
            total = sum_ref[:, at : at + half].astype(BF16)
            back_ref[:, pl.ds(start, half)] = total
            spare_ref[:, pl.ds(start, half)] = total[main:]


def project_back(grads_main, grads_spare, near, far, tile, *after):
    main, width = grads_main.shape
    spare = grads_spare.shape[0]
    half = near.shape[0]
    slots = main + spare
    return call(
        back_kernel,
        width // tile,
        by_columns(tile, grads_main, grads_spare, near, far),
        entire(bf16(slots, 2 * half), bf16(spare, 2 * half)),
        [pltpu.VMEM((slots, 2 * half), F32), pltpu.VMEM((slots, tile), BF16)],
        after,
        cost=LONG,
    )


def place_kernel(back_ref, spare_ref, out_ref):
    out_ref[...] = spare_ref[...]


def with_spare(back, back_spare, *after):
    slots, hid = back.shape
    spare = back_spare.shape[0]
    last = pl.BlockSpec((spare, hid), lambda step: (slots // spare - 1, 0))
    ins = [(back, anywhere())] + entire(back_spare)
    return call(place_kernel, 1, ins, (bf16(slots, hid), last), (), after, {0: 0})


def local(hidden_saved, down_weight, route_device, replica_flag, gate_values, grad_out):
    count = lax.axis_size("expert")
    half = count // 2
    tok, top = route_device.shape
    width = grad_out.shape[1]
    cap = 5 * tok * top // (4 * count)
    main = 3 * tok * top // 4
    hidden = hidden_saved[0, 0]
    near = down_weight[0]
    slots = hidden.shape[0]
    tile = width // 4
    groups = [list(range(half)), list(range(half, count))]

    def to_half(rows):
        return lax.all_to_all(
            rows.reshape(half, cap, -1), "expert", 0, 0, axis_index_groups=groups, tiled=True
        ).reshape(half * cap, -1)

    spare = slots - main
    routes = (route_device.T, replica_flag.T, gate_values.T)
    spare_hidden = swapped(tail_of(hidden, spare), "expert", half)
    far = swapped(near, "dp", 1)
    packed_own, mix_own = pack_own(routes, grad_out, cap, half, tile)
    arrived_own = to_half(touched(packed_own, spare_hidden))
    mirrors = [swapped(part, "expert", half) for part in payloads(routes, grad_out, spare_hidden)]
    out_main, out_spare, turned, far_turned = project(
        hidden, spare_hidden, near, far, tile, mix_own
    )
    other_turned = swapped(far_turned, "dp", 1)
    packed_first, sel, gate, mix_mirror = pack_first(mirrors[0], cap, top, half, tile, out_spare)
    arrived_first = to_half(packed_first)
    packed_second = pack(sel, gate, mirrors[1], tile)
    out_spare = swapped(out_spare, "expert", half)
    arrived_second = to_half(packed_second)
    given_first, slot_mirror = give_plan(
        arrived_first, arrived_own, out_main, out_spare, half, True, width // 2, tile, LONG
    )
    returned_first = to_half(given_first)
    given_second = give(slot_mirror, out_main, out_spare, width // 2 // tile, tile)
    returned_second = to_half(given_second)
    grads_main, grads_spare = take(
        arrived_own, arrived_first, arrived_second, main, spare, half, tile, given_second
    )
    given_own, _ = give_plan(
        arrived_own, arrived_first, out_main, out_spare, half, False, width, tile, 0, grads_spare
    )
    returned_own = to_half(given_own)
    other_main = swapped(grads_main, "dp", 1)
    grads_spare = swapped(grads_spare, "expert", half)
    other_spare = swapped(grads_spare, "dp", 1)
    part_first = combine(mix_mirror, returned_first, [], tile, given_own)
    part_second = combine(mix_mirror, returned_second, [], tile, part_first)
    back, back_spare = project_back(grads_main, grads_spare, near, far, tile, part_second)
    grad_weight = weight_grad(
        turned, other_turned, (grads_main, grads_spare), (other_main, other_spare), tile, back
    )
    parts = [swapped(part, "expert", half) for part in (part_first, part_second)]
    back_spare = swapped(back_spare, "expert", half)
    layer_out = combine(mix_own, returned_own, parts, tile, grad_weight)
    grad_hidden = with_spare(back, back_spare, layer_out)
    return (layer_out, grad_hidden[None, None], grad_weight[None])


def solution(mesh):
    in_specs = (
        P("dp", "expert", None, None),
        P("expert", "dp", None),
        P(("dp", "expert"), None),
        P(("dp", "expert"), None),
        P(("dp", "expert"), None),
        P(("dp", "expert"), None),
    )
    out_specs = (P(("dp", "expert"), None), P("dp", "expert", None, None), P("expert", "dp", None))
    return jax.shard_map(local, mesh=mesh, in_specs=in_specs, out_specs=out_specs, check_vma=False)
```

```python
import functools
import jax
import jax.numpy as jnp
from jax import lax
from jax.experimental import pallas as pl
from jax.experimental.pallas import tpu as pltpu
from jax.sharding import PartitionSpec as P

F32, BF16, I32 = jnp.float32, jnp.bfloat16, jnp.int32
LANES = 128
LONG = 4_000_000_000_000
VMEM_LIMIT = 60 * 1024 * 1024


def swapped(value, axis, distance):
    count = lax.axis_size(axis)
    pairs = [(source, (source + distance) % count) for source in range(count)]
    return lax.ppermute(value, axis, pairs)


def dot(left, right, left_dim=1, right_dim=0):
    contract = (((left_dim,), (right_dim,)), ((), ()))
    return lax.dot_general(left, right, contract, preferred_element_type=F32)


def iota(shape, dim):
    return lax.broadcasted_iota(I32, shape, dim).astype(F32)


def row_of(rows, cap, lanes):
    row = iota((rows, lanes), 0)
    group = jnp.floor((row + 0.5) * (1.0 / cap))
    return group, row - group * cap


def before_mask(size):
    return (iota((size, size), 0) < iota((size, size), 1)).astype(BF16)


def bf16(*shape):
    return jax.ShapeDtypeStruct(shape, BF16)


def f32(*shape):
    return jax.ShapeDtypeStruct(shape, F32)


def call(body, grid, ins, outs, scratch=(), after=(), alias=None, cost=0):
    single = not isinstance(outs, list)
    pairs = [outs] if single else outs
    specs = [spec for _, spec in pairs]
    shapes = [shape for shape, _ in pairs]
    count = len(ins)

    def kernel(*refs):
        body(*refs[:count], *refs[count + len(after) :])

    return pl.pallas_call(
        kernel,
        grid=(grid,),
        in_specs=[spec for _, spec in ins] + [anywhere()] * len(after),
        out_specs=specs[0] if single else specs,
        out_shape=shapes[0] if single else shapes,
        scratch_shapes=list(scratch),
        input_output_aliases=alias or {},
        compiler_params=pltpu.CompilerParams(vmem_limit_bytes=VMEM_LIMIT),
        cost_estimate=pl.CostEstimate(flops=cost, bytes_accessed=0, transcendentals=0),
    )(*[array for array, _ in ins], *after)


def anywhere():
    return pl.BlockSpec(memory_space=pl.ANY)


def whole(array):
    return pl.BlockSpec(array.shape, lambda step: (0,) * len(array.shape))


def columns(array, tile):
    return pl.BlockSpec((array.shape[0], tile), lambda step: (0, step))


def entire(*arrays):
    return [(array, whole(array)) for array in arrays]


def by_columns(tile, *arrays):
    return [(array, columns(array, tile)) for array in arrays]


def head_kernel(device_ref, flag_ref, gate_ref, hidden_ref, meta_ref, spare_ref):
    top = device_ref.shape[0]
    codes = (device_ref[...] * 2 + flag_ref[...]).astype(F32)
    count = meta_ref.shape[0]
    meta_ref[:, :top, :] = jnp.broadcast_to(codes[None], (count, *codes.shape))
    meta_ref[:, top:, :] = jnp.broadcast_to(gate_ref[...][None], (count, *codes.shape))
    spare_ref[...] = hidden_ref[...]


def head(devices, flags, gates, hidden, spare, count):
    top, tok = devices.shape
    slots, hid = hidden.shape
    last = pl.BlockSpec((spare, hid), lambda step: (slots // spare - 1, 0))
    outs = entire(f32(count, 2 * top, tok), bf16(spare, hid))
    return call(head_kernel, 1, entire(devices, flags, gates) + [(hidden, last)], outs)


def copy_kernel(source_ref, target_ref):
    target_ref[...] = source_ref[...]


def copied(array, tile, *after):
    ins, outs = by_columns(tile, array), by_columns(tile, bf16(*array.shape))[0]
    return call(copy_kernel, array.shape[1] // tile, ins, outs, (), after)


def touch_kernel(source_ref, target_ref):
    pass


def touched(array, *after):
    shape = jax.ShapeDtypeStruct(array.shape, array.dtype)
    return call(touch_kernel, 1, [(array, anywhere())], (shape, anywhere()), (), after, {0: 0})


def plan_rows(meta, cap, half, sel_ref, gate_ref, mix_ref):
    rows, tok = sel_ref.shape
    top = meta.shape[0] // 2
    me = lax.axis_index("expert")
    first = (lax.div(me, half) * half).astype(F32)
    dest = iota((LANES, tok), 0)
    inside = dest < half
    dest = dest + first
    hit = jnp.zeros((LANES, tok), F32)
    gate = jnp.zeros((LANES, tok), F32)
    for k in range(top):
        device = jnp.floor(meta[k : k + 1] * 0.5)
        named = (dest == device) & inside
        hit = jnp.where(named, 1.0, hit)
        gate = jnp.where(named, meta[top + k : top + k + 1], gate)
    place = dot(hit.astype(BF16), before_mask(tok))
    place = jnp.where(hit > 0.5, place, -1.0)
    group, at = row_of(rows, cap, LANES)
    spread = (iota((rows, LANES), 1) == group).astype(BF16)
    to_rows = lambda table: dot(spread, table.astype(BF16))
    chosen = jnp.where(to_rows(place) == at, 1.0, jnp.zeros((rows, tok), F32))
    high = gate.astype(BF16).astype(F32)
    mid = (gate - high).astype(BF16).astype(F32)
    low = gate - high - mid
    high, mid, low = to_rows(high), to_rows(mid), to_rows(low)
    scale = jnp.sum(chosen * (high + mid + low), axis=1, keepdims=True)
    sel_ref[...] = chosen.astype(BF16)
    gate_ref[...] = jnp.broadcast_to(scale, (rows, LANES))
    mix_ref[:tok] = (chosen * high).T.astype(BF16)
    mix_ref[tok:] = (chosen * mid).T.astype(BF16)


def packed_rows(sel_ref, gate_ref, tokens_ref, packed_ref):
    packed_ref[...] = (dot(sel_ref[...], tokens_ref[...]) * gate_ref[:, :1]).astype(BF16)


def pack_own_kernel(cap, half, meta_ref, tokens_ref, packed_ref, mix_ref, sel_ref, gate_ref):
    @pl.when(pl.program_id(0) == 0)
    def _():
        plan_rows(meta_ref[0], cap, half, sel_ref, gate_ref, mix_ref)

    packed_rows(sel_ref, gate_ref, tokens_ref, packed_ref)


def pack_own(meta, tokens, cap, half, tile, *after):
    tok, width = tokens.shape
    rows = half * cap
    first = pl.BlockSpec((1, *meta.shape[1:]), lambda step: (0, 0, 0))
    return call(
        functools.partial(pack_own_kernel, cap, half),
        width // tile,
        [(meta, first)] + by_columns(tile, tokens),
        by_columns(tile, bf16(rows, width)) + entire(bf16(2 * tok, rows)),
        [pltpu.VMEM((rows, tok), BF16), pltpu.VMEM((rows, LANES), F32)],
        after,
    )


def pack(sel, gate, tokens, tile, *after):
    rows, width = sel.shape[0], tokens.shape[1]
    return call(
        packed_rows,
        width // tile,
        entire(sel, gate) + by_columns(tile, tokens),
        by_columns(tile, bf16(rows, width))[0],
        after=after,
        cost=LONG,
    )


def plan_kernel(cap, half, main, metas_ref, sel_ref, gate_ref, mix_ref, *slot_refs):
    count, tops, tok = metas_ref.shape
    top = tops // 2
    rows, slots = slot_refs[0].shape
    spare = slots - main
    me = lax.axis_index("expert")
    mirror = lax.rem(me + half, count)
    plan_rows(metas_ref[mirror], cap, half, sel_ref, gate_ref, mix_ref)

    mine, other = me.astype(F32), mirror.astype(F32)
    none = jnp.zeros((count, tok), F32)
    here, flag, clash = none, none, none
    for k in range(top):
        code = metas_ref[:, k, :]
        device = jnp.floor(code * 0.5)
        here = jnp.where(device == mine, 1.0, here)
        flag = jnp.where(device == mine, code - 2.0 * device, flag)
        clash = jnp.where(device == other, 1.0, clash)
    at_spare = here * flag * (1.0 - clash)
    at_main = here - at_spare
    before = before_mask(tok)
    ones = jnp.ones((tok, LANES), BF16)
    lower = (iota((count, count), 1) < iota((count, count), 0)).astype(BF16)

    def rank(flags):
        flags = flags.astype(BF16)
        return dot(flags, before) + dot(lower, dot(flags, ones).astype(BF16))

    rank_main, rank_spare = rank(at_main), rank(at_spare)
    slot = jnp.where((at_main > 0.5) & (rank_main < main), rank_main + 1.0, none)
    slot = jnp.where((at_spare > 0.5) & (rank_spare < spare), rank_spare + (main + 1.0), slot)
    place = jnp.where(here > 0.5, dot(here.astype(BF16), before), -1.0).astype(BF16)
    tens = jnp.floor(slot * (1.0 / 32.0))
    units = (slot - tens * 32.0).astype(BF16)
    tens = tens.astype(BF16)
    group, _ = row_of(rows, cap, count)
    _, at = row_of(rows, cap, tok)
    start = lax.div(me, half) * half
    for side, base in enumerate((start, lax.rem(start + half, count))):
        spread = (iota((rows, count), 1) == group + base.astype(F32)).astype(BF16)
        chosen = dot(spread, place) == at
        number = dot(spread, tens) * 32.0 + dot(spread, units)
        number = jnp.sum(jnp.where(chosen, number, 0.0), axis=1, keepdims=True)
        give_ref, take_ref = slot_refs[2 * side : 2 * side + 2]
        give_ref[...] = (iota((rows, slots), 1) + 1.0 == number).astype(BF16)
        number = jnp.broadcast_to(number, (rows, LANES)).T[0:1]
        take_ref[...] = (iota((slots, rows), 0) + 1.0 == number).astype(BF16)


def plan(metas, cap, half, main, slots):
    tok = metas.shape[2]
    rows = half * cap
    sides = [bf16(rows, slots), bf16(slots, rows)] * 2
    outs = entire(bf16(rows, tok), f32(rows, LANES), bf16(2 * tok, rows), *sides)
    return call(functools.partial(plan_kernel, cap, half, main), 1, entire(metas), outs)


def side_by_side(source, target_ref):
    half = target_ref.shape[1] // 2
    core = lax.axis_index("dp")
    for at, which in ((0, core), (half, 1 - core)):
        start = pl.multiple_of(which * half, LANES)
        target_ref[:, at : at + half] = source[: target_ref.shape[0], pl.ds(start, half)]


def projected(stack_ref, near_ref, far_ref, out_ref):
    half = near_ref.shape[0]
    total = dot(stack_ref[:, :half], near_ref[...]) + dot(stack_ref[:, half:], far_ref[...])
    out_ref[...] = total.astype(BF16)


def project_spare_kernel(spare_ref, near_ref, far_ref, out_ref, stack_ref):
    @pl.when(pl.program_id(0) == 0)
    def _():
        side_by_side(spare_ref, stack_ref)

    projected(stack_ref, near_ref, far_ref, out_ref)


def project_spare(spare_hidden, near, far, tile, *after):
    width = near.shape[1]
    return call(
        project_spare_kernel,
        width // tile,
        entire(spare_hidden) + by_columns(tile, near, far),
        by_columns(tile, bf16(spare_hidden.shape[0], width))[0],
        [pltpu.VMEM(spare_hidden.shape, BF16)],
        after,
    )


def project_kernel(hidden_ref, spare_ref, near_ref, far_ref, out_ref, near_turned, far_turned, stack_ref, side_ref):
    main, half = out_ref.shape[0], near_ref.shape[0]

    @pl.when(pl.program_id(0) == 0)
    def _():
        side_by_side(hidden_ref, stack_ref)
        side_by_side(spare_ref, side_ref)
        for at, turned_ref in ((0, near_turned), (half, far_turned)):
            turned_ref[:, :main] = stack_ref[:, at : at + half].T
            turned_ref[:, main:] = side_ref[:, at : at + half].T

    projected(stack_ref, near_ref, far_ref, out_ref)


def project(hidden, spare_hidden, near, far, tile, *after):
    half, width = near.shape
    spare = spare_hidden.shape[0]
    slots, hid = hidden.shape
    turned = [bf16(half, slots), bf16(half, slots)]
    return call(
        project_kernel,
        width // tile,
        entire(hidden, spare_hidden) + by_columns(tile, near, far),
        by_columns(tile, bf16(slots - spare, width)) + entire(*turned),
        [pltpu.VMEM((slots - spare, hid), BF16), pltpu.VMEM((spare, hid), BF16)],
        after,
    )


def give_kernel(own_slot, mirror_slot, main_ref, spare_ref, own_ref, mirror_ref):
    main = main_ref.shape[0]
    for slot_ref, out_ref in ((own_slot, own_ref), (mirror_slot, mirror_ref)):
        packed = dot(slot_ref[:, :main], main_ref[...]) + dot(slot_ref[:, main:], spare_ref[...])
        out_ref[...] = packed.astype(BF16)


def give(own_slot, mirror_slot, out_main, out_spare, tile):
    rows, width = own_slot.shape[0], out_main.shape[1]
    return call(
        give_kernel,
        width // tile,
        entire(own_slot, mirror_slot) + by_columns(tile, out_main, out_spare),
        by_columns(tile, bf16(rows, width), bf16(rows, width)),
    )


def take_kernel(own_slot, mirror_slot, own_ref, mirror_ref, main_ref, spare_ref):
    total = dot(own_slot[...], own_ref[...]) + dot(mirror_slot[...], mirror_ref[...])
    total = total.astype(BF16)
    main = main_ref.shape[0]
    main_ref[...] = total[:main]
    spare_ref[...] = total[main:]


def take(own_slot, mirror_slot, own, mirror, main, tile, *after):
    slots, width = own_slot.shape[0], own.shape[1]
    return call(
        take_kernel,
        width // tile,
        entire(own_slot, mirror_slot) + by_columns(tile, own, mirror),
        by_columns(tile, bf16(main, width), bf16(slots - main, width)),
        after=after,
    )


def mixed(mix_ref, rows_ref):
    both = dot(mix_ref[...], rows_ref[...])
    tok = both.shape[0] // 2
    return both[:tok] + both[tok:]


def part_kernel(mix_ref, rows_ref, part_ref):
    part_ref[...] = mixed(mix_ref, rows_ref).astype(BF16)


def total_kernel(mix_ref, rows_ref, other_ref, total_ref):
    total_ref[...] = (mixed(mix_ref, rows_ref) + other_ref[...].astype(F32)).astype(BF16)


def combine(mix, rows, others, tile, *after):
    width = rows.shape[1]
    return call(
        total_kernel if others else part_kernel,
        width // tile,
        entire(mix) + by_columns(tile, rows, *others),
        by_columns(tile, bf16(mix.shape[0] // 2, width))[0],
        after=after,
    )


def stack_grads(main_ref, spare_ref, grads_ref):
    main = main_ref.shape[0]
    grads_ref[:main] = main_ref[...]
    grads_ref[main:] = spare_ref[...]


def weight_kernel(turned, other_turned, main_ref, spare_ref, other_main, other_spare, out_ref, grads_ref):
    stack_grads(main_ref, spare_ref, grads_ref)
    total = dot(turned[...], grads_ref[...])
    stack_grads(other_main, other_spare, grads_ref)
    out_ref[...] = (total + dot(other_turned[...], grads_ref[...])).astype(BF16)


def weight_grad(turned, other_turned, grads, other_grads, tile, *after):
    half, slots = turned.shape
    width = grads[0].shape[1]
    return call(
        weight_kernel,
        width // tile,
        entire(turned, other_turned) + by_columns(tile, *grads, *other_grads),
        by_columns(tile, bf16(half, width))[0],
        [pltpu.VMEM((slots, tile), BF16)],
        after,
    )


def back_kernel(main_ref, grad_ref, near_ref, far_ref, back_ref, spare_ref, sum_ref, grads_ref):
    step = pl.program_id(0)
    half = near_ref.shape[0]
    main = main_ref.shape[0]

    @pl.when(step == 0)
    def _():
        sum_ref[...] = jnp.zeros_like(sum_ref)

    stack_grads(main_ref, grad_ref, grads_ref)
    sum_ref[:, :half] += dot(grads_ref[...], near_ref[...], 1, 1)
    sum_ref[:, half:] += dot(grads_ref[...], far_ref[...], 1, 1)

    @pl.when(step == pl.num_programs(0) - 1)
    def _():
        core = lax.axis_index("dp")
        for at, which in ((0, core), (half, 1 - core)):
            start = pl.multiple_of(which * half, LANES)
            total = sum_ref[:, at : at + half].astype(BF16)
            back_ref[:, pl.ds(start, half)] = total
            spare_ref[:, pl.ds(start, half)] = total[main:]


def project_back(grads_main, grads_spare, near, far, tile, *after):
    main, width = grads_main.shape
    spare = grads_spare.shape[0]
    half = near.shape[0]
    slots = main + spare
    return call(
        back_kernel,
        width // tile,
        by_columns(tile, grads_main, grads_spare, near, far),
        entire(bf16(slots, 2 * half), bf16(spare, 2 * half)),
        [pltpu.VMEM((slots, 2 * half), F32), pltpu.VMEM((slots, tile), BF16)],
        after,
    )


def place_kernel(back_ref, spare_ref, out_ref):
    out_ref[...] = spare_ref[...]


def with_spare(back, back_spare, *after):
    slots, hid = back.shape
    spare = back_spare.shape[0]
    last = pl.BlockSpec((spare, hid), lambda step: (slots // spare - 1, 0))
    ins = [(back, anywhere())] + entire(back_spare)
    return call(place_kernel, 1, ins, (bf16(slots, hid), last), (), after, {0: 0})


def local(hidden_saved, down_weight, route_device, replica_flag, gate_values, grad_out):
    count = lax.axis_size("expert")
    half = count // 2
    tok, top = route_device.shape
    width = grad_out.shape[1]
    cap = 5 * tok * top // (4 * count)
    main = 3 * tok * top // 4
    hidden = hidden_saved[0, 0]
    near = down_weight[0]
    slots = hidden.shape[0]
    tile = width // 4
    groups = [list(range(half)), list(range(half, count))]

    def to_half(rows):
        return lax.all_to_all(
            rows.reshape(half, cap, width), "expert", 0, 0, axis_index_groups=groups, tiled=True
        ).reshape(half * cap, width)

    far = swapped(near, "dp", 1)
    meta, spare_hidden = head(
        route_device.T, replica_flag.T, gate_values.T, hidden, slots - main, count
    )
    spare_hidden = swapped(spare_hidden, "expert", half)
    metas = lax.all_to_all(meta, "expert", 0, 0, tiled=True)
    packed_own, mix_own = pack_own(meta, grad_out, cap, half, tile)
    arrived_own = to_half(touched(packed_own, metas, spare_hidden, far))
    out_spare = project_spare(spare_hidden, near, far, tile, mix_own)
    sel, gate, mix_mirror, give_own, take_own, give_mirror, take_mirror = plan(
        metas, cap, half, main, slots
    )
    out_main, turned, far_turned = project(hidden, spare_hidden, near, far, tile, out_spare)
    out_spare = swapped(out_spare, "expert", half)
    mirror = swapped(touched(copied(grad_out, width // 2), out_spare, out_main, sel), "expert", half)
    other_turned = swapped(far_turned, "dp", 1)
    given_own, given_mirror = give(give_own, give_mirror, out_main, out_spare, tile)
    returned_mirror = to_half(touched(given_mirror, arrived_own))
    packed_mirror = pack(sel, gate, mirror, tile, given_own)
    arrived_mirror = to_half(touched(packed_mirror, returned_mirror))
    part = swapped(combine(mix_mirror, returned_mirror, [], tile), "expert", half)
    grads_main, grads_spare = take(take_own, take_mirror, arrived_own, arrived_mirror, main, tile)
    returned_own = to_half(touched(given_own, arrived_mirror, part))
    other_main = swapped(grads_main, "dp", 1)
    grads_spare = swapped(grads_spare, "expert", half)
    other_spare = swapped(grads_spare, "dp", 1)
    layer_out = combine(mix_own, returned_own, [part], tile)
    back, back_spare = project_back(grads_main, grads_spare, near, far, tile)
    back_spare = swapped(back_spare, "expert", half)
    grad_weight = weight_grad(
        turned, other_turned, (grads_main, grads_spare), (other_main, other_spare), tile, back
    )
    grad_hidden = with_spare(back, back_spare, layer_out, grad_weight)
    return (layer_out, grad_hidden[None, None], grad_weight[None])


def solution(mesh):
    in_specs = (
        P("dp", "expert", None, None),
        P("expert", "dp", None),
        P(("dp", "expert"), None),
        P(("dp", "expert"), None),
        P(("dp", "expert"), None),
        P(("dp", "expert"), None),
    )
    out_specs = (P(("dp", "expert"), None), P("dp", "expert", None, None), P("expert", "dp", None))
    return jax.shard_map(local, mesh=mesh, in_specs=in_specs, out_specs=out_specs, check_vma=False)
```

```python
import functools
import jax
import jax.numpy as jnp
from jax import lax
from jax.experimental import pallas as pl
from jax.experimental.pallas import tpu as pltpu
from jax.sharding import PartitionSpec as P

F32, BF16, I32 = jnp.float32, jnp.bfloat16, jnp.int32
LANES = 128
LONG = 4_000_000_000_000
GIVE_COST = 5_000_000_000
BACK_COST = 40_000_000_000
VMEM_LIMIT = 60 * 1024 * 1024


def swapped(value, axis, distance):
    count = lax.axis_size(axis)
    pairs = [(source, (source + distance) % count) for source in range(count)]
    return lax.ppermute(value, axis, pairs)


def dot(left, right, left_dim=1, right_dim=0):
    contract = (((left_dim,), (right_dim,)), ((), ()))
    return lax.dot_general(left, right, contract, preferred_element_type=F32)


def iota(shape, dim):
    return lax.broadcasted_iota(I32, shape, dim).astype(F32)


def row_of(rows, cap, lanes):
    row = iota((rows, lanes), 0)
    group = jnp.floor((row + 0.5) * (1.0 / cap))
    return group, row - group * cap


def before_mask(size):
    return (iota((size, size), 0) < iota((size, size), 1)).astype(BF16)


def bf16(*shape):
    return jax.ShapeDtypeStruct(shape, BF16)


def f32(*shape):
    return jax.ShapeDtypeStruct(shape, F32)


def call(body, grid, ins, outs, scratch=(), after=(), alias=None, cost=0):
    single = not isinstance(outs, list)
    pairs = [outs] if single else outs
    specs = [spec for _, spec in pairs]
    shapes = [shape for shape, _ in pairs]
    count = len(ins)

    def kernel(*refs):
        body(*refs[:count], *refs[count + len(after) :])

    return pl.pallas_call(
        kernel,
        grid=(grid,),
        in_specs=[spec for _, spec in ins] + [anywhere()] * len(after),
        out_specs=specs[0] if single else specs,
        out_shape=shapes[0] if single else shapes,
        scratch_shapes=list(scratch),
        input_output_aliases=alias or {},
        compiler_params=pltpu.CompilerParams(vmem_limit_bytes=VMEM_LIMIT),
        cost_estimate=pl.CostEstimate(flops=cost, bytes_accessed=0, transcendentals=0),
    )(*[array for array, _ in ins], *after)


def anywhere():
    return pl.BlockSpec(memory_space=pl.ANY)


def whole(array):
    return pl.BlockSpec(array.shape, lambda step: (0,) * len(array.shape))


def columns(array, tile):
    return pl.BlockSpec((array.shape[0], tile), lambda step: (0, step))


def entire(*arrays):
    return [(array, whole(array)) for array in arrays]


def by_columns(tile, *arrays):
    return [(array, columns(array, tile)) for array in arrays]


def head_kernel(device_ref, flag_ref, gate_ref, hidden_ref, meta_ref, spare_ref):
    top = device_ref.shape[0]
    codes = (device_ref[...] * 2 + flag_ref[...]).astype(F32)
    count = meta_ref.shape[0]
    meta_ref[:, :top, :] = jnp.broadcast_to(codes[None], (count, *codes.shape))
    meta_ref[:, top:, :] = jnp.broadcast_to(gate_ref[...][None], (count, *codes.shape))
    spare_ref[...] = hidden_ref[...]


def head(devices, flags, gates, hidden, spare, count):
    top, tok = devices.shape
    slots, hid = hidden.shape
    last = pl.BlockSpec((spare, hid), lambda step: (slots // spare - 1, 0))
    outs = entire(f32(count, 2 * top, tok), bf16(spare, hid))
    return call(head_kernel, 1, entire(devices, flags, gates) + [(hidden, last)], outs)


def copy_kernel(source_ref, target_ref):
    target_ref[...] = source_ref[...]


def copied(array, tile, *after):
    ins, outs = by_columns(tile, array), by_columns(tile, bf16(*array.shape))[0]
    return call(copy_kernel, array.shape[1] // tile, ins, outs, (), after)


def touch_kernel(source_ref, target_ref):
    pass


def touched(array, *after):
    shape = jax.ShapeDtypeStruct(array.shape, array.dtype)
    return call(touch_kernel, 1, [(array, anywhere())], (shape, anywhere()), (), after, {0: 0})


def plan_rows(meta, cap, half, sel_ref, gate_ref, mix_ref):
    rows, tok = sel_ref.shape
    top = meta.shape[0] // 2
    me = lax.axis_index("expert")
    first = (lax.div(me, half) * half).astype(F32)
    dest = iota((LANES, tok), 0)
    inside = dest < half
    dest = dest + first
    hit = jnp.zeros((LANES, tok), F32)
    gate = jnp.zeros((LANES, tok), F32)
    for k in range(top):
        device = jnp.floor(meta[k : k + 1] * 0.5)
        named = (dest == device) & inside
        hit = jnp.where(named, 1.0, hit)
        gate = jnp.where(named, meta[top + k : top + k + 1], gate)
    place = dot(hit.astype(BF16), before_mask(tok))
    place = jnp.where(hit > 0.5, place, -1.0)
    group, at = row_of(rows, cap, LANES)
    spread = (iota((rows, LANES), 1) == group).astype(BF16)
    to_rows = lambda table: dot(spread, table.astype(BF16))
    chosen = jnp.where(to_rows(place) == at, 1.0, jnp.zeros((rows, tok), F32))
    high = gate.astype(BF16).astype(F32)
    mid = (gate - high).astype(BF16).astype(F32)
    low = gate - high - mid
    high, mid, low = to_rows(high), to_rows(mid), to_rows(low)
    scale = jnp.sum(chosen * (high + mid + low), axis=1, keepdims=True)
    sel_ref[...] = chosen.astype(BF16)
    gate_ref[...] = jnp.broadcast_to(scale, (rows, LANES))
    mix_ref[:tok] = (chosen * high).T.astype(BF16)
    mix_ref[tok:] = (chosen * mid).T.astype(BF16)


def packed_rows(sel_ref, gate_ref, tokens_ref, packed_ref):
    packed_ref[...] = (dot(sel_ref[...], tokens_ref[...]) * gate_ref[:, :1]).astype(BF16)


def pack_own_kernel(cap, half, meta_ref, tokens_ref, packed_ref, mix_ref, sel_ref, gate_ref):
    @pl.when(pl.program_id(0) == 0)
    def _():
        plan_rows(meta_ref[0], cap, half, sel_ref, gate_ref, mix_ref)

    packed_rows(sel_ref, gate_ref, tokens_ref, packed_ref)


def pack_own(meta, tokens, cap, half, tile, *after):
    tok, width = tokens.shape
    rows = half * cap
    first = pl.BlockSpec((1, *meta.shape[1:]), lambda step: (0, 0, 0))
    return call(
        functools.partial(pack_own_kernel, cap, half),
        width // tile,
        [(meta, first)] + by_columns(tile, tokens),
        by_columns(tile, bf16(rows, width)) + entire(bf16(2 * tok, rows)),
        [pltpu.VMEM((rows, tok), BF16), pltpu.VMEM((rows, LANES), F32)],
        after,
    )


def pack(sel, gate, tokens, tile, *after):
    rows, width = sel.shape[0], tokens.shape[1]
    return call(
        packed_rows,
        width // tile,
        entire(sel, gate) + by_columns(tile, tokens),
        by_columns(tile, bf16(rows, width))[0],
        after=after,
        cost=LONG,
    )


def plan_kernel(cap, half, main, metas_ref, sel_ref, gate_ref, mix_ref, *slot_refs):
    count, tops, tok = metas_ref.shape
    top = tops // 2
    rows, slots = slot_refs[0].shape
    spare = slots - main
    me = lax.axis_index("expert")
    mirror = lax.rem(me + half, count)
    plan_rows(metas_ref[mirror], cap, half, sel_ref, gate_ref, mix_ref)

    mine, other = me.astype(F32), mirror.astype(F32)
    none = jnp.zeros((count, tok), F32)
    here, flag, clash = none, none, none
    for k in range(top):
        code = metas_ref[:, k, :]
        device = jnp.floor(code * 0.5)
        here = jnp.where(device == mine, 1.0, here)
        flag = jnp.where(device == mine, code - 2.0 * device, flag)
        clash = jnp.where(device == other, 1.0, clash)
    at_spare = here * flag * (1.0 - clash)
    at_main = here - at_spare
    before = before_mask(tok)
    ones = jnp.ones((tok, LANES), BF16)
    lower = (iota((count, count), 1) < iota((count, count), 0)).astype(BF16)

    def rank(flags):
        flags = flags.astype(BF16)
        return dot(flags, before) + dot(lower, dot(flags, ones).astype(BF16))

    rank_main, rank_spare = rank(at_main), rank(at_spare)
    slot = jnp.where((at_main > 0.5) & (rank_main < main), rank_main + 1.0, none)
    slot = jnp.where((at_spare > 0.5) & (rank_spare < spare), rank_spare + (main + 1.0), slot)
    place = jnp.where(here > 0.5, dot(here.astype(BF16), before), -1.0).astype(BF16)
    tens = jnp.floor(slot * (1.0 / 32.0))
    units = (slot - tens * 32.0).astype(BF16)
    tens = tens.astype(BF16)
    group, _ = row_of(rows, cap, count)
    _, at = row_of(rows, cap, tok)
    start = lax.div(me, half) * half
    for side, base in enumerate((start, lax.rem(start + half, count))):
        spread = (iota((rows, count), 1) == group + base.astype(F32)).astype(BF16)
        chosen = dot(spread, place) == at
        number = dot(spread, tens) * 32.0 + dot(spread, units)
        number = jnp.sum(jnp.where(chosen, number, 0.0), axis=1, keepdims=True)
        give_ref, take_ref = slot_refs[2 * side : 2 * side + 2]
        give_ref[...] = (iota((rows, slots), 1) + 1.0 == number).astype(BF16)
        number = jnp.broadcast_to(number, (rows, LANES)).T[0:1]
        take_ref[...] = (iota((slots, rows), 0) + 1.0 == number).astype(BF16)


def plan(metas, cap, half, main, slots):
    tok = metas.shape[2]
    rows = half * cap
    sides = [bf16(rows, slots), bf16(slots, rows)] * 2
    outs = entire(bf16(rows, tok), f32(rows, LANES), bf16(2 * tok, rows), *sides)
    return call(functools.partial(plan_kernel, cap, half, main), 1, entire(metas), outs)


def side_by_side(source, target_ref):
    half = target_ref.shape[1] // 2
    core = lax.axis_index("dp")
    for at, which in ((0, core), (half, 1 - core)):
        start = pl.multiple_of(which * half, LANES)
        target_ref[:, at : at + half] = source[: target_ref.shape[0], pl.ds(start, half)]


def projected(stack_ref, near_ref, far_ref, out_ref):
    half = near_ref.shape[0]
    total = dot(stack_ref[:, :half], near_ref[...]) + dot(stack_ref[:, half:], far_ref[...])
    out_ref[...] = total.astype(BF16)


def project_spare_kernel(spare_ref, near_ref, far_ref, out_ref, stack_ref):
    @pl.when(pl.program_id(0) == 0)
    def _():
        side_by_side(spare_ref, stack_ref)

    projected(stack_ref, near_ref, far_ref, out_ref)


def project_spare(spare_hidden, near, far, tile, *after):
    width = near.shape[1]
    return call(
        project_spare_kernel,
        width // tile,
        entire(spare_hidden) + by_columns(tile, near, far),
        by_columns(tile, bf16(spare_hidden.shape[0], width))[0],
        [pltpu.VMEM(spare_hidden.shape, BF16)],
        after,
    )


def project_kernel(hidden_ref, spare_ref, near_ref, far_ref, out_ref, near_turned, far_turned, stack_ref, side_ref):
    main, half = out_ref.shape[0], near_ref.shape[0]

    @pl.when(pl.program_id(0) == 0)
    def _():
        side_by_side(hidden_ref, stack_ref)
        side_by_side(spare_ref, side_ref)
        for at, turned_ref in ((0, near_turned), (half, far_turned)):
            turned_ref[:, :main] = stack_ref[:, at : at + half].T
            turned_ref[:, main:] = side_ref[:, at : at + half].T

    projected(stack_ref, near_ref, far_ref, out_ref)


def project(hidden, spare_hidden, near, far, tile, *after):
    half, width = near.shape
    spare = spare_hidden.shape[0]
    slots, hid = hidden.shape
    turned = [bf16(half, slots), bf16(half, slots)]
    return call(
        project_kernel,
        width // tile,
        entire(hidden, spare_hidden) + by_columns(tile, near, far),
        by_columns(tile, bf16(slots - spare, width)) + entire(*turned),
        [pltpu.VMEM((slots - spare, hid), BF16), pltpu.VMEM((spare, hid), BF16)],
        after,
    )


def give_kernel(own_slot, mirror_slot, main_ref, spare_ref, own_ref, mirror_ref):
    main = main_ref.shape[0]
    for slot_ref, out_ref in ((own_slot, own_ref), (mirror_slot, mirror_ref)):
        packed = dot(slot_ref[:, :main], main_ref[...]) + dot(slot_ref[:, main:], spare_ref[...])
        out_ref[...] = packed.astype(BF16)


def give(own_slot, mirror_slot, out_main, out_spare, tile):
    rows, width = own_slot.shape[0], out_main.shape[1]
    return call(
        give_kernel,
        width // tile,
        entire(own_slot, mirror_slot) + by_columns(tile, out_main, out_spare),
        by_columns(tile, bf16(rows, width), bf16(rows, width)),
        cost=GIVE_COST,
    )


def take_kernel(first, own_slot, mirror_slot, own_ref, mirror_ref, out_ref):
    rows = pl.ds(first, out_ref.shape[0])
    total = dot(own_slot[rows, :], own_ref[...]) + dot(mirror_slot[rows, :], mirror_ref[...])
    out_ref[...] = total.astype(BF16)


def take(own_slot, mirror_slot, own, mirror, first, count, tile, *after):
    return call(
        functools.partial(take_kernel, first),
        own.shape[1] // tile,
        entire(own_slot, mirror_slot) + by_columns(tile, own, mirror),
        by_columns(tile, bf16(count, own.shape[1]))[0],
        after=after,
    )


def mixed(mix_ref, rows_ref):
    both = dot(mix_ref[...], rows_ref[...])
    tok = both.shape[0] // 2
    return both[:tok] + both[tok:]


def part_kernel(mix_ref, rows_ref, part_ref):
    part_ref[...] = mixed(mix_ref, rows_ref).astype(BF16)


def total_kernel(mix_ref, rows_ref, other_ref, total_ref):
    total_ref[...] = (mixed(mix_ref, rows_ref) + other_ref[...].astype(F32)).astype(BF16)


def combine(mix, rows, others, tile, *after):
    width = rows.shape[1]
    return call(
        total_kernel if others else part_kernel,
        width // tile,
        entire(mix) + by_columns(tile, rows, *others),
        by_columns(tile, bf16(mix.shape[0] // 2, width))[0],
        after=after,
    )


def stack_grads(main_ref, spare_ref, grads_ref):
    main = main_ref.shape[0]
    grads_ref[:main] = main_ref[...]
    grads_ref[main:] = spare_ref[...]


def weight_kernel(turned, other_turned, main_ref, spare_ref, other_main, other_spare, out_ref, grads_ref):
    stack_grads(main_ref, spare_ref, grads_ref)
    total = dot(turned[...], grads_ref[...])
    stack_grads(other_main, other_spare, grads_ref)
    out_ref[...] = (total + dot(other_turned[...], grads_ref[...])).astype(BF16)


def weight_grad(turned, other_turned, grads, other_grads, tile, *after):
    half, slots = turned.shape
    width = grads[0].shape[1]
    return call(
        weight_kernel,
        width // tile,
        entire(turned, other_turned) + by_columns(tile, *grads, *other_grads),
        by_columns(tile, bf16(half, width))[0],
        [pltpu.VMEM((slots, tile), BF16)],
        after,
    )


def back_kernel(main_ref, grad_ref, near_ref, far_ref, back_ref, spare_ref, sum_ref, grads_ref):
    step = pl.program_id(0)
    half = near_ref.shape[0]
    main = main_ref.shape[0]

    @pl.when(step == 0)
    def _():
        sum_ref[...] = jnp.zeros_like(sum_ref)

    stack_grads(main_ref, grad_ref, grads_ref)
    sum_ref[:, :half] += dot(grads_ref[...], near_ref[...], 1, 1)
    sum_ref[:, half:] += dot(grads_ref[...], far_ref[...], 1, 1)

    @pl.when(step == pl.num_programs(0) - 1)
    def _():
        core = lax.axis_index("dp")
        for at, which in ((0, core), (half, 1 - core)):
            start = pl.multiple_of(which * half, LANES)
            total = sum_ref[:, at : at + half].astype(BF16)
            back_ref[:, pl.ds(start, half)] = total
            spare_ref[:, pl.ds(start, half)] = total[main:]


def project_back(grads_main, grads_spare, near, far, tile, *after):
    main, width = grads_main.shape
    spare = grads_spare.shape[0]
    half = near.shape[0]
    slots = main + spare
    return call(
        back_kernel,
        width // tile,
        by_columns(tile, grads_main, grads_spare, near, far),
        entire(bf16(slots, 2 * half), bf16(spare, 2 * half)),
        [pltpu.VMEM((slots, 2 * half), F32), pltpu.VMEM((slots, tile), BF16)],
        after,
        cost=BACK_COST,
    )


def place_kernel(back_ref, spare_ref, out_ref):
    out_ref[...] = spare_ref[...]


def with_spare(back, back_spare, *after):
    slots, hid = back.shape
    spare = back_spare.shape[0]
    last = pl.BlockSpec((spare, hid), lambda step: (slots // spare - 1, 0))
    ins = [(back, anywhere())] + entire(back_spare)
    return call(place_kernel, 1, ins, (bf16(slots, hid), last), (), after, {0: 0})


def local(hidden_saved, down_weight, route_device, replica_flag, gate_values, grad_out):
    count = lax.axis_size("expert")
    half = count // 2
    tok, top = route_device.shape
    width = grad_out.shape[1]
    cap = 5 * tok * top // (4 * count)
    main = 3 * tok * top // 4
    hidden = hidden_saved[0, 0]
    near = down_weight[0]
    slots = hidden.shape[0]
    tile = width // 4
    groups = [list(range(half)), list(range(half, count))]

    def to_half(rows):
        return lax.all_to_all(
            rows.reshape(half, cap, width), "expert", 0, 0, axis_index_groups=groups, tiled=True
        ).reshape(half * cap, width)

    far = swapped(near, "dp", 1)
    meta, spare_hidden = head(
        route_device.T, replica_flag.T, gate_values.T, hidden, slots - main, count
    )
    spare_hidden = swapped(spare_hidden, "expert", half)
    metas = lax.all_to_all(meta, "expert", 0, 0, tiled=True)
    packed_own, mix_own = pack_own(meta, grad_out, cap, half, tile)
    arrived_own = to_half(touched(packed_own, metas, spare_hidden, far))
    out_spare = project_spare(spare_hidden, near, far, tile, mix_own)
    sel, gate, mix_mirror, give_own, take_own, give_mirror, take_mirror = plan(
        metas, cap, half, main, slots
    )
    out_main, turned, far_turned = project(hidden, spare_hidden, near, far, tile, out_spare)
    out_spare = swapped(out_spare, "expert", half)
    mirror = swapped(touched(copied(grad_out, width // 2), out_main, sel), "expert", half)
    other_turned = swapped(far_turned, "dp", 1)
    given_own, given_mirror = give(give_own, give_mirror, out_main, out_spare, tile)
    returned_mirror = to_half(touched(given_mirror, arrived_own))
    packed_mirror = pack(sel, gate, mirror, tile, given_own)
    arrived_mirror = to_half(touched(packed_mirror, returned_mirror))
    part = swapped(combine(mix_mirror, returned_mirror, [], tile), "expert", half)
    arrived = (take_own, take_mirror, arrived_own, arrived_mirror)
    grads_spare = take(*arrived, main, slots - main, tile)
    returned_own = to_half(touched(given_own, part, grads_spare))
    grads_main = take(*arrived, 0, main, tile, grads_spare)
    other_main = swapped(grads_main, "dp", 1)
    grads_spare = swapped(grads_spare, "expert", half)
    other_spare = swapped(grads_spare, "dp", 1)
    layer_out = combine(mix_own, returned_own, [part], tile)
    back, back_spare = project_back(grads_main, grads_spare, near, far, tile)
    back_spare = swapped(back_spare, "expert", half)
    grad_weight = weight_grad(
        turned, other_turned, (grads_main, grads_spare), (other_main, other_spare), tile, back
    )
    grad_hidden = with_spare(back, back_spare, layer_out, grad_weight)
    return (layer_out, grad_hidden[None, None], grad_weight[None])


def solution(mesh):
    in_specs = (
        P("dp", "expert", None, None),
        P("expert", "dp", None),
        P(("dp", "expert"), None),
        P(("dp", "expert"), None),
        P(("dp", "expert"), None),
        P(("dp", "expert"), None),
    )
    out_specs = (P(("dp", "expert"), None), P("dp", "expert", None, None), P("expert", "dp", None))
    return jax.shard_map(local, mesh=mesh, in_specs=in_specs, out_specs=out_specs, check_vma=False)
```

```python
import functools
import jax
import jax.numpy as jnp
from jax import lax
from jax.experimental import pallas as pl
from jax.experimental.pallas import tpu as pltpu
from jax.sharding import PartitionSpec as P

F32, BF16, I32 = jnp.float32, jnp.bfloat16, jnp.int32
LANES = 128
LONG = 4_000_000_000_000
GIVE_COST = 40_000_000_000
BACK_COST = 40_000_000_000
VMEM_LIMIT = 60 * 1024 * 1024


def swapped(value, axis, distance):
    count = lax.axis_size(axis)
    pairs = [(source, (source + distance) % count) for source in range(count)]
    return lax.ppermute(value, axis, pairs)


def dot(left, right, left_dim=1, right_dim=0):
    contract = (((left_dim,), (right_dim,)), ((), ()))
    return lax.dot_general(left, right, contract, preferred_element_type=F32)


def iota(shape, dim):
    return lax.broadcasted_iota(I32, shape, dim).astype(F32)


def row_of(rows, cap, lanes):
    row = iota((rows, lanes), 0)
    group = jnp.floor((row + 0.5) * (1.0 / cap))
    return group, row - group * cap


def before_mask(size):
    return (iota((size, size), 0) < iota((size, size), 1)).astype(BF16)


def bf16(*shape):
    return jax.ShapeDtypeStruct(shape, BF16)


def f32(*shape):
    return jax.ShapeDtypeStruct(shape, F32)


def call(body, grid, ins, outs, scratch=(), after=(), alias=None, cost=0):
    single = not isinstance(outs, list)
    pairs = [outs] if single else outs
    specs = [spec for _, spec in pairs]
    shapes = [shape for shape, _ in pairs]
    count = len(ins)

    def kernel(*refs):
        body(*refs[:count], *refs[count + len(after) :])

    return pl.pallas_call(
        kernel,
        grid=(grid,),
        in_specs=[spec for _, spec in ins] + [anywhere()] * len(after),
        out_specs=specs[0] if single else specs,
        out_shape=shapes[0] if single else shapes,
        scratch_shapes=list(scratch),
        input_output_aliases=alias or {},
        compiler_params=pltpu.CompilerParams(vmem_limit_bytes=VMEM_LIMIT),
        cost_estimate=pl.CostEstimate(flops=cost, bytes_accessed=0, transcendentals=0),
    )(*[array for array, _ in ins], *after)


def anywhere():
    return pl.BlockSpec(memory_space=pl.ANY)


def whole(array):
    return pl.BlockSpec(array.shape, lambda step: (0,) * len(array.shape))


def columns(array, tile):
    return pl.BlockSpec((array.shape[0], tile), lambda step: (0, step))


def entire(*arrays):
    return [(array, whole(array)) for array in arrays]


def by_columns(tile, *arrays):
    return [(array, columns(array, tile)) for array in arrays]


def head_kernel(device_ref, flag_ref, gate_ref, hidden_ref, meta_ref, spare_ref):
    top = device_ref.shape[0]
    codes = (device_ref[...] * 2 + flag_ref[...]).astype(F32)
    count = meta_ref.shape[0]
    meta_ref[:, :top, :] = jnp.broadcast_to(codes[None], (count, *codes.shape))
    meta_ref[:, top:, :] = jnp.broadcast_to(gate_ref[...][None], (count, *codes.shape))
    spare_ref[...] = hidden_ref[...]


def head(devices, flags, gates, hidden, spare, count):
    top, tok = devices.shape
    slots, hid = hidden.shape
    last = pl.BlockSpec((spare, hid), lambda step: (slots // spare - 1, 0))
    outs = entire(f32(count, 2 * top, tok), bf16(spare, hid))
    return call(head_kernel, 1, entire(devices, flags, gates) + [(hidden, last)], outs)


def copy_kernel(source_ref, target_ref):
    target_ref[...] = source_ref[...]


def copied(array, tile, *after):
    ins, outs = by_columns(tile, array), by_columns(tile, bf16(*array.shape))[0]
    return call(copy_kernel, array.shape[1] // tile, ins, outs, (), after)


def touch_kernel(source_ref, target_ref):
    pass


def touched(array, *after):
    shape = jax.ShapeDtypeStruct(array.shape, array.dtype)
    return call(touch_kernel, 1, [(array, anywhere())], (shape, anywhere()), (), after, {0: 0})


def plan_rows(meta, cap, half, sel_ref, gate_ref, mix_ref):
    rows, tok = sel_ref.shape
    top = meta.shape[0] // 2
    me = lax.axis_index("expert")
    first = (lax.div(me, half) * half).astype(F32)
    dest = iota((LANES, tok), 0)
    inside = dest < half
    dest = dest + first
    hit = jnp.zeros((LANES, tok), F32)
    gate = jnp.zeros((LANES, tok), F32)
    for k in range(top):
        device = jnp.floor(meta[k : k + 1] * 0.5)
        named = (dest == device) & inside
        hit = jnp.where(named, 1.0, hit)
        gate = jnp.where(named, meta[top + k : top + k + 1], gate)
    place = dot(hit.astype(BF16), before_mask(tok))
    place = jnp.where(hit > 0.5, place, -1.0)
    group, at = row_of(rows, cap, LANES)
    spread = (iota((rows, LANES), 1) == group).astype(BF16)
    to_rows = lambda table: dot(spread, table.astype(BF16))
    chosen = jnp.where(to_rows(place) == at, 1.0, jnp.zeros((rows, tok), F32))
    high = gate.astype(BF16).astype(F32)
    mid = (gate - high).astype(BF16).astype(F32)
    low = gate - high - mid
    high, mid, low = to_rows(high), to_rows(mid), to_rows(low)
    scale = jnp.sum(chosen * (high + mid + low), axis=1, keepdims=True)
    sel_ref[...] = chosen.astype(BF16)
    gate_ref[...] = jnp.broadcast_to(scale, (rows, LANES))
    mix_ref[:tok] = (chosen * high).T.astype(BF16)
    mix_ref[tok:] = (chosen * mid).T.astype(BF16)


def packed_rows(sel_ref, gate_ref, tokens_ref, packed_ref):
    packed_ref[...] = (dot(sel_ref[...], tokens_ref[...]) * gate_ref[:, :1]).astype(BF16)


def pack_own_kernel(cap, half, meta_ref, tokens_ref, packed_ref, mix_ref, sel_ref, gate_ref):
    @pl.when(pl.program_id(0) == 0)
    def _():
        plan_rows(meta_ref[0], cap, half, sel_ref, gate_ref, mix_ref)

    packed_rows(sel_ref, gate_ref, tokens_ref, packed_ref)


def pack_own(meta, tokens, cap, half, tile, *after):
    tok, width = tokens.shape
    rows = half * cap
    first = pl.BlockSpec((1, *meta.shape[1:]), lambda step: (0, 0, 0))
    return call(
        functools.partial(pack_own_kernel, cap, half),
        width // tile,
        [(meta, first)] + by_columns(tile, tokens),
        by_columns(tile, bf16(rows, width)) + entire(bf16(2 * tok, rows)),
        [pltpu.VMEM((rows, tok), BF16), pltpu.VMEM((rows, LANES), F32)],
        after,
    )


def pack(sel, gate, tokens, tile, *after):
    rows, width = sel.shape[0], tokens.shape[1]
    return call(
        packed_rows,
        width // tile,
        entire(sel, gate) + by_columns(tile, tokens),
        by_columns(tile, bf16(rows, width))[0],
        after=after,
        cost=LONG,
    )


def plan_kernel(cap, half, main, metas_ref, sel_ref, gate_ref, mix_ref, *slot_refs):
    count, tops, tok = metas_ref.shape
    top = tops // 2
    rows, slots = slot_refs[0].shape
    spare = slots - main
    me = lax.axis_index("expert")
    mirror = lax.rem(me + half, count)
    plan_rows(metas_ref[mirror], cap, half, sel_ref, gate_ref, mix_ref)

    mine, other = me.astype(F32), mirror.astype(F32)
    none = jnp.zeros((count, tok), F32)
    here, flag, clash = none, none, none
    for k in range(top):
        code = metas_ref[:, k, :]
        device = jnp.floor(code * 0.5)
        here = jnp.where(device == mine, 1.0, here)
        flag = jnp.where(device == mine, code - 2.0 * device, flag)
        clash = jnp.where(device == other, 1.0, clash)
    at_spare = here * flag * (1.0 - clash)
    at_main = here - at_spare
    before = before_mask(tok)
    ones = jnp.ones((tok, LANES), BF16)
    lower = (iota((count, count), 1) < iota((count, count), 0)).astype(BF16)

    def rank(flags):
        flags = flags.astype(BF16)
        return dot(flags, before) + dot(lower, dot(flags, ones).astype(BF16))

    rank_main, rank_spare = rank(at_main), rank(at_spare)
    slot = jnp.where((at_main > 0.5) & (rank_main < main), rank_main + 1.0, none)
    slot = jnp.where((at_spare > 0.5) & (rank_spare < spare), rank_spare + (main + 1.0), slot)
    place = jnp.where(here > 0.5, dot(here.astype(BF16), before), -1.0).astype(BF16)
    tens = jnp.floor(slot * (1.0 / 32.0))
    units = (slot - tens * 32.0).astype(BF16)
    tens = tens.astype(BF16)
    group, _ = row_of(rows, cap, count)
    _, at = row_of(rows, cap, tok)
    start = lax.div(me, half) * half
    for side, base in enumerate((start, lax.rem(start + half, count))):
        spread = (iota((rows, count), 1) == group + base.astype(F32)).astype(BF16)
        chosen = dot(spread, place) == at
        number = dot(spread, tens) * 32.0 + dot(spread, units)
        number = jnp.sum(jnp.where(chosen, number, 0.0), axis=1, keepdims=True)
        give_ref, take_ref = slot_refs[2 * side : 2 * side + 2]
        give_ref[...] = (iota((rows, slots), 1) + 1.0 == number).astype(BF16)
        number = jnp.broadcast_to(number, (rows, LANES)).T[0:1]
        take_ref[...] = (iota((slots, rows), 0) + 1.0 == number).astype(BF16)


def plan(metas, cap, half, main, slots):
    tok = metas.shape[2]
    rows = half * cap
    sides = [bf16(rows, slots), bf16(slots, rows)] * 2
    outs = entire(bf16(rows, tok), f32(rows, LANES), bf16(2 * tok, rows), *sides)
    return call(functools.partial(plan_kernel, cap, half, main), 1, entire(metas), outs)


def side_by_side(source, target_ref):
    half = target_ref.shape[1] // 2
    core = lax.axis_index("dp")
    for at, which in ((0, core), (half, 1 - core)):
        start = pl.multiple_of(which * half, LANES)
        target_ref[:, at : at + half] = source[: target_ref.shape[0], pl.ds(start, half)]


def projected(stack_ref, near_ref, far_ref, out_ref):
    half = near_ref.shape[0]
    total = dot(stack_ref[:, :half], near_ref[...]) + dot(stack_ref[:, half:], far_ref[...])
    out_ref[...] = total.astype(BF16)


def project_spare_kernel(spare_ref, near_ref, far_ref, out_ref, stack_ref):
    @pl.when(pl.program_id(0) == 0)
    def _():
        side_by_side(spare_ref, stack_ref)

    projected(stack_ref, near_ref, far_ref, out_ref)


def project_spare(spare_hidden, near, far, tile, *after):
    width = near.shape[1]
    return call(
        project_spare_kernel,
        width // tile,
        entire(spare_hidden) + by_columns(tile, near, far),
        by_columns(tile, bf16(spare_hidden.shape[0], width))[0],
        [pltpu.VMEM(spare_hidden.shape, BF16)],
        after,
    )


def project_kernel(hidden_ref, spare_ref, near_ref, far_ref, out_ref, near_turned, far_turned, stack_ref, side_ref):
    main, half = out_ref.shape[0], near_ref.shape[0]

    @pl.when(pl.program_id(0) == 0)
    def _():
        side_by_side(hidden_ref, stack_ref)
        side_by_side(spare_ref, side_ref)
        for at, turned_ref in ((0, near_turned), (half, far_turned)):
            turned_ref[:, :main] = stack_ref[:, at : at + half].T
            turned_ref[:, main:] = side_ref[:, at : at + half].T

    projected(stack_ref, near_ref, far_ref, out_ref)


def project(hidden, spare_hidden, near, far, tile, *after):
    half, width = near.shape
    spare = spare_hidden.shape[0]
    slots, hid = hidden.shape
    turned = [bf16(half, slots), bf16(half, slots)]
    return call(
        project_kernel,
        width // tile,
        entire(hidden, spare_hidden) + by_columns(tile, near, far),
        by_columns(tile, bf16(slots - spare, width)) + entire(*turned),
        [pltpu.VMEM((slots - spare, hid), BF16), pltpu.VMEM((spare, hid), BF16)],
        after,
    )


def give_kernel(slot_ref, main_ref, spare_ref, out_ref):
    main = main_ref.shape[0]
    packed = dot(slot_ref[:, :main], main_ref[...]) + dot(slot_ref[:, main:], spare_ref[...])
    out_ref[...] = packed.astype(BF16)


def give(slot, out_main, out_spare, tile, cost, *after):
    rows, width = slot.shape[0], out_main.shape[1]
    return call(
        give_kernel,
        width // tile,
        entire(slot) + by_columns(tile, out_main, out_spare),
        by_columns(tile, bf16(rows, width))[0],
        after=after,
        cost=cost,
    )


def take_kernel(first, own_slot, mirror_slot, own_ref, mirror_ref, out_ref):
    rows = pl.ds(first, out_ref.shape[0])
    total = dot(own_slot[rows, :], own_ref[...]) + dot(mirror_slot[rows, :], mirror_ref[...])
    out_ref[...] = total.astype(BF16)


def take(own_slot, mirror_slot, own, mirror, first, count, tile, *after):
    return call(
        functools.partial(take_kernel, first),
        own.shape[1] // tile,
        entire(own_slot, mirror_slot) + by_columns(tile, own, mirror),
        by_columns(tile, bf16(count, own.shape[1]))[0],
        after=after,
    )


def mixed(mix_ref, rows_ref):
    both = dot(mix_ref[...], rows_ref[...])
    tok = both.shape[0] // 2
    return both[:tok] + both[tok:]


def part_kernel(mix_ref, rows_ref, part_ref):
    part_ref[...] = mixed(mix_ref, rows_ref).astype(BF16)


def total_kernel(mix_ref, rows_ref, other_ref, total_ref):
    total_ref[...] = (mixed(mix_ref, rows_ref) + other_ref[...].astype(F32)).astype(BF16)


def combine(mix, rows, others, tile, *after):
    width = rows.shape[1]
    return call(
        total_kernel if others else part_kernel,
        width // tile,
        entire(mix) + by_columns(tile, rows, *others),
        by_columns(tile, bf16(mix.shape[0] // 2, width))[0],
        after=after,
    )


def stack_grads(main_ref, spare_ref, grads_ref):
    main = main_ref.shape[0]
    grads_ref[:main] = main_ref[...]
    grads_ref[main:] = spare_ref[...]


def weight_kernel(turned, other_turned, main_ref, spare_ref, other_main, other_spare, out_ref, grads_ref):
    stack_grads(main_ref, spare_ref, grads_ref)
    total = dot(turned[...], grads_ref[...])
    stack_grads(other_main, other_spare, grads_ref)
    out_ref[...] = (total + dot(other_turned[...], grads_ref[...])).astype(BF16)


def weight_grad(turned, other_turned, grads, other_grads, tile, *after):
    half, slots = turned.shape
    width = grads[0].shape[1]
    return call(
        weight_kernel,
        width // tile,
        entire(turned, other_turned) + by_columns(tile, *grads, *other_grads),
        by_columns(tile, bf16(half, width))[0],
        [pltpu.VMEM((slots, tile), BF16)],
        after,
    )


def back_kernel(main_ref, grad_ref, near_ref, far_ref, back_ref, spare_ref, sum_ref, grads_ref):
    step = pl.program_id(0)
    half = near_ref.shape[0]
    main = main_ref.shape[0]

    @pl.when(step == 0)
    def _():
        sum_ref[...] = jnp.zeros_like(sum_ref)

    stack_grads(main_ref, grad_ref, grads_ref)
    sum_ref[:, :half] += dot(grads_ref[...], near_ref[...], 1, 1)
    sum_ref[:, half:] += dot(grads_ref[...], far_ref[...], 1, 1)

    @pl.when(step == pl.num_programs(0) - 1)
    def _():
        core = lax.axis_index("dp")
        for at, which in ((0, core), (half, 1 - core)):
            start = pl.multiple_of(which * half, LANES)
            total = sum_ref[:, at : at + half].astype(BF16)
            back_ref[:, pl.ds(start, half)] = total
            spare_ref[:, pl.ds(start, half)] = total[main:]


def project_back(grads_main, grads_spare, near, far, tile, *after):
    main, width = grads_main.shape
    spare = grads_spare.shape[0]
    half = near.shape[0]
    slots = main + spare
    return call(
        back_kernel,
        width // tile,
        by_columns(tile, grads_main, grads_spare, near, far),
        entire(bf16(slots, 2 * half), bf16(spare, 2 * half)),
        [pltpu.VMEM((slots, 2 * half), F32), pltpu.VMEM((slots, tile), BF16)],
        after,
        cost=BACK_COST,
    )


def place_kernel(back_ref, spare_ref, out_ref):
    out_ref[...] = spare_ref[...]


def with_spare(back, back_spare, *after):
    slots, hid = back.shape
    spare = back_spare.shape[0]
    last = pl.BlockSpec((spare, hid), lambda step: (slots // spare - 1, 0))
    ins = [(back, anywhere())] + entire(back_spare)
    return call(place_kernel, 1, ins, (bf16(slots, hid), last), (), after, {0: 0})


def local(hidden_saved, down_weight, route_device, replica_flag, gate_values, grad_out):
    count = lax.axis_size("expert")
    half = count // 2
    tok, top = route_device.shape
    width = grad_out.shape[1]
    cap = 5 * tok * top // (4 * count)
    main = 3 * tok * top // 4
    hidden = hidden_saved[0, 0]
    near = down_weight[0]
    slots = hidden.shape[0]
    tile = width // 4
    groups = [list(range(half)), list(range(half, count))]

    def to_half(rows):
        return lax.all_to_all(
            rows.reshape(half, cap, width), "expert", 0, 0, axis_index_groups=groups, tiled=True
        ).reshape(half * cap, width)

    far = swapped(near, "dp", 1)
    meta, spare_hidden = head(
        route_device.T, replica_flag.T, gate_values.T, hidden, slots - main, count
    )
    spare_hidden = swapped(spare_hidden, "expert", half)
    metas = lax.all_to_all(meta, "expert", 0, 0, tiled=True)
    packed_own, mix_own = pack_own(meta, grad_out, cap, half, tile)
    out_spare = project_spare(spare_hidden, near, far, width // 7, mix_own, metas)
    arrived_own = to_half(touched(packed_own, metas, out_spare))
    sel, gate, mix_mirror, give_own, take_own, give_mirror, take_mirror = plan(
        metas, cap, half, main, slots
    )
    out_main, turned, far_turned = project(hidden, spare_hidden, near, far, tile, out_spare)
    out_spare = swapped(out_spare, "expert", half)
    mirror = swapped(touched(copied(grad_out, width // 2), out_main, sel), "expert", half)
    other_turned = swapped(far_turned, "dp", 1)
    given_mirror = give(give_mirror, out_main, out_spare, tile, GIVE_COST)
    given_own = give(give_own, out_main, out_spare, tile, 0, given_mirror)
    returned_mirror = to_half(touched(given_mirror, arrived_own))
    packed_mirror = pack(sel, gate, mirror, tile, given_own)
    arrived_mirror = to_half(touched(packed_mirror, returned_mirror))
    part = swapped(combine(mix_mirror, returned_mirror, [], tile), "expert", half)
    arrived = (take_own, take_mirror, arrived_own, arrived_mirror)
    grads_spare = take(*arrived, main, slots - main, tile)
    returned_own = to_half(touched(given_own, part, grads_spare))
    grads_main = take(*arrived, 0, main, tile, grads_spare)
    other_main = swapped(grads_main, "dp", 1)
    grads_spare = swapped(grads_spare, "expert", half)
    other_spare = swapped(grads_spare, "dp", 1)
    layer_out = combine(mix_own, returned_own, [part], tile)
    back, back_spare = project_back(grads_main, grads_spare, near, far, tile)
    back_spare = swapped(back_spare, "expert", half)
    grad_weight = weight_grad(
        turned, other_turned, (grads_main, grads_spare), (other_main, other_spare), tile, back
    )
    grad_hidden = with_spare(back, back_spare, grad_weight)
    return (layer_out, grad_hidden[None, None], grad_weight[None])


def solution(mesh):
    in_specs = (
        P("dp", "expert", None, None),
        P("expert", "dp", None),
        P(("dp", "expert"), None),
        P(("dp", "expert"), None),
        P(("dp", "expert"), None),
        P(("dp", "expert"), None),
    )
    out_specs = (P(("dp", "expert"), None), P("dp", "expert", None, None), P("expert", "dp", None))
    return jax.shard_map(local, mesh=mesh, in_specs=in_specs, out_specs=out_specs, check_vma=False)
```

```python
import functools
import jax
import jax.numpy as jnp
from jax import lax
from jax.experimental import pallas as pl
from jax.experimental.pallas import tpu as pltpu
from jax.sharding import PartitionSpec as P

F32, BF16, I32 = jnp.float32, jnp.bfloat16, jnp.int32
LANES = 128
LONG = 4_000_000_000_000
GIVE_COST = 5_000_000_000
BACK_COST = 40_000_000_000
VMEM_LIMIT = 64 * 1024 * 1024 - 65536


def swapped(value, axis, distance):
    count = lax.axis_size(axis)
    pairs = [(source, (source + distance) % count) for source in range(count)]
    return lax.ppermute(value, axis, pairs)


def dot(left, right, left_dim=1, right_dim=0):
    contract = (((left_dim,), (right_dim,)), ((), ()))
    return lax.dot_general(left, right, contract, preferred_element_type=F32)


def iota(shape, dim):
    return lax.broadcasted_iota(I32, shape, dim).astype(F32)


def row_of(rows, cap, lanes):
    row = iota((rows, lanes), 0)
    group = jnp.floor((row + 0.5) * (1.0 / cap))
    return group, row - group * cap


def before_mask(size):
    return (iota((size, size), 0) < iota((size, size), 1)).astype(BF16)


def bf16(*shape):
    return jax.ShapeDtypeStruct(shape, BF16)


def f32(*shape):
    return jax.ShapeDtypeStruct(shape, F32)


def call(body, grid, ins, outs, scratch=(), after=(), alias=None, cost=0):
    single = not isinstance(outs, list)
    pairs = [outs] if single else outs
    specs = [spec for _, spec in pairs]
    shapes = [shape for shape, _ in pairs]
    count = len(ins)

    def kernel(*refs):
        body(*refs[:count], *refs[count + len(after) :])

    return pl.pallas_call(
        kernel,
        grid=(grid,),
        in_specs=[spec for _, spec in ins] + [anywhere()] * len(after),
        out_specs=specs[0] if single else specs,
        out_shape=shapes[0] if single else shapes,
        scratch_shapes=list(scratch),
        input_output_aliases=alias or {},
        compiler_params=pltpu.CompilerParams(vmem_limit_bytes=VMEM_LIMIT),
        cost_estimate=pl.CostEstimate(flops=cost, bytes_accessed=0, transcendentals=0),
    )(*[array for array, _ in ins], *after)


def anywhere():
    return pl.BlockSpec(memory_space=pl.ANY)


def whole(array):
    return pl.BlockSpec(array.shape, lambda step: (0,) * len(array.shape))


def columns(array, tile):
    return pl.BlockSpec((array.shape[0], tile), lambda step: (0, step))


def entire(*arrays):
    return [(array, whole(array)) for array in arrays]


def by_columns(tile, *arrays):
    return [(array, columns(array, tile)) for array in arrays]


def head_kernel(device_ref, flag_ref, gate_ref, hidden_ref, meta_ref, spare_ref):
    top = device_ref.shape[0]
    codes = (device_ref[...] * 2 + flag_ref[...]).astype(F32)
    count = meta_ref.shape[0]
    meta_ref[:, :top, :] = jnp.broadcast_to(codes[None], (count, *codes.shape))
    meta_ref[:, top:, :] = jnp.broadcast_to(gate_ref[...][None], (count, *codes.shape))
    spare_ref[...] = hidden_ref[...]


def head(devices, flags, gates, hidden, spare, count):
    top, tok = devices.shape
    slots, hid = hidden.shape
    last = pl.BlockSpec((spare, hid), lambda step: (slots // spare - 1, 0))
    outs = entire(f32(count, 2 * top, tok), bf16(spare, hid))
    return call(head_kernel, 1, entire(devices, flags, gates) + [(hidden, last)], outs)


def copy_kernel(source_ref, target_ref):
    target_ref[...] = source_ref[...]


def copied(array, tile, *after):
    ins, outs = by_columns(tile, array), by_columns(tile, bf16(*array.shape))[0]
    return call(copy_kernel, array.shape[1] // tile, ins, outs, (), after)


def touch_kernel(source_ref, target_ref):
    pass


def touched(array, *after):
    shape = jax.ShapeDtypeStruct(array.shape, array.dtype)
    return call(touch_kernel, 1, [(array, anywhere())], (shape, anywhere()), (), after, {0: 0})


def plan_rows(meta, cap, half, sel_ref, gate_ref, mix_ref):
    rows, tok = sel_ref.shape
    top = meta.shape[0] // 2
    me = lax.axis_index("expert")
    first = (lax.div(me, half) * half).astype(F32)
    dest = iota((LANES, tok), 0)
    inside = dest < half
    dest = dest + first
    hit = jnp.zeros((LANES, tok), F32)
    gate = jnp.zeros((LANES, tok), F32)
    for k in range(top):
        device = jnp.floor(meta[k : k + 1] * 0.5)
        named = (dest == device) & inside
        hit = jnp.where(named, 1.0, hit)
        gate = jnp.where(named, meta[top + k : top + k + 1], gate)
    place = dot(hit.astype(BF16), before_mask(tok))
    place = jnp.where(hit > 0.5, place, -1.0)
    group, at = row_of(rows, cap, LANES)
    spread = (iota((rows, LANES), 1) == group).astype(BF16)
    to_rows = lambda table: dot(spread, table.astype(BF16))
    chosen = jnp.where(to_rows(place) == at, 1.0, jnp.zeros((rows, tok), F32))
    high = gate.astype(BF16).astype(F32)
    mid = (gate - high).astype(BF16).astype(F32)
    low = gate - high - mid
    high, mid, low = to_rows(high), to_rows(mid), to_rows(low)
    scale = jnp.sum(chosen * (high + mid + low), axis=1, keepdims=True)
    sel_ref[...] = chosen.astype(BF16)
    gate_ref[...] = jnp.broadcast_to(scale, (rows, LANES))
    mix_ref[:tok] = (chosen * high).T.astype(BF16)
    mix_ref[tok:] = (chosen * mid).T.astype(BF16)


def packed_rows(sel_ref, gate_ref, tokens_ref, packed_ref):
    packed_ref[...] = (dot(sel_ref[...], tokens_ref[...]) * gate_ref[:, :1]).astype(BF16)


def pack_own_kernel(cap, half, meta_ref, tokens_ref, packed_ref, mix_ref, sel_ref, gate_ref):
    @pl.when(pl.program_id(0) == 0)
    def _():
        plan_rows(meta_ref[0], cap, half, sel_ref, gate_ref, mix_ref)

    packed_rows(sel_ref, gate_ref, tokens_ref, packed_ref)


def pack_own(meta, tokens, cap, half, tile, *after):
    tok, width = tokens.shape
    rows = half * cap
    first = pl.BlockSpec((1, *meta.shape[1:]), lambda step: (0, 0, 0))
    return call(
        functools.partial(pack_own_kernel, cap, half),
        width // tile,
        [(meta, first)] + by_columns(tile, tokens),
        by_columns(tile, bf16(rows, width)) + entire(bf16(2 * tok, rows)),
        [pltpu.VMEM((rows, tok), BF16), pltpu.VMEM((rows, LANES), F32)],
        after,
    )


def pack(sel, gate, tokens, tile, *after):
    rows, width = sel.shape[0], tokens.shape[1]
    return call(
        packed_rows,
        width // tile,
        entire(sel, gate) + by_columns(tile, tokens),
        by_columns(tile, bf16(rows, width))[0],
        after=after,
        cost=LONG,
    )


def plan_kernel(cap, half, main, metas_ref, sel_ref, gate_ref, mix_ref, *slot_refs):
    count, tops, tok = metas_ref.shape
    top = tops // 2
    rows, slots = slot_refs[0].shape
    spare = slots - main
    me = lax.axis_index("expert")
    mirror = lax.rem(me + half, count)
    plan_rows(metas_ref[mirror], cap, half, sel_ref, gate_ref, mix_ref)

    mine, other = me.astype(F32), mirror.astype(F32)
    none = jnp.zeros((count, tok), F32)
    here, flag, clash = none, none, none
    for k in range(top):
        code = metas_ref[:, k, :]
        device = jnp.floor(code * 0.5)
        here = jnp.where(device == mine, 1.0, here)
        flag = jnp.where(device == mine, code - 2.0 * device, flag)
        clash = jnp.where(device == other, 1.0, clash)
    at_spare = here * flag * (1.0 - clash)
    at_main = here - at_spare
    before = before_mask(tok)
    ones = jnp.ones((tok, LANES), BF16)
    lower = (iota((count, count), 1) < iota((count, count), 0)).astype(BF16)

    def rank(flags):
        flags = flags.astype(BF16)
        return dot(flags, before) + dot(lower, dot(flags, ones).astype(BF16))

    rank_main, rank_spare = rank(at_main), rank(at_spare)
    slot = jnp.where((at_main > 0.5) & (rank_main < main), rank_main + 1.0, none)
    slot = jnp.where((at_spare > 0.5) & (rank_spare < spare), rank_spare + (main + 1.0), slot)
    place = jnp.where(here > 0.5, dot(here.astype(BF16), before), -1.0).astype(BF16)
    tens = jnp.floor(slot * (1.0 / 32.0))
    units = (slot - tens * 32.0).astype(BF16)
    tens = tens.astype(BF16)
    group, _ = row_of(rows, cap, count)
    _, at = row_of(rows, cap, tok)
    start = lax.div(me, half) * half
    for side, base in enumerate((start, lax.rem(start + half, count))):
        spread = (iota((rows, count), 1) == group + base.astype(F32)).astype(BF16)
        chosen = dot(spread, place) == at
        number = dot(spread, tens) * 32.0 + dot(spread, units)
        number = jnp.sum(jnp.where(chosen, number, 0.0), axis=1, keepdims=True)
        give_ref, take_ref = slot_refs[2 * side : 2 * side + 2]
        give_ref[...] = (iota((rows, slots), 1) + 1.0 == number).astype(BF16)
        number = jnp.broadcast_to(number, (rows, LANES)).T[0:1]
        take_ref[...] = (iota((slots, rows), 0) + 1.0 == number).astype(BF16)


def plan(metas, cap, half, main, slots):
    tok = metas.shape[2]
    rows = half * cap
    sides = [bf16(rows, slots), bf16(slots, rows)] * 2
    outs = entire(bf16(rows, tok), f32(rows, LANES), bf16(2 * tok, rows), *sides)
    return call(functools.partial(plan_kernel, cap, half, main), 1, entire(metas), outs)


def side_by_side(source, target_ref):
    half = target_ref.shape[1] // 2
    core = lax.axis_index("dp")
    for at, which in ((0, core), (half, 1 - core)):
        start = pl.multiple_of(which * half, LANES)
        target_ref[:, at : at + half] = source[: target_ref.shape[0], pl.ds(start, half)]


def projected(stack_ref, near_ref, far_ref, out_ref):
    half = near_ref.shape[0]
    total = dot(stack_ref[:, :half], near_ref[...]) + dot(stack_ref[:, half:], far_ref[...])
    out_ref[...] = total.astype(BF16)


def project_spare_kernel(spare_ref, near_ref, far_ref, out_ref, stack_ref):
    @pl.when(pl.program_id(0) == 0)
    def _():
        side_by_side(spare_ref, stack_ref)

    projected(stack_ref, near_ref, far_ref, out_ref)


def project_spare(spare_hidden, near, far, tile, *after):
    width = near.shape[1]
    return call(
        project_spare_kernel,
        width // tile,
        entire(spare_hidden) + by_columns(tile, near, far),
        by_columns(tile, bf16(spare_hidden.shape[0], width))[0],
        [pltpu.VMEM(spare_hidden.shape, BF16)],
        after,
    )


def project_kernel(hidden_ref, spare_ref, near_ref, far_ref, out_ref, near_turned, far_turned, stack_ref, side_ref):
    main, half = out_ref.shape[0], near_ref.shape[0]

    @pl.when(pl.program_id(0) == 0)
    def _():
        side_by_side(hidden_ref, stack_ref)
        side_by_side(spare_ref, side_ref)
        for at, turned_ref in ((0, near_turned), (half, far_turned)):
            turned_ref[:, :main] = stack_ref[:, at : at + half].T
            turned_ref[:, main:] = side_ref[:, at : at + half].T

    projected(stack_ref, near_ref, far_ref, out_ref)


def project(hidden, spare_hidden, near, far, tile, *after):
    half, width = near.shape
    spare = spare_hidden.shape[0]
    slots, hid = hidden.shape
    turned = [bf16(half, slots), bf16(half, slots)]
    return call(
        project_kernel,
        width // tile,
        entire(hidden, spare_hidden) + by_columns(tile, near, far),
        by_columns(tile, bf16(slots - spare, width)) + entire(*turned),
        [pltpu.VMEM((slots - spare, hid), BF16), pltpu.VMEM((spare, hid), BF16)],
        after,
    )


def give_kernel(slot_ref, main_ref, spare_ref, out_ref):
    main = main_ref.shape[0]
    packed = dot(slot_ref[:, :main], main_ref[...]) + dot(slot_ref[:, main:], spare_ref[...])
    out_ref[...] = packed.astype(BF16)


def give(slot, out_main, out_spare, tile, cost, *after):
    rows, width = slot.shape[0], out_main.shape[1]
    return call(
        give_kernel,
        width // tile,
        entire(slot) + by_columns(tile, out_main, out_spare),
        by_columns(tile, bf16(rows, width))[0],
        after=after,
        cost=cost,
    )


def take_kernel(first, own_slot, mirror_slot, own_ref, mirror_ref, out_ref):
    rows = pl.ds(first, out_ref.shape[0])
    total = dot(own_slot[rows, :], own_ref[...]) + dot(mirror_slot[rows, :], mirror_ref[...])
    out_ref[...] = total.astype(BF16)


def take(own_slot, mirror_slot, own, mirror, first, count, tile, *after):
    return call(
        functools.partial(take_kernel, first),
        own.shape[1] // tile,
        entire(own_slot, mirror_slot) + by_columns(tile, own, mirror),
        by_columns(tile, bf16(count, own.shape[1]))[0],
        after=after,
    )


def mixed(mix_ref, rows_ref):
    both = dot(mix_ref[...], rows_ref[...])
    tok = both.shape[0] // 2
    return both[:tok] + both[tok:]


def part_kernel(mix_ref, rows_ref, part_ref):
    part_ref[...] = mixed(mix_ref, rows_ref).astype(BF16)


def total_kernel(mix_ref, rows_ref, other_ref, total_ref):
    total_ref[...] = (mixed(mix_ref, rows_ref) + other_ref[...].astype(F32)).astype(BF16)


def combine(mix, rows, others, tile, *after):
    width = rows.shape[1]
    return call(
        total_kernel if others else part_kernel,
        width // tile,
        entire(mix) + by_columns(tile, rows, *others),
        by_columns(tile, bf16(mix.shape[0] // 2, width))[0],
        after=after,
    )


def stack_grads(main_ref, spare_ref, grads_ref):
    main = main_ref.shape[0]
    grads_ref[:main] = main_ref[...]
    grads_ref[main:] = spare_ref[...]


def weight_kernel(turned, other_turned, main_ref, spare_ref, other_main, other_spare, out_ref, grads_ref):
    stack_grads(main_ref, spare_ref, grads_ref)
    total = dot(turned[...], grads_ref[...])
    stack_grads(other_main, other_spare, grads_ref)
    out_ref[...] = (total + dot(other_turned[...], grads_ref[...])).astype(BF16)


def weight_grad(turned, other_turned, grads, other_grads, tile, *after):
    half, slots = turned.shape
    width = grads[0].shape[1]
    return call(
        weight_kernel,
        width // tile,
        entire(turned, other_turned) + by_columns(tile, *grads, *other_grads),
        by_columns(tile, bf16(half, width))[0],
        [pltpu.VMEM((slots, tile), BF16)],
        after,
    )


def back_kernel(main_ref, grad_ref, near_ref, far_ref, back_ref, spare_ref, sum_ref, grads_ref):
    step = pl.program_id(0)
    half = near_ref.shape[0]
    main = main_ref.shape[0]

    @pl.when(step == 0)
    def _():
        sum_ref[...] = jnp.zeros_like(sum_ref)

    stack_grads(main_ref, grad_ref, grads_ref)
    sum_ref[:, :half] += dot(grads_ref[...], near_ref[...], 1, 1)
    sum_ref[:, half:] += dot(grads_ref[...], far_ref[...], 1, 1)

    @pl.when(step == pl.num_programs(0) - 1)
    def _():
        core = lax.axis_index("dp")
        for at, which in ((0, core), (half, 1 - core)):
            start = pl.multiple_of(which * half, LANES)
            total = sum_ref[:, at : at + half].astype(BF16)
            back_ref[:, pl.ds(start, half)] = total
            spare_ref[:, pl.ds(start, half)] = total[main:]


def project_back(grads_main, grads_spare, near, far, tile, *after):
    main, width = grads_main.shape
    spare = grads_spare.shape[0]
    half = near.shape[0]
    slots = main + spare
    return call(
        back_kernel,
        width // tile,
        by_columns(tile, grads_main, grads_spare, near, far),
        entire(bf16(slots, 2 * half), bf16(spare, 2 * half)),
        [pltpu.VMEM((slots, 2 * half), F32), pltpu.VMEM((slots, tile), BF16)],
        after,
        cost=BACK_COST,
    )


def place_kernel(back_ref, spare_ref, out_ref):
    out_ref[...] = spare_ref[...]


def with_spare(back, back_spare, *after):
    slots, hid = back.shape
    spare = back_spare.shape[0]
    last = pl.BlockSpec((spare, hid), lambda step: (slots // spare - 1, 0))
    ins = [(back, anywhere())] + entire(back_spare)
    return call(place_kernel, 1, ins, (bf16(slots, hid), last), (), after, {0: 0})


def local(hidden_saved, down_weight, route_device, replica_flag, gate_values, grad_out):
    count = lax.axis_size("expert")
    half = count // 2
    tok, top = route_device.shape
    width = grad_out.shape[1]
    cap = 5 * tok * top // (4 * count)
    main = 3 * tok * top // 4
    hidden = hidden_saved[0, 0]
    near = down_weight[0]
    slots = hidden.shape[0]
    tile = width // 4
    groups = [list(range(half)), list(range(half, count))]

    def to_half(rows):
        return lax.all_to_all(
            rows.reshape(half, cap, width), "expert", 0, 0, axis_index_groups=groups, tiled=True
        ).reshape(half * cap, width)

    far = swapped(near, "dp", 1)
    meta, spare_hidden = head(
        route_device.T, replica_flag.T, gate_values.T, hidden, slots - main, count
    )
    spare_hidden = swapped(spare_hidden, "expert", half)
    metas = lax.all_to_all(meta, "expert", 0, 0, tiled=True)
    packed_own, mix_own = pack_own(meta, grad_out, cap, half, tile)
    arrived_own = to_half(touched(packed_own, metas, spare_hidden, far))
    out_spare = project_spare(spare_hidden, near, far, tile, mix_own)
    sel, gate, mix_mirror, give_own, take_own, give_mirror, take_mirror = plan(
        metas, cap, half, main, slots
    )
    out_main, turned, far_turned = project(hidden, spare_hidden, near, far, tile, out_spare)
    out_spare = swapped(out_spare, "expert", half)
    mirror = swapped(touched(copied(grad_out, width // 2), out_main, sel), "expert", half)
    other_turned = swapped(far_turned, "dp", 1)
    given_mirror = give(give_mirror, out_main, out_spare, tile, GIVE_COST)
    returned_mirror = to_half(touched(given_mirror, arrived_own))
    packed_mirror = pack(sel, gate, mirror, tile)
    given_own = give(give_own, out_main, out_spare, tile, 0, packed_mirror)
    arrived_mirror = to_half(touched(packed_mirror, returned_mirror, given_own))
    part = swapped(combine(mix_mirror, returned_mirror, [], tile), "expert", half)
    arrived = (take_own, take_mirror, arrived_own, arrived_mirror)
    grads_spare = take(*arrived, main, slots - main, tile)
    returned_own = to_half(touched(given_own, part, grads_spare))
    grads_main = take(*arrived, 0, main, tile, grads_spare)
    other_main = swapped(grads_main, "dp", 1)
    grads_spare = swapped(grads_spare, "expert", half)
    other_spare = swapped(grads_spare, "dp", 1)
    layer_out = combine(mix_own, returned_own, [part], tile)
    back, back_spare = project_back(grads_main, grads_spare, near, far, tile)
    back_spare = swapped(back_spare, "expert", half)
    grad_weight = weight_grad(
        turned, other_turned, (grads_main, grads_spare), (other_main, other_spare), tile, back
    )
    grad_hidden = with_spare(back, back_spare, grad_weight)
    return (layer_out, grad_hidden[None, None], grad_weight[None])


def solution(mesh):
    in_specs = (
        P("dp", "expert", None, None),
        P("expert", "dp", None),
        P(("dp", "expert"), None),
        P(("dp", "expert"), None),
        P(("dp", "expert"), None),
        P(("dp", "expert"), None),
    )
    out_specs = (P(("dp", "expert"), None), P("dp", "expert", None, None), P("expert", "dp", None))
    return jax.shard_map(local, mesh=mesh, in_specs=in_specs, out_specs=out_specs, check_vma=False)
```

```python
import functools
import jax
import jax.numpy as jnp
from jax import lax
from jax.experimental import pallas as pl
from jax.experimental.pallas import tpu as pltpu
from jax.sharding import PartitionSpec as P

F32, BF16, I32 = jnp.float32, jnp.bfloat16, jnp.int32
LANES = 128
LONG = 4_000_000_000_000
GIVE_COST = 5_000_000_000
BACK_COST = 40_000_000_000
HEAD_COST = 5_000_000_000
VMEM_LIMIT = 64 * 1024 * 1024 - 65536


def swapped(value, axis, distance):
    count = lax.axis_size(axis)
    pairs = [(source, (source + distance) % count) for source in range(count)]
    return lax.ppermute(value, axis, pairs)


def dot(left, right, left_dim=1, right_dim=0):
    contract = (((left_dim,), (right_dim,)), ((), ()))
    return lax.dot_general(left, right, contract, preferred_element_type=F32)


def iota(shape, dim):
    return lax.broadcasted_iota(I32, shape, dim).astype(F32)


def row_of(rows, cap, lanes):
    row = iota((rows, lanes), 0)
    group = jnp.floor((row + 0.5) * (1.0 / cap))
    return group, row - group * cap


def before_mask(size):
    return (iota((size, size), 0) < iota((size, size), 1)).astype(BF16)


def bf16(*shape):
    return jax.ShapeDtypeStruct(shape, BF16)


def f32(*shape):
    return jax.ShapeDtypeStruct(shape, F32)


def call(body, grid, ins, outs, scratch=(), after=(), alias=None, cost=0):
    single = not isinstance(outs, list)
    pairs = [outs] if single else outs
    specs = [spec for _, spec in pairs]
    shapes = [shape for shape, _ in pairs]
    count = len(ins)

    def kernel(*refs):
        body(*refs[:count], *refs[count + len(after) :])

    return pl.pallas_call(
        kernel,
        grid=(grid,),
        in_specs=[spec for _, spec in ins] + [anywhere()] * len(after),
        out_specs=specs[0] if single else specs,
        out_shape=shapes[0] if single else shapes,
        scratch_shapes=list(scratch),
        input_output_aliases=alias or {},
        compiler_params=pltpu.CompilerParams(vmem_limit_bytes=VMEM_LIMIT),
        cost_estimate=pl.CostEstimate(flops=cost, bytes_accessed=0, transcendentals=0),
    )(*[array for array, _ in ins], *after)


def anywhere():
    return pl.BlockSpec(memory_space=pl.ANY)


def whole(array):
    return pl.BlockSpec(array.shape, lambda step: (0,) * len(array.shape))


def columns(array, tile):
    return pl.BlockSpec((array.shape[0], tile), lambda step: (0, step))


def entire(*arrays):
    return [(array, whole(array)) for array in arrays]


def by_columns(tile, *arrays):
    return [(array, columns(array, tile)) for array in arrays]


def head_kernel(device_ref, flag_ref, gate_ref, hidden_ref, meta_ref, spare_ref):
    top = device_ref.shape[0]
    codes = (device_ref[...] * 2 + flag_ref[...]).astype(F32)
    count = meta_ref.shape[0]
    meta_ref[:, :top, :] = jnp.broadcast_to(codes[None], (count, *codes.shape))
    meta_ref[:, top:, :] = jnp.broadcast_to(gate_ref[...][None], (count, *codes.shape))
    spare_ref[...] = hidden_ref[...]


def head(devices, flags, gates, hidden, spare, count):
    top, tok = devices.shape
    slots, hid = hidden.shape
    last = pl.BlockSpec((spare, hid), lambda step: (slots // spare - 1, 0))
    outs = entire(f32(count, 2 * top, tok), bf16(spare, hid))
    return call(head_kernel, 1, entire(devices, flags, gates) + [(hidden, last)], outs)


def copy_kernel(source_ref, target_ref):
    target_ref[...] = source_ref[...]


def copied(array, tile, *after):
    ins, outs = by_columns(tile, array), by_columns(tile, bf16(*array.shape))[0]
    return call(copy_kernel, array.shape[1] // tile, ins, outs, (), after)


def touch_kernel(source_ref, target_ref):
    pass


def touched(array, *after, cost=0):
    shape = jax.ShapeDtypeStruct(array.shape, array.dtype)
    return call(touch_kernel, 1, [(array, anywhere())], (shape, anywhere()), (), after, {0: 0}, cost)


def plan_rows(meta, cap, half, sel_ref, gate_ref, mix_ref):
    rows, tok = sel_ref.shape
    top = meta.shape[0] // 2
    me = lax.axis_index("expert")
    first = (lax.div(me, half) * half).astype(F32)
    dest = iota((LANES, tok), 0)
    inside = dest < half
    dest = dest + first
    hit = jnp.zeros((LANES, tok), F32)
    gate = jnp.zeros((LANES, tok), F32)
    for k in range(top):
        device = jnp.floor(meta[k : k + 1] * 0.5)
        named = (dest == device) & inside
        hit = jnp.where(named, 1.0, hit)
        gate = jnp.where(named, meta[top + k : top + k + 1], gate)
    place = dot(hit.astype(BF16), before_mask(tok))
    place = jnp.where(hit > 0.5, place, -1.0)
    group, at = row_of(rows, cap, LANES)
    spread = (iota((rows, LANES), 1) == group).astype(BF16)
    to_rows = lambda table: dot(spread, table.astype(BF16))
    chosen = jnp.where(to_rows(place) == at, 1.0, jnp.zeros((rows, tok), F32))
    high = gate.astype(BF16).astype(F32)
    mid = (gate - high).astype(BF16).astype(F32)
    low = gate - high - mid
    high, mid, low = to_rows(high), to_rows(mid), to_rows(low)
    scale = jnp.sum(chosen * (high + mid + low), axis=1, keepdims=True)
    sel_ref[...] = chosen.astype(BF16)
    gate_ref[...] = jnp.broadcast_to(scale, (rows, LANES))
    mix_ref[:tok] = (chosen * high).T.astype(BF16)
    mix_ref[tok:] = (chosen * mid).T.astype(BF16)


def packed_rows(sel_ref, gate_ref, tokens_ref, packed_ref):
    packed_ref[...] = (dot(sel_ref[...], tokens_ref[...]) * gate_ref[:, :1]).astype(BF16)


def pack_own_kernel(cap, half, meta_ref, tokens_ref, packed_ref, mix_ref, sel_ref, gate_ref):
    @pl.when(pl.program_id(0) == 0)
    def _():
        plan_rows(meta_ref[0], cap, half, sel_ref, gate_ref, mix_ref)

    packed_rows(sel_ref, gate_ref, tokens_ref, packed_ref)


def pack_own(meta, tokens, cap, half, tile, *after):
    tok, width = tokens.shape
    rows = half * cap
    first = pl.BlockSpec((1, *meta.shape[1:]), lambda step: (0, 0, 0))
    return call(
        functools.partial(pack_own_kernel, cap, half),
        width // tile,
        [(meta, first)] + by_columns(tile, tokens),
        by_columns(tile, bf16(rows, width)) + entire(bf16(2 * tok, rows)),
        [pltpu.VMEM((rows, tok), BF16), pltpu.VMEM((rows, LANES), F32)],
        after,
    )


def pack(sel, gate, tokens, tile, *after):
    rows, width = sel.shape[0], tokens.shape[1]
    return call(
        packed_rows,
        width // tile,
        entire(sel, gate) + by_columns(tile, tokens),
        by_columns(tile, bf16(rows, width))[0],
        after=after,
        cost=LONG,
    )


def plan_kernel(cap, half, main, metas_ref, sel_ref, gate_ref, mix_ref, *slot_refs):
    count, tops, tok = metas_ref.shape
    top = tops // 2
    rows, slots = slot_refs[0].shape
    spare = slots - main
    me = lax.axis_index("expert")
    mirror = lax.rem(me + half, count)
    plan_rows(metas_ref[mirror], cap, half, sel_ref, gate_ref, mix_ref)

    mine, other = me.astype(F32), mirror.astype(F32)
    none = jnp.zeros((count, tok), F32)
    here, flag, clash = none, none, none
    for k in range(top):
        code = metas_ref[:, k, :]
        device = jnp.floor(code * 0.5)
        here = jnp.where(device == mine, 1.0, here)
        flag = jnp.where(device == mine, code - 2.0 * device, flag)
        clash = jnp.where(device == other, 1.0, clash)
    at_spare = here * flag * (1.0 - clash)
    at_main = here - at_spare
    before = before_mask(tok)
    ones = jnp.ones((tok, LANES), BF16)
    lower = (iota((count, count), 1) < iota((count, count), 0)).astype(BF16)

    def rank(flags):
        flags = flags.astype(BF16)
        return dot(flags, before) + dot(lower, dot(flags, ones).astype(BF16))

    rank_main, rank_spare = rank(at_main), rank(at_spare)
    slot = jnp.where((at_main > 0.5) & (rank_main < main), rank_main + 1.0, none)
    slot = jnp.where((at_spare > 0.5) & (rank_spare < spare), rank_spare + (main + 1.0), slot)
    place = jnp.where(here > 0.5, dot(here.astype(BF16), before), -1.0).astype(BF16)
    tens = jnp.floor(slot * (1.0 / 32.0))
    units = (slot - tens * 32.0).astype(BF16)
    tens = tens.astype(BF16)
    group, _ = row_of(rows, cap, count)
    _, at = row_of(rows, cap, tok)
    start = lax.div(me, half) * half
    for side, base in enumerate((start, lax.rem(start + half, count))):
        spread = (iota((rows, count), 1) == group + base.astype(F32)).astype(BF16)
        chosen = dot(spread, place) == at
        number = dot(spread, tens) * 32.0 + dot(spread, units)
        number = jnp.sum(jnp.where(chosen, number, 0.0), axis=1, keepdims=True)
        give_ref, take_ref = slot_refs[2 * side : 2 * side + 2]
        give_ref[...] = (iota((rows, slots), 1) + 1.0 == number).astype(BF16)
        number = jnp.broadcast_to(number, (rows, LANES)).T[0:1]
        take_ref[...] = (iota((slots, rows), 0) + 1.0 == number).astype(BF16)


def plan(metas, cap, half, main, slots):
    tok = metas.shape[2]
    rows = half * cap
    sides = [bf16(rows, slots), bf16(slots, rows)] * 2
    outs = entire(bf16(rows, tok), f32(rows, LANES), bf16(2 * tok, rows), *sides)
    return call(functools.partial(plan_kernel, cap, half, main), 1, entire(metas), outs)


def side_by_side(source, target_ref):
    half = target_ref.shape[1] // 2
    core = lax.axis_index("dp")
    for at, which in ((0, core), (half, 1 - core)):
        start = pl.multiple_of(which * half, LANES)
        target_ref[:, at : at + half] = source[: target_ref.shape[0], pl.ds(start, half)]


def projected(stack_ref, near_ref, far_ref, out_ref):
    half = near_ref.shape[0]
    total = dot(stack_ref[:, :half], near_ref[...]) + dot(stack_ref[:, half:], far_ref[...])
    out_ref[...] = total.astype(BF16)


def project_spare_kernel(spare_ref, near_ref, far_ref, out_ref, stack_ref):
    @pl.when(pl.program_id(0) == 0)
    def _():
        side_by_side(spare_ref, stack_ref)

    projected(stack_ref, near_ref, far_ref, out_ref)


def project_spare(spare_hidden, near, far, tile, *after):
    width = near.shape[1]
    return call(
        project_spare_kernel,
        width // tile,
        entire(spare_hidden) + by_columns(tile, near, far),
        by_columns(tile, bf16(spare_hidden.shape[0], width))[0],
        [pltpu.VMEM(spare_hidden.shape, BF16)],
        after,
    )


def project_kernel(hidden_ref, spare_ref, near_ref, far_ref, out_ref, near_turned, far_turned, stack_ref, side_ref):
    main, half = out_ref.shape[0], near_ref.shape[0]

    @pl.when(pl.program_id(0) == 0)
    def _():
        side_by_side(hidden_ref, stack_ref)
        side_by_side(spare_ref, side_ref)
        for at, turned_ref in ((0, near_turned), (half, far_turned)):
            turned_ref[:, :main] = stack_ref[:, at : at + half].T
            turned_ref[:, main:] = side_ref[:, at : at + half].T

    projected(stack_ref, near_ref, far_ref, out_ref)


def project(hidden, spare_hidden, near, far, tile, *after):
    half, width = near.shape
    spare = spare_hidden.shape[0]
    slots, hid = hidden.shape
    turned = [bf16(half, slots), bf16(half, slots)]
    return call(
        project_kernel,
        width // tile,
        entire(hidden, spare_hidden) + by_columns(tile, near, far),
        by_columns(tile, bf16(slots - spare, width)) + entire(*turned),
        [pltpu.VMEM((slots - spare, hid), BF16), pltpu.VMEM((spare, hid), BF16)],
        after,
    )


def give_kernel(slot_ref, main_ref, spare_ref, out_ref):
    main = main_ref.shape[0]
    packed = dot(slot_ref[:, :main], main_ref[...]) + dot(slot_ref[:, main:], spare_ref[...])
    out_ref[...] = packed.astype(BF16)


def give(slot, out_main, out_spare, tile, cost, *after):
    rows, width = slot.shape[0], out_main.shape[1]
    return call(
        give_kernel,
        width // tile,
        entire(slot) + by_columns(tile, out_main, out_spare),
        by_columns(tile, bf16(rows, width))[0],
        after=after,
        cost=cost,
    )


def give_main_kernel(slot_ref, main_ref, out_ref):
    out_ref[...] = dot(slot_ref[:, : main_ref.shape[0]], main_ref[...]).astype(BF16)


def give_main(slot, out_main, tile):
    rows, width = slot.shape[0], out_main.shape[1]
    return call(
        give_main_kernel,
        width // tile,
        entire(slot) + by_columns(tile, out_main),
        by_columns(tile, bf16(rows, width))[0],
    )


def give_rest_kernel(slot_ref, given_ref, spare_ref, out_ref):
    rest = dot(slot_ref[:, slot_ref.shape[1] - spare_ref.shape[0] :], spare_ref[...])
    out_ref[...] = given_ref[...] + rest.astype(BF16)


def give_rest(slot, given, out_spare, tile, cost):
    return call(
        give_rest_kernel,
        given.shape[1] // tile,
        entire(slot) + by_columns(tile, given, out_spare),
        by_columns(tile, bf16(*given.shape))[0],
        cost=cost,
    )


def take_kernel(first, own_slot, mirror_slot, own_ref, mirror_ref, out_ref):
    rows = pl.ds(first, out_ref.shape[0])
    total = dot(own_slot[rows, :], own_ref[...]) + dot(mirror_slot[rows, :], mirror_ref[...])
    out_ref[...] = total.astype(BF16)


def take(own_slot, mirror_slot, own, mirror, first, count, tile, *after):
    return call(
        functools.partial(take_kernel, first),
        own.shape[1] // tile,
        entire(own_slot, mirror_slot) + by_columns(tile, own, mirror),
        by_columns(tile, bf16(count, own.shape[1]))[0],
        after=after,
    )


def mixed(mix_ref, rows_ref):
    both = dot(mix_ref[...], rows_ref[...])
    tok = both.shape[0] // 2
    return both[:tok] + both[tok:]


def part_kernel(mix_ref, rows_ref, part_ref):
    part_ref[...] = mixed(mix_ref, rows_ref).astype(BF16)


def total_kernel(mix_ref, rows_ref, other_ref, total_ref):
    total_ref[...] = (mixed(mix_ref, rows_ref) + other_ref[...].astype(F32)).astype(BF16)


def combine(mix, rows, others, tile, *after):
    width = rows.shape[1]
    return call(
        total_kernel if others else part_kernel,
        width // tile,
        entire(mix) + by_columns(tile, rows, *others),
        by_columns(tile, bf16(mix.shape[0] // 2, width))[0],
        after=after,
    )


def stack_grads(main_ref, spare_ref, grads_ref):
    main = main_ref.shape[0]
    grads_ref[:main] = main_ref[...]
    grads_ref[main:] = spare_ref[...]


def weight_kernel(turned, other_turned, main_ref, spare_ref, other_main, other_spare, out_ref, grads_ref):
    stack_grads(main_ref, spare_ref, grads_ref)
    total = dot(turned[...], grads_ref[...])
    stack_grads(other_main, other_spare, grads_ref)
    out_ref[...] = (total + dot(other_turned[...], grads_ref[...])).astype(BF16)


def weight_grad(turned, other_turned, grads, other_grads, tile, *after):
    half, slots = turned.shape
    width = grads[0].shape[1]
    return call(
        weight_kernel,
        width // tile,
        entire(turned, other_turned) + by_columns(tile, *grads, *other_grads),
        by_columns(tile, bf16(half, width))[0],
        [pltpu.VMEM((slots, tile), BF16)],
        after,
    )


def back_kernel(main_ref, grad_ref, near_ref, far_ref, back_ref, spare_ref, sum_ref, grads_ref):
    step = pl.program_id(0)
    half = near_ref.shape[0]
    main = main_ref.shape[0]

    @pl.when(step == 0)
    def _():
        sum_ref[...] = jnp.zeros_like(sum_ref)

    stack_grads(main_ref, grad_ref, grads_ref)
    sum_ref[:, :half] += dot(grads_ref[...], near_ref[...], 1, 1)
    sum_ref[:, half:] += dot(grads_ref[...], far_ref[...], 1, 1)

    @pl.when(step == pl.num_programs(0) - 1)
    def _():
        core = lax.axis_index("dp")
        for at, which in ((0, core), (half, 1 - core)):
            start = pl.multiple_of(which * half, LANES)
            total = sum_ref[:, at : at + half].astype(BF16)
            back_ref[:, pl.ds(start, half)] = total
            spare_ref[:, pl.ds(start, half)] = total[main:]


def project_back(grads_main, grads_spare, near, far, tile, *after):
    main, width = grads_main.shape
    spare = grads_spare.shape[0]
    half = near.shape[0]
    slots = main + spare
    return call(
        back_kernel,
        width // tile,
        by_columns(tile, grads_main, grads_spare, near, far),
        entire(bf16(slots, 2 * half), bf16(spare, 2 * half)),
        [pltpu.VMEM((slots, 2 * half), F32), pltpu.VMEM((slots, tile), BF16)],
        after,
        cost=BACK_COST,
    )


def place_kernel(back_ref, spare_ref, out_ref):
    out_ref[...] = spare_ref[...]


def with_spare(back, back_spare, *after):
    slots, hid = back.shape
    spare = back_spare.shape[0]
    last = pl.BlockSpec((spare, hid), lambda step: (slots // spare - 1, 0))
    ins = [(back, anywhere())] + entire(back_spare)
    return call(place_kernel, 1, ins, (bf16(slots, hid), last), (), after, {0: 0})


def local(hidden_saved, down_weight, route_device, replica_flag, gate_values, grad_out):
    count = lax.axis_size("expert")
    half = count // 2
    tok, top = route_device.shape
    width = grad_out.shape[1]
    cap = 5 * tok * top // (4 * count)
    main = 3 * tok * top // 4
    hidden = hidden_saved[0, 0]
    near = down_weight[0]
    slots = hidden.shape[0]
    tile = width // 2
    groups = [list(range(half)), list(range(half, count))]

    def to_half(rows):
        return lax.all_to_all(
            rows.reshape(half, cap, width), "expert", 0, 0, axis_index_groups=groups, tiled=True
        ).reshape(half * cap, width)

    far = swapped(near, "dp", 1)
    meta, spare_hidden = head(
        route_device.T, replica_flag.T, gate_values.T, hidden, slots - main, count
    )
    spare_hidden = swapped(spare_hidden, "expert", half)
    metas = lax.all_to_all(meta, "expert", 0, 0, tiled=True)
    packed_own, mix_own = pack_own(meta, grad_out, cap, half, tile)
    arrived_own = to_half(touched(touched(packed_own, metas, cost=HEAD_COST), spare_hidden, far))
    out_spare = project_spare(spare_hidden, near, far, tile, mix_own)
    sel, gate, mix_mirror, give_own, take_own, give_mirror, take_mirror = plan(
        metas, cap, half, main, slots
    )
    out_main, turned, far_turned = project(hidden, spare_hidden, near, far, tile, out_spare)
    out_spare = swapped(out_spare, "expert", half)
    given_main = give_main(give_mirror, out_main, tile)
    mirror = swapped(touched(copied(grad_out, tile), out_main, sel), "expert", half)
    other_turned = swapped(far_turned, "dp", 1)
    given_mirror = give_rest(give_mirror, given_main, out_spare, tile, GIVE_COST)
    returned_mirror = to_half(touched(given_mirror, arrived_own))
    packed_mirror = pack(sel, gate, mirror, tile)
    given_own = give(give_own, out_main, out_spare, tile, 0, packed_mirror)
    arrived_mirror = to_half(touched(packed_mirror, returned_mirror, given_own))
    part = swapped(combine(mix_mirror, returned_mirror, [], tile), "expert", half)
    arrived = (take_own, take_mirror, arrived_own, arrived_mirror)
    grads_spare = take(*arrived, main, slots - main, tile)
    returned_own = to_half(touched(given_own, part, grads_spare))
    grads_main = take(*arrived, 0, main, tile, grads_spare)
    other_main = swapped(grads_main, "dp", 1)
    grads_spare = swapped(grads_spare, "expert", half)
    other_spare = swapped(grads_spare, "dp", 1)
    layer_out = combine(mix_own, returned_own, [part], tile)
    back, back_spare = project_back(grads_main, grads_spare, near, far, tile)
    back_spare = swapped(back_spare, "expert", half)
    grad_weight = weight_grad(
        turned, other_turned, (grads_main, grads_spare), (other_main, other_spare), tile, back
    )
    grad_hidden = with_spare(back, back_spare, grad_weight)
    return (layer_out, grad_hidden[None, None], grad_weight[None])


def solution(mesh):
    in_specs = (
        P("dp", "expert", None, None),
        P("expert", "dp", None),
        P(("dp", "expert"), None),
        P(("dp", "expert"), None),
        P(("dp", "expert"), None),
        P(("dp", "expert"), None),
    )
    out_specs = (P(("dp", "expert"), None), P("dp", "expert", None, None), P("expert", "dp", None))
    return jax.shard_map(local, mesh=mesh, in_specs=in_specs, out_specs=out_specs, check_vma=False)
```

```python
import functools
import jax
import jax.numpy as jnp
from jax import lax
from jax.experimental import pallas as pl
from jax.experimental.pallas import tpu as pltpu
from jax.sharding import PartitionSpec as P

F32, BF16, I32 = jnp.float32, jnp.bfloat16, jnp.int32
LANES = 128
LONG = 4_000_000_000_000
GIVE_COST = 5_000_000_000
BACK_COST = 40_000_000_000
VMEM_LIMIT = 64 * 1024 * 1024 - 65536


def swapped(value, axis, distance):
    count = lax.axis_size(axis)
    pairs = [(source, (source + distance) % count) for source in range(count)]
    return lax.ppermute(value, axis, pairs)


def dot(left, right, left_dim=1, right_dim=0):
    contract = (((left_dim,), (right_dim,)), ((), ()))
    return lax.dot_general(left, right, contract, preferred_element_type=F32)


def iota(shape, dim):
    return lax.broadcasted_iota(I32, shape, dim).astype(F32)


def row_of(rows, cap, lanes):
    row = iota((rows, lanes), 0)
    group = jnp.floor((row + 0.5) * (1.0 / cap))
    return group, row - group * cap


def before_mask(size):
    return (iota((size, size), 0) < iota((size, size), 1)).astype(BF16)


def bf16(*shape):
    return jax.ShapeDtypeStruct(shape, BF16)


def f32(*shape):
    return jax.ShapeDtypeStruct(shape, F32)


def call(body, grid, ins, outs, scratch=(), after=(), alias=None, cost=0):
    single = not isinstance(outs, list)
    pairs = [outs] if single else outs
    specs = [spec for _, spec in pairs]
    shapes = [shape for shape, _ in pairs]
    count = len(ins)

    def kernel(*refs):
        body(*refs[:count], *refs[count + len(after) :])

    return pl.pallas_call(
        kernel,
        grid=(grid,),
        in_specs=[spec for _, spec in ins] + [anywhere()] * len(after),
        out_specs=specs[0] if single else specs,
        out_shape=shapes[0] if single else shapes,
        scratch_shapes=list(scratch),
        input_output_aliases=alias or {},
        compiler_params=pltpu.CompilerParams(vmem_limit_bytes=VMEM_LIMIT),
        cost_estimate=pl.CostEstimate(flops=cost, bytes_accessed=0, transcendentals=0),
    )(*[array for array, _ in ins], *after)


def anywhere():
    return pl.BlockSpec(memory_space=pl.ANY)


def whole(array):
    return pl.BlockSpec(array.shape, lambda step: (0,) * len(array.shape))


def columns(array, tile):
    return pl.BlockSpec((array.shape[0], tile), lambda step: (0, step))


def entire(*arrays):
    return [(array, whole(array)) for array in arrays]


def by_columns(tile, *arrays):
    return [(array, columns(array, tile)) for array in arrays]


def head_kernel(device_ref, flag_ref, gate_ref, hidden_ref, meta_ref, spare_ref):
    top = device_ref.shape[0]
    codes = (device_ref[...] * 2 + flag_ref[...]).astype(F32)
    count = meta_ref.shape[0]
    meta_ref[:, :top, :] = jnp.broadcast_to(codes[None], (count, *codes.shape))
    meta_ref[:, top:, :] = jnp.broadcast_to(gate_ref[...][None], (count, *codes.shape))
    spare_ref[...] = hidden_ref[...]


def head(devices, flags, gates, hidden, spare, count):
    top, tok = devices.shape
    slots, hid = hidden.shape
    last = pl.BlockSpec((spare, hid), lambda step: (slots // spare - 1, 0))
    outs = entire(f32(count, 2 * top, tok), bf16(spare, hid))
    return call(head_kernel, 1, entire(devices, flags, gates) + [(hidden, last)], outs)


def copy_kernel(source_ref, target_ref):
    target_ref[...] = source_ref[...]


def copied(array, tile, *after):
    ins, outs = by_columns(tile, array), by_columns(tile, bf16(*array.shape))[0]
    return call(copy_kernel, array.shape[1] // tile, ins, outs, (), after)


def touch_kernel(source_ref, target_ref):
    pass


def touched(array, *after):
    shape = jax.ShapeDtypeStruct(array.shape, array.dtype)
    return call(touch_kernel, 1, [(array, anywhere())], (shape, anywhere()), (), after, {0: 0})


def plan_rows(meta, cap, half, sel_ref, gate_ref, mix_ref):
    rows, tok = sel_ref.shape
    top = meta.shape[0] // 2
    me = lax.axis_index("expert")
    first = (lax.div(me, half) * half).astype(F32)
    dest = iota((LANES, tok), 0)
    inside = dest < half
    dest = dest + first
    hit = jnp.zeros((LANES, tok), F32)
    gate = jnp.zeros((LANES, tok), F32)
    for k in range(top):
        device = jnp.floor(meta[k : k + 1] * 0.5)
        named = (dest == device) & inside
        hit = jnp.where(named, 1.0, hit)
        gate = jnp.where(named, meta[top + k : top + k + 1], gate)
    place = dot(hit.astype(BF16), before_mask(tok))
    place = jnp.where(hit > 0.5, place, -1.0)
    group, at = row_of(rows, cap, LANES)
    spread = (iota((rows, LANES), 1) == group).astype(BF16)
    to_rows = lambda table: dot(spread, table.astype(BF16))
    chosen = jnp.where(to_rows(place) == at, 1.0, jnp.zeros((rows, tok), F32))
    high = gate.astype(BF16).astype(F32)
    mid = (gate - high).astype(BF16).astype(F32)
    low = gate - high - mid
    high, mid, low = to_rows(high), to_rows(mid), to_rows(low)
    scale = jnp.sum(chosen * (high + mid + low), axis=1, keepdims=True)
    sel_ref[...] = chosen.astype(BF16)
    gate_ref[...] = jnp.broadcast_to(scale, (rows, LANES))
    mix_ref[:tok] = (chosen * high).T.astype(BF16)
    mix_ref[tok:] = (chosen * mid).T.astype(BF16)


def packed_rows(sel_ref, gate_ref, tokens_ref, packed_ref):
    packed_ref[...] = (dot(sel_ref[...], tokens_ref[...]) * gate_ref[:, :1]).astype(BF16)


def pack_own_kernel(cap, half, meta_ref, tokens_ref, packed_ref, mix_ref, sel_ref, gate_ref):
    @pl.when(pl.program_id(0) == 0)
    def _():
        plan_rows(meta_ref[0], cap, half, sel_ref, gate_ref, mix_ref)

    packed_rows(sel_ref, gate_ref, tokens_ref, packed_ref)


def pack_own(meta, tokens, cap, half, tile, *after):
    tok, width = tokens.shape
    rows = half * cap
    first = pl.BlockSpec((1, *meta.shape[1:]), lambda step: (0, 0, 0))
    return call(
        functools.partial(pack_own_kernel, cap, half),
        width // tile,
        [(meta, first)] + by_columns(tile, tokens),
        by_columns(tile, bf16(rows, width)) + entire(bf16(2 * tok, rows)),
        [pltpu.VMEM((rows, tok), BF16), pltpu.VMEM((rows, LANES), F32)],
        after,
    )


def pack(sel, gate, tokens, tile, *after):
    rows, width = sel.shape[0], tokens.shape[1]
    return call(
        packed_rows,
        width // tile,
        entire(sel, gate) + by_columns(tile, tokens),
        by_columns(tile, bf16(rows, width))[0],
        after=after,
        cost=LONG,
    )


def plan_kernel(cap, half, main, metas_ref, sel_ref, gate_ref, mix_ref, *slot_refs):
    count, tops, tok = metas_ref.shape
    top = tops // 2
    rows, slots = slot_refs[0].shape
    spare = slots - main
    me = lax.axis_index("expert")
    mirror = lax.rem(me + half, count)
    plan_rows(metas_ref[mirror], cap, half, sel_ref, gate_ref, mix_ref)

    mine, other = me.astype(F32), mirror.astype(F32)
    none = jnp.zeros((count, tok), F32)
    here, flag, clash = none, none, none
    for k in range(top):
        code = metas_ref[:, k, :]
        device = jnp.floor(code * 0.5)
        here = jnp.where(device == mine, 1.0, here)
        flag = jnp.where(device == mine, code - 2.0 * device, flag)
        clash = jnp.where(device == other, 1.0, clash)
    at_spare = here * flag * (1.0 - clash)
    at_main = here - at_spare
    before = before_mask(tok)
    ones = jnp.ones((tok, LANES), BF16)
    lower = (iota((count, count), 1) < iota((count, count), 0)).astype(BF16)

    def rank(flags):
        flags = flags.astype(BF16)
        return dot(flags, before) + dot(lower, dot(flags, ones).astype(BF16))

    rank_main, rank_spare = rank(at_main), rank(at_spare)
    slot = jnp.where((at_main > 0.5) & (rank_main < main), rank_main + 1.0, none)
    slot = jnp.where((at_spare > 0.5) & (rank_spare < spare), rank_spare + (main + 1.0), slot)
    place = jnp.where(here > 0.5, dot(here.astype(BF16), before), -1.0).astype(BF16)
    tens = jnp.floor(slot * (1.0 / 32.0))
    units = (slot - tens * 32.0).astype(BF16)
    tens = tens.astype(BF16)
    group, _ = row_of(rows, cap, count)
    _, at = row_of(rows, cap, tok)
    start = lax.div(me, half) * half
    for side, base in enumerate((start, lax.rem(start + half, count))):
        spread = (iota((rows, count), 1) == group + base.astype(F32)).astype(BF16)
        chosen = dot(spread, place) == at
        number = dot(spread, tens) * 32.0 + dot(spread, units)
        number = jnp.sum(jnp.where(chosen, number, 0.0), axis=1, keepdims=True)
        give_ref, take_ref = slot_refs[2 * side : 2 * side + 2]
        give_ref[...] = (iota((rows, slots), 1) + 1.0 == number).astype(BF16)
        number = jnp.broadcast_to(number, (rows, LANES)).T[0:1]
        take_ref[...] = (iota((slots, rows), 0) + 1.0 == number).astype(BF16)


def plan(metas, cap, half, main, slots):
    tok = metas.shape[2]
    rows = half * cap
    sides = [bf16(rows, slots), bf16(slots, rows)] * 2
    outs = entire(bf16(rows, tok), f32(rows, LANES), bf16(2 * tok, rows), *sides)
    return call(functools.partial(plan_kernel, cap, half, main), 1, entire(metas), outs)


def side_by_side(source, target_ref):
    half = target_ref.shape[1] // 2
    core = lax.axis_index("dp")
    for at, which in ((0, core), (half, 1 - core)):
        start = pl.multiple_of(which * half, LANES)
        target_ref[:, at : at + half] = source[: target_ref.shape[0], pl.ds(start, half)]


def projected(stack_ref, near_ref, far_ref, out_ref):
    half = near_ref.shape[0]
    total = dot(stack_ref[:, :half], near_ref[...]) + dot(stack_ref[:, half:], far_ref[...])
    out_ref[...] = total.astype(BF16)


def project_spare_kernel(spare_ref, near_ref, far_ref, out_ref, stack_ref):
    @pl.when(pl.program_id(0) == 0)
    def _():
        side_by_side(spare_ref, stack_ref)

    projected(stack_ref, near_ref, far_ref, out_ref)


def project_spare(spare_hidden, near, far, tile, *after):
    width = near.shape[1]
    return call(
        project_spare_kernel,
        width // tile,
        entire(spare_hidden) + by_columns(tile, near, far),
        by_columns(tile, bf16(spare_hidden.shape[0], width))[0],
        [pltpu.VMEM(spare_hidden.shape, BF16)],
        after,
    )


def project_kernel(hidden_ref, spare_ref, near_ref, far_ref, out_ref, near_turned, far_turned, stack_ref, side_ref):
    main, half = out_ref.shape[0], near_ref.shape[0]

    @pl.when(pl.program_id(0) == 0)
    def _():
        side_by_side(hidden_ref, stack_ref)
        side_by_side(spare_ref, side_ref)
        for at, turned_ref in ((0, near_turned), (half, far_turned)):
            turned_ref[:, :main] = stack_ref[:, at : at + half].T
            turned_ref[:, main:] = side_ref[:, at : at + half].T

    projected(stack_ref, near_ref, far_ref, out_ref)


def project(hidden, spare_hidden, near, far, tile, *after):
    half, width = near.shape
    spare = spare_hidden.shape[0]
    slots, hid = hidden.shape
    turned = [bf16(half, slots), bf16(half, slots)]
    return call(
        project_kernel,
        width // tile,
        entire(hidden, spare_hidden) + by_columns(tile, near, far),
        by_columns(tile, bf16(slots - spare, width)) + entire(*turned),
        [pltpu.VMEM((slots - spare, hid), BF16), pltpu.VMEM((spare, hid), BF16)],
        after,
    )


def give_kernel(slot_ref, main_ref, spare_ref, out_ref):
    main = main_ref.shape[0]
    packed = dot(slot_ref[:, :main], main_ref[...]) + dot(slot_ref[:, main:], spare_ref[...])
    out_ref[...] = packed.astype(BF16)


def give(slot, out_main, out_spare, tile, cost, *after):
    rows, width = slot.shape[0], out_main.shape[1]
    return call(
        give_kernel,
        width // tile,
        entire(slot) + by_columns(tile, out_main, out_spare),
        by_columns(tile, bf16(rows, width))[0],
        after=after,
        cost=cost,
    )


def give_main_kernel(slot_ref, main_ref, out_ref):
    out_ref[...] = dot(slot_ref[:, : main_ref.shape[0]], main_ref[...]).astype(BF16)


def give_main(slot, out_main, tile):
    rows, width = slot.shape[0], out_main.shape[1]
    return call(
        give_main_kernel,
        width // tile,
        entire(slot) + by_columns(tile, out_main),
        by_columns(tile, bf16(rows, width))[0],
    )


def give_rest_kernel(slot_ref, given_ref, spare_ref, out_ref):
    rest = dot(slot_ref[:, slot_ref.shape[1] - spare_ref.shape[0] :], spare_ref[...])
    out_ref[...] = given_ref[...] + rest.astype(BF16)


def give_rest(slot, given, out_spare, tile, cost):
    return call(
        give_rest_kernel,
        given.shape[1] // tile,
        entire(slot) + by_columns(tile, given, out_spare),
        by_columns(tile, bf16(*given.shape))[0],
        cost=cost,
    )


def take_kernel(first, own_slot, mirror_slot, own_ref, mirror_ref, out_ref):
    rows = pl.ds(first, out_ref.shape[0])
    total = dot(own_slot[rows, :], own_ref[...]) + dot(mirror_slot[rows, :], mirror_ref[...])
    out_ref[...] = total.astype(BF16)


def take(own_slot, mirror_slot, own, mirror, first, count, tile, *after):
    return call(
        functools.partial(take_kernel, first),
        own.shape[1] // tile,
        entire(own_slot, mirror_slot) + by_columns(tile, own, mirror),
        by_columns(tile, bf16(count, own.shape[1]))[0],
        after=after,
    )


def mixed(mix_ref, rows_ref):
    both = dot(mix_ref[...], rows_ref[...])
    tok = both.shape[0] // 2
    return both[:tok] + both[tok:]


def part_kernel(mix_ref, rows_ref, part_ref):
    part_ref[...] = mixed(mix_ref, rows_ref).astype(BF16)


def total_kernel(mix_ref, rows_ref, other_ref, total_ref):
    total_ref[...] = (mixed(mix_ref, rows_ref) + other_ref[...].astype(F32)).astype(BF16)


def combine(mix, rows, others, tile, *after):
    width = rows.shape[1]
    return call(
        total_kernel if others else part_kernel,
        width // tile,
        entire(mix) + by_columns(tile, rows, *others),
        by_columns(tile, bf16(mix.shape[0] // 2, width))[0],
        after=after,
    )


def stack_grads(main_ref, spare_ref, grads_ref):
    main = main_ref.shape[0]
    grads_ref[:main] = main_ref[...]
    grads_ref[main:] = spare_ref[...]


def weight_kernel(turned, other_turned, main_ref, spare_ref, other_main, other_spare, out_ref, grads_ref):
    stack_grads(main_ref, spare_ref, grads_ref)
    total = dot(turned[...], grads_ref[...])
    stack_grads(other_main, other_spare, grads_ref)
    out_ref[...] = (total + dot(other_turned[...], grads_ref[...])).astype(BF16)


def weight_grad(turned, other_turned, grads, other_grads, tile, *after):
    half, slots = turned.shape
    width = grads[0].shape[1]
    return call(
        weight_kernel,
        width // tile,
        entire(turned, other_turned) + by_columns(tile, *grads, *other_grads),
        by_columns(tile, bf16(half, width))[0],
        [pltpu.VMEM((slots, tile), BF16)],
        after,
    )


def back_kernel(main_ref, grad_ref, near_ref, far_ref, back_ref, spare_ref, sum_ref, grads_ref):
    step = pl.program_id(0)
    half = near_ref.shape[0]
    main = main_ref.shape[0]

    @pl.when(step == 0)
    def _():
        sum_ref[...] = jnp.zeros_like(sum_ref)

    stack_grads(main_ref, grad_ref, grads_ref)
    sum_ref[:, :half] += dot(grads_ref[...], near_ref[...], 1, 1)
    sum_ref[:, half:] += dot(grads_ref[...], far_ref[...], 1, 1)

    @pl.when(step == pl.num_programs(0) - 1)
    def _():
        core = lax.axis_index("dp")
        for at, which in ((0, core), (half, 1 - core)):
            start = pl.multiple_of(which * half, LANES)
            total = sum_ref[:, at : at + half].astype(BF16)
            back_ref[:, pl.ds(start, half)] = total
            spare_ref[:, pl.ds(start, half)] = total[main:]


def project_back(grads_main, grads_spare, near, far, tile, *after):
    main, width = grads_main.shape
    spare = grads_spare.shape[0]
    half = near.shape[0]
    slots = main + spare
    return call(
        back_kernel,
        width // tile,
        by_columns(tile, grads_main, grads_spare, near, far),
        entire(bf16(slots, 2 * half), bf16(spare, 2 * half)),
        [pltpu.VMEM((slots, 2 * half), F32), pltpu.VMEM((slots, tile), BF16)],
        after,
        cost=BACK_COST,
    )


def place_kernel(back_ref, spare_ref, out_ref):
    out_ref[...] = spare_ref[...]


def with_spare(back, back_spare, *after):
    slots, hid = back.shape
    spare = back_spare.shape[0]
    last = pl.BlockSpec((spare, hid), lambda step: (slots // spare - 1, 0))
    ins = [(back, anywhere())] + entire(back_spare)
    return call(place_kernel, 1, ins, (bf16(slots, hid), last), (), after, {0: 0})


def local(hidden_saved, down_weight, route_device, replica_flag, gate_values, grad_out):
    count = lax.axis_size("expert")
    half = count // 2
    tok, top = route_device.shape
    width = grad_out.shape[1]
    cap = 5 * tok * top // (4 * count)
    main = 3 * tok * top // 4
    hidden = hidden_saved[0, 0]
    near = down_weight[0]
    slots = hidden.shape[0]
    tile = width // 2
    groups = [list(range(half)), list(range(half, count))]

    def to_half(rows):
        return lax.all_to_all(
            rows.reshape(half, cap, width), "expert", 0, 0, axis_index_groups=groups, tiled=True
        ).reshape(half * cap, width)

    far = swapped(near, "dp", 1)
    meta, spare_hidden = head(
        route_device.T, replica_flag.T, gate_values.T, hidden, slots - main, count
    )
    spare_hidden = swapped(spare_hidden, "expert", half)
    metas = lax.all_to_all(meta, "expert", 0, 0, tiled=True)
    packed_own, mix_own = pack_own(meta, grad_out, cap, half, tile)
    arrived_own = to_half(touched(packed_own, metas, spare_hidden, far))
    out_spare = project_spare(spare_hidden, near, far, tile, mix_own)
    sel, gate, mix_mirror, give_own, take_own, give_mirror, take_mirror = plan(
        metas, cap, half, main, slots
    )
    out_main, turned, far_turned = project(hidden, spare_hidden, near, far, tile, out_spare)
    out_spare = swapped(out_spare, "expert", half)
    given_main = give_main(give_mirror, out_main, tile)
    mirror = swapped(touched(copied(grad_out, tile), out_main, sel), "expert", half)
    other_turned = swapped(far_turned, "dp", 1)
    given_mirror = give_rest(give_mirror, given_main, out_spare, tile, GIVE_COST)
    returned_mirror = to_half(touched(given_mirror, arrived_own))
    packed_mirror = pack(sel, gate, mirror, tile)
    given_own = give(give_own, out_main, out_spare, tile, 0, packed_mirror)
    arrived_mirror = to_half(touched(packed_mirror, returned_mirror, given_own))
    part = swapped(combine(mix_mirror, returned_mirror, [], tile), "expert", half)
    arrived = (take_own, take_mirror, arrived_own, arrived_mirror)
    grads_spare = take(*arrived, main, slots - main, tile)
    returned_own = to_half(touched(given_own, part, grads_spare))
    grads_main = take(*arrived, 0, main, tile, grads_spare)
    other_main = swapped(grads_main, "dp", 1)
    grads_spare = swapped(grads_spare, "expert", half)
    other_spare = swapped(grads_spare, "dp", 1)
    layer_out = combine(mix_own, returned_own, [part], tile)
    back, back_spare = project_back(grads_main, grads_spare, near, far, tile)
    back_spare = swapped(back_spare, "expert", half)
    grad_weight = weight_grad(
        turned, other_turned, (grads_main, grads_spare), (other_main, other_spare), tile, back
    )
    grad_hidden = with_spare(back, back_spare, grad_weight)
    return (layer_out, grad_hidden[None, None], grad_weight[None])


def solution(mesh):
    in_specs = (
        P("dp", "expert", None, None),
        P("expert", "dp", None),
        P(("dp", "expert"), None),
        P(("dp", "expert"), None),
        P(("dp", "expert"), None),
        P(("dp", "expert"), None),
    )
    out_specs = (P(("dp", "expert"), None), P("dp", "expert", None, None), P("expert", "dp", None))
    return jax.shard_map(local, mesh=mesh, in_specs=in_specs, out_specs=out_specs, check_vma=False)
```

```python
import functools
import jax
import jax.numpy as jnp
from jax import lax
from jax.experimental import pallas as pl
from jax.experimental.pallas import tpu as pltpu
from jax.sharding import PartitionSpec as P

F32, BF16, I32 = jnp.float32, jnp.bfloat16, jnp.int32
LANES = 128
LONG = 4_000_000_000_000
GIVE_COST = 5_000_000_000
BACK_COST = 40_000_000_000
VMEM_LIMIT = 64 * 1024 * 1024 - 65536


def swapped(value, axis, distance):
    count = lax.axis_size(axis)
    pairs = [(source, (source + distance) % count) for source in range(count)]
    return lax.ppermute(value, axis, pairs)


def dot(left, right, left_dim=1, right_dim=0):
    contract = (((left_dim,), (right_dim,)), ((), ()))
    return lax.dot_general(left, right, contract, preferred_element_type=F32)


def iota(shape, dim):
    return lax.broadcasted_iota(I32, shape, dim).astype(F32)


def row_of(rows, cap, lanes):
    row = iota((rows, lanes), 0)
    group = jnp.floor((row + 0.5) * (1.0 / cap))
    return group, row - group * cap


def before_mask(size):
    return (iota((size, size), 0) < iota((size, size), 1)).astype(BF16)


def bf16(*shape):
    return jax.ShapeDtypeStruct(shape, BF16)


def f32(*shape):
    return jax.ShapeDtypeStruct(shape, F32)


def call(body, grid, ins, outs, scratch=(), after=(), alias=None, cost=0):
    single = not isinstance(outs, list)
    pairs = [outs] if single else outs
    specs = [spec for _, spec in pairs]
    shapes = [shape for shape, _ in pairs]
    count = len(ins)

    def kernel(*refs):
        body(*refs[:count], *refs[count + len(after) :])

    return pl.pallas_call(
        kernel,
        grid=(grid,),
        in_specs=[spec for _, spec in ins] + [anywhere()] * len(after),
        out_specs=specs[0] if single else specs,
        out_shape=shapes[0] if single else shapes,
        scratch_shapes=list(scratch),
        input_output_aliases=alias or {},
        compiler_params=pltpu.CompilerParams(vmem_limit_bytes=VMEM_LIMIT),
        cost_estimate=pl.CostEstimate(flops=cost, bytes_accessed=0, transcendentals=0),
    )(*[array for array, _ in ins], *after)


def anywhere():
    return pl.BlockSpec(memory_space=pl.ANY)


def whole(array):
    return pl.BlockSpec(array.shape, lambda step: (0,) * len(array.shape))


def columns(array, tile):
    return pl.BlockSpec((array.shape[0], tile), lambda step: (0, step))


def entire(*arrays):
    return [(array, whole(array)) for array in arrays]


def by_columns(tile, *arrays):
    return [(array, columns(array, tile)) for array in arrays]


def head_kernel(device_ref, flag_ref, gate_ref, hidden_ref, meta_ref, spare_ref):
    top = device_ref.shape[0]
    codes = (device_ref[...] * 2 + flag_ref[...]).astype(F32)
    count = meta_ref.shape[0]
    meta_ref[:, :top, :] = jnp.broadcast_to(codes[None], (count, *codes.shape))
    meta_ref[:, top:, :] = jnp.broadcast_to(gate_ref[...][None], (count, *codes.shape))
    spare_ref[...] = hidden_ref[...]


def head(devices, flags, gates, hidden, spare, count):
    top, tok = devices.shape
    slots, hid = hidden.shape
    last = pl.BlockSpec((spare, hid), lambda step: (slots // spare - 1, 0))
    outs = entire(f32(count, 2 * top, tok), bf16(spare, hid))
    return call(head_kernel, 1, entire(devices, flags, gates) + [(hidden, last)], outs)


def copy_kernel(source_ref, target_ref):
    target_ref[...] = source_ref[...]


def copied(array, tile, *after):
    ins, outs = by_columns(tile, array), by_columns(tile, bf16(*array.shape))[0]
    return call(copy_kernel, array.shape[1] // tile, ins, outs, (), after)


def touch_kernel(source_ref, target_ref):
    pass


def touched(array, *after):
    shape = jax.ShapeDtypeStruct(array.shape, array.dtype)
    return call(touch_kernel, 1, [(array, anywhere())], (shape, anywhere()), (), after, {0: 0})


def plan_rows(meta, cap, half, sel_ref, gate_ref, mix_ref):
    rows, tok = sel_ref.shape
    top = meta.shape[0] // 2
    me = lax.axis_index("expert")
    first = (lax.div(me, half) * half).astype(F32)
    dest = iota((LANES, tok), 0)
    inside = dest < half
    dest = dest + first
    hit = jnp.zeros((LANES, tok), F32)
    gate = jnp.zeros((LANES, tok), F32)
    for k in range(top):
        device = jnp.floor(meta[k : k + 1] * 0.5)
        named = (dest == device) & inside
        hit = jnp.where(named, 1.0, hit)
        gate = jnp.where(named, meta[top + k : top + k + 1], gate)
    place = dot(hit.astype(BF16), before_mask(tok))
    place = jnp.where(hit > 0.5, place, -1.0)
    group, at = row_of(rows, cap, LANES)
    spread = (iota((rows, LANES), 1) == group).astype(BF16)
    to_rows = lambda table: dot(spread, table.astype(BF16))
    chosen = jnp.where(to_rows(place) == at, 1.0, jnp.zeros((rows, tok), F32))
    high = gate.astype(BF16).astype(F32)
    mid = (gate - high).astype(BF16).astype(F32)
    low = gate - high - mid
    high, mid, low = to_rows(high), to_rows(mid), to_rows(low)
    scale = jnp.sum(chosen * (high + mid + low), axis=1, keepdims=True)
    sel_ref[...] = chosen.astype(BF16)
    gate_ref[...] = jnp.broadcast_to(scale, (rows, LANES))
    mix_ref[:tok] = (chosen * high).T.astype(BF16)
    mix_ref[tok:] = (chosen * mid).T.astype(BF16)


def packed_rows(sel_ref, gate_ref, tokens_ref, packed_ref):
    packed_ref[...] = (dot(sel_ref[...], tokens_ref[...]) * gate_ref[:, :1]).astype(BF16)


def pack(sel, gate, tokens, tile, *after):
    rows, width = sel.shape[0], tokens.shape[1]
    return call(
        packed_rows,
        width // tile,
        entire(sel, gate) + by_columns(tile, tokens),
        by_columns(tile, bf16(rows, width))[0],
        after=after,
        cost=LONG,
    )


def plan_plane(metas_ref, cap, turned, sel_ref, gate_ref):
    count, tops, tok = metas_ref.shape
    rows = sel_ref.shape[0]
    top = tops // 2
    size = count // 4
    me = lax.axis_index("expert")
    plane, mine = lax.div(me, size), lax.rem(me, size)
    index = lax.broadcasted_iota(I32, (LANES, tok), 0)
    inside = index < size
    dest = ((index ^ mine if turned else index) + plane * size).astype(F32)
    group, at = row_of(rows, cap, LANES)
    block = jnp.floor(group * 0.5)
    side = group - 2.0 * block
    scale = jnp.zeros((rows, 1), F32)
    for which, source in enumerate((me, (plane ^ 1) * size + mine)):
        meta = metas_ref[source]
        hit = jnp.zeros((LANES, tok), F32)
        gate = jnp.zeros((LANES, tok), F32)
        for k in range(top):
            named = (dest == jnp.floor(meta[k : k + 1] * 0.5)) & inside
            hit = jnp.where(named, 1.0, hit)
            gate = jnp.where(named, meta[top + k : top + k + 1], gate)
        place = dot(hit.astype(BF16), before_mask(tok))
        place = jnp.where(hit > 0.5, place + 1.0, 0.0)
        spread = ((iota((rows, LANES), 1) == block) & (side == 1.0 * which)).astype(BF16)
        to_rows = lambda table: dot(spread, table.astype(BF16))
        chosen = jnp.where(to_rows(place) == at + 1.0, 1.0, jnp.zeros((rows, tok), F32))
        high = gate.astype(BF16).astype(F32)
        mid = (gate - high).astype(BF16).astype(F32)
        low = gate - high - mid
        total = to_rows(high) + to_rows(mid) + to_rows(low)
        scale = scale + jnp.sum(chosen * total, axis=1, keepdims=True)
        sel_ref[:, which * tok : (which + 1) * tok] = chosen.astype(BF16)
    gate_ref[...] = jnp.broadcast_to(scale, (rows, LANES))


def plan_kernel(cap, half, main, turned, metas_ref, *refs):
    sel_ref, gate_ref, mix_ref, plane_sel, plane_gate, mix_own = refs[:6]
    give_own, take_plane, give_mirror, take_mirror = refs[6:10]
    spare_sel, spare_gate = refs[10:]
    count, tops, tok = metas_ref.shape
    top = tops // 2
    rows, slots = give_own.shape
    spare = slots - main
    size = count // 4
    me = lax.axis_index("expert")
    mirror = lax.rem(me + half, count)
    plan_plane(metas_ref, cap, turned, plane_sel, plane_gate)
    plan_rows(metas_ref[me], cap, half, spare_sel, spare_gate, mix_own)
    plan_rows(metas_ref[mirror], cap, half, sel_ref, gate_ref, mix_ref)

    mine, other = me.astype(F32), mirror.astype(F32)
    none = jnp.zeros((count, tok), F32)
    here, flag, clash = none, none, none
    for k in range(top):
        code = metas_ref[:, k, :]
        device = jnp.floor(code * 0.5)
        here = jnp.where(device == mine, 1.0, here)
        flag = jnp.where(device == mine, code - 2.0 * device, flag)
        clash = jnp.where(device == other, 1.0, clash)
    at_spare = here * flag * (1.0 - clash)
    at_main = here - at_spare
    before = before_mask(tok)
    ones = jnp.ones((tok, LANES), BF16)
    lower = (iota((count, count), 1) < iota((count, count), 0)).astype(BF16)

    def rank(flags):
        flags = flags.astype(BF16)
        return dot(flags, before) + dot(lower, dot(flags, ones).astype(BF16))

    rank_main, rank_spare = rank(at_main), rank(at_spare)
    slot = jnp.where((at_main > 0.5) & (rank_main < main), rank_main + 1.0, none)
    slot = jnp.where((at_spare > 0.5) & (rank_spare < spare), rank_spare + (main + 1.0), slot)
    place = jnp.where(here > 0.5, dot(here.astype(BF16), before), -1.0).astype(BF16)
    tens = jnp.floor(slot * (1.0 / 32.0))
    units = (slot - tens * 32.0).astype(BF16)
    tens = tens.astype(BF16)
    group, _ = row_of(rows, cap, count)
    _, at = row_of(rows, cap, tok)

    def numbers(sources):
        spread = (iota((rows, count), 1) == sources).astype(BF16)
        chosen = dot(spread, place) == at
        number = dot(spread, tens) * 32.0 + dot(spread, units)
        return jnp.sum(jnp.where(chosen, number, 0.0), axis=1, keepdims=True)

    def give_to(ref, number):
        ref[...] = (iota((rows, slots), 1) + 1.0 == number).astype(BF16)

    def take_to(ref, number):
        number = jnp.broadcast_to(number, (rows, LANES)).T[0:1]
        ref[...] = (iota((slots, rows), 0) + 1.0 == number).astype(BF16)

    start = lax.div(me, half) * half
    give_to(give_own, numbers(group + start.astype(F32)))
    number = numbers(group + lax.rem(start + half, count).astype(F32))
    give_to(give_mirror, number)
    take_to(take_mirror, number)
    block = jnp.floor(group * 0.5)
    side = group - 2.0 * block
    plane = lax.div(me, size)
    holder = block.astype(I32)
    holder = (holder ^ lax.rem(me, size) if turned else holder).astype(F32)
    start = jnp.where(side == 0.0, (plane * size).astype(F32), ((plane ^ 1) * size).astype(F32))
    take_to(take_plane, numbers(holder + start))


def plan(metas, cap, half, main, slots, turned):
    tok = metas.shape[2]
    rows = half * cap
    outs = [bf16(rows, tok), f32(rows, LANES), bf16(2 * tok, rows)]
    outs += [bf16(rows, 2 * tok), f32(rows, LANES), bf16(2 * tok, rows)]
    outs += [bf16(rows, slots), bf16(slots, rows)] * 2
    scratch = [pltpu.VMEM((rows, tok), BF16), pltpu.VMEM((rows, LANES), F32)]
    body = functools.partial(plan_kernel, cap, half, main, turned)
    return call(body, 1, entire(metas), entire(*outs), scratch)


def pack_plane_kernel(sel_ref, gate_ref, own_ref, neighbour_ref, *outs):
    tok = own_ref.shape[0]
    packed = dot(sel_ref[:, :tok], own_ref[...]) + dot(sel_ref[:, tok:], neighbour_ref[...])
    packed = (packed * gate_ref[:, :1]).astype(BF16)
    rows = outs[0].shape[0]
    for index, out_ref in enumerate(outs):
        out_ref[...] = packed[index * rows : (index + 1) * rows]


def pack_plane(sel, gate, own, neighbour, blocks, tile):
    width = own.shape[1]
    shapes = [bf16(sel.shape[0] // blocks, width)] * blocks
    ins = entire(sel, gate) + by_columns(tile, own, neighbour)
    return call(pack_plane_kernel, width // tile, ins, by_columns(tile, *shapes))


def side_by_side(source, target_ref):
    half = target_ref.shape[1] // 2
    core = lax.axis_index("dp")
    for at, which in ((0, core), (half, 1 - core)):
        start = pl.multiple_of(which * half, LANES)
        target_ref[:, at : at + half] = source[: target_ref.shape[0], pl.ds(start, half)]


def projected(stack_ref, near_ref, far_ref, out_ref):
    half = near_ref.shape[0]
    total = dot(stack_ref[:, :half], near_ref[...]) + dot(stack_ref[:, half:], far_ref[...])
    out_ref[...] = total.astype(BF16)


def project_spare_kernel(spare_ref, near_ref, far_ref, out_ref, stack_ref):
    @pl.when(pl.program_id(0) == 0)
    def _():
        side_by_side(spare_ref, stack_ref)

    projected(stack_ref, near_ref, far_ref, out_ref)


def project_spare(spare_hidden, near, far, tile, *after):
    width = near.shape[1]
    return call(
        project_spare_kernel,
        width // tile,
        entire(spare_hidden) + by_columns(tile, near, far),
        by_columns(tile, bf16(spare_hidden.shape[0], width))[0],
        [pltpu.VMEM(spare_hidden.shape, BF16)],
        after,
    )


def project_kernel(hidden_ref, spare_ref, near_ref, far_ref, out_ref, near_turned, far_turned, stack_ref, side_ref):
    main, half = out_ref.shape[0], near_ref.shape[0]

    @pl.when(pl.program_id(0) == 0)
    def _():
        side_by_side(hidden_ref, stack_ref)
        side_by_side(spare_ref, side_ref)
        for at, turned_ref in ((0, near_turned), (half, far_turned)):
            turned_ref[:, :main] = stack_ref[:, at : at + half].T
            turned_ref[:, main:] = side_ref[:, at : at + half].T

    projected(stack_ref, near_ref, far_ref, out_ref)


def project(hidden, spare_hidden, near, far, tile, *after):
    half, width = near.shape
    spare = spare_hidden.shape[0]
    slots, hid = hidden.shape
    turned = [bf16(half, slots), bf16(half, slots)]
    return call(
        project_kernel,
        width // tile,
        entire(hidden, spare_hidden) + by_columns(tile, near, far),
        by_columns(tile, bf16(slots - spare, width)) + entire(*turned),
        [pltpu.VMEM((slots - spare, hid), BF16), pltpu.VMEM((spare, hid), BF16)],
        after,
    )


def give_kernel(slot_ref, main_ref, spare_ref, out_ref):
    main = main_ref.shape[0]
    packed = dot(slot_ref[:, :main], main_ref[...]) + dot(slot_ref[:, main:], spare_ref[...])
    out_ref[...] = packed.astype(BF16)


def give(slot, out_main, out_spare, tile, cost, *after):
    rows, width = slot.shape[0], out_main.shape[1]
    return call(
        give_kernel,
        width // tile,
        entire(slot) + by_columns(tile, out_main, out_spare),
        by_columns(tile, bf16(rows, width))[0],
        after=after,
        cost=cost,
    )


def give_main_kernel(slot_ref, main_ref, out_ref):
    out_ref[...] = dot(slot_ref[:, : main_ref.shape[0]], main_ref[...]).astype(BF16)


def give_main(slot, out_main, tile):
    rows, width = slot.shape[0], out_main.shape[1]
    return call(
        give_main_kernel,
        width // tile,
        entire(slot) + by_columns(tile, out_main),
        by_columns(tile, bf16(rows, width))[0],
    )


def give_rest_kernel(slot_ref, given_ref, spare_ref, out_ref):
    rest = dot(slot_ref[:, slot_ref.shape[1] - spare_ref.shape[0] :], spare_ref[...])
    out_ref[...] = given_ref[...] + rest.astype(BF16)


def give_rest(slot, given, out_spare, tile, cost):
    return call(
        give_rest_kernel,
        given.shape[1] // tile,
        entire(slot) + by_columns(tile, given, out_spare),
        by_columns(tile, bf16(*given.shape))[0],
        cost=cost,
    )


def take_kernel(first, own_slot, mirror_slot, mirror_ref, *rest):
    blocks, (out_ref, stack_ref) = rest[:-2], rest[-2:]
    size = blocks[0].shape[0]
    for index, block_ref in enumerate(blocks):
        stack_ref[index * size : (index + 1) * size] = block_ref[...]
    rows = pl.ds(first, out_ref.shape[0])
    total = dot(own_slot[rows, :], stack_ref[...]) + dot(mirror_slot[rows, :], mirror_ref[...])
    out_ref[...] = total.astype(BF16)


def take(own_slot, mirror_slot, mirror, own, first, count, tile, *after):
    rows, width = mirror.shape
    return call(
        functools.partial(take_kernel, first),
        width // tile,
        entire(own_slot, mirror_slot) + by_columns(tile, mirror, *own),
        by_columns(tile, bf16(count, width))[0],
        [pltpu.VMEM((rows, tile), BF16)],
        after,
    )


def mixed(mix_ref, rows_ref):
    both = dot(mix_ref[...], rows_ref[...])
    tok = both.shape[0] // 2
    return both[:tok] + both[tok:]


def part_kernel(mix_ref, rows_ref, part_ref):
    part_ref[...] = mixed(mix_ref, rows_ref).astype(BF16)


def total_kernel(mix_ref, rows_ref, other_ref, total_ref):
    total_ref[...] = (mixed(mix_ref, rows_ref) + other_ref[...].astype(F32)).astype(BF16)


def combine(mix, rows, others, tile, *after):
    width = rows.shape[1]
    return call(
        total_kernel if others else part_kernel,
        width // tile,
        entire(mix) + by_columns(tile, rows, *others),
        by_columns(tile, bf16(mix.shape[0] // 2, width))[0],
        after=after,
    )


def stack_grads(main_ref, spare_ref, grads_ref):
    main = main_ref.shape[0]
    grads_ref[:main] = main_ref[...]
    grads_ref[main:] = spare_ref[...]


def weight_kernel(turned, other_turned, main_ref, spare_ref, other_main, other_spare, out_ref, grads_ref):
    stack_grads(main_ref, spare_ref, grads_ref)
    total = dot(turned[...], grads_ref[...])
    stack_grads(other_main, other_spare, grads_ref)
    out_ref[...] = (total + dot(other_turned[...], grads_ref[...])).astype(BF16)


def weight_grad(turned, other_turned, grads, other_grads, tile, *after):
    half, slots = turned.shape
    width = grads[0].shape[1]
    return call(
        weight_kernel,
        width // tile,
        entire(turned, other_turned) + by_columns(tile, *grads, *other_grads),
        by_columns(tile, bf16(half, width))[0],
        [pltpu.VMEM((slots, tile), BF16)],
        after,
    )


def back_kernel(main_ref, grad_ref, near_ref, far_ref, back_ref, spare_ref, sum_ref, grads_ref):
    step = pl.program_id(0)
    half = near_ref.shape[0]
    main = main_ref.shape[0]

    @pl.when(step == 0)
    def _():
        sum_ref[...] = jnp.zeros_like(sum_ref)

    stack_grads(main_ref, grad_ref, grads_ref)
    sum_ref[:, :half] += dot(grads_ref[...], near_ref[...], 1, 1)
    sum_ref[:, half:] += dot(grads_ref[...], far_ref[...], 1, 1)

    @pl.when(step == pl.num_programs(0) - 1)
    def _():
        core = lax.axis_index("dp")
        for at, which in ((0, core), (half, 1 - core)):
            start = pl.multiple_of(which * half, LANES)
            total = sum_ref[:, at : at + half].astype(BF16)
            back_ref[:, pl.ds(start, half)] = total
            spare_ref[:, pl.ds(start, half)] = total[main:]


def project_back(grads_main, grads_spare, near, far, tile, *after):
    main, width = grads_main.shape
    spare = grads_spare.shape[0]
    half = near.shape[0]
    slots = main + spare
    return call(
        back_kernel,
        width // tile,
        by_columns(tile, grads_main, grads_spare, near, far),
        entire(bf16(slots, 2 * half), bf16(spare, 2 * half)),
        [pltpu.VMEM((slots, 2 * half), F32), pltpu.VMEM((slots, tile), BF16)],
        after,
        cost=BACK_COST,
    )


def place_kernel(back_ref, spare_ref, out_ref):
    out_ref[...] = spare_ref[...]


def with_spare(back, back_spare, *after):
    slots, hid = back.shape
    spare = back_spare.shape[0]
    last = pl.BlockSpec((spare, hid), lambda step: (slots // spare - 1, 0))
    ins = [(back, anywhere())] + entire(back_spare)
    return call(place_kernel, 1, ins, (bf16(slots, hid), last), (), after, {0: 0})


def local(hidden_saved, down_weight, route_device, replica_flag, gate_values, grad_out):
    count = lax.axis_size("expert")
    half = count // 2
    tok, top = route_device.shape
    width = grad_out.shape[1]
    cap = 5 * tok * top // (4 * count)
    main = 3 * tok * top // 4
    hidden = hidden_saved[0, 0]
    near = down_weight[0]
    slots = hidden.shape[0]
    tile = width // 2
    groups = [list(range(half)), list(range(half, count))]

    def to_half(rows):
        return lax.all_to_all(
            rows.reshape(half, cap, width), "expert", 0, 0, axis_index_groups=groups, tiled=True
        ).reshape(half * cap, width)

    far = swapped(near, "dp", 1)
    meta, spare_hidden = head(
        route_device.T, replica_flag.T, gate_values.T, hidden, slots - main, count
    )
    spare_hidden = swapped(spare_hidden, "expert", half)
    metas = lax.all_to_all(meta, "expert", 0, 0, tiled=True)
    size = count // 4
    turned_blocks = size == 4
    place_of = lambda plane, index: plane * size + index
    across = [(d, place_of(d // size ^ 1, d % size)) for d in range(count)]
    neighbour = lax.ppermute(grad_out, "expert", across)
    out_spare = project_spare(spare_hidden, near, far, tile)
    plans = plan(metas, cap, half, main, slots, turned_blocks)
    sel, gate, mix_mirror, plane_sel, plane_gate, mix_own = plans[:6]
    give_own, take_own, give_mirror, take_mirror = plans[6:]
    blocks = 4 if turned_blocks else 1
    packed_own = pack_plane(plane_sel, plane_gate, grad_out, neighbour, blocks, tile)
    if turned_blocks:
        ways = [[(d, d // size * size + (d % size ^ way)) for d in range(count)] for way in range(blocks)]
        arrived_own = [packed_own[0]]
        arrived_own += [lax.ppermute(packed_own[way], "expert", ways[way]) for way in range(1, blocks)]
    else:
        planes = [[place_of(plane, index) for index in range(size)] for plane in range(4)]
        rows = packed_own[0].reshape(size, 2 * cap, width)
        rows = lax.all_to_all(rows, "expert", 0, 0, axis_index_groups=planes, tiled=True)
        arrived_own = [rows.reshape(half * cap, width)]
    out_main, turned, far_turned = project(hidden, spare_hidden, near, far, tile, out_spare, packed_own[0])
    out_spare = swapped(out_spare, "expert", half)
    given_main = give_main(give_mirror, out_main, tile)
    mirror = swapped(touched(copied(grad_out, tile), out_main, sel), "expert", half)
    other_turned = swapped(far_turned, "dp", 1)
    given_mirror = give_rest(give_mirror, given_main, out_spare, tile, GIVE_COST)
    returned_mirror = to_half(given_mirror)
    packed_mirror = pack(sel, gate, mirror, tile, *arrived_own[1:])
    given_own = give(give_own, out_main, out_spare, tile, 0, packed_mirror)
    arrived_mirror = to_half(touched(packed_mirror, returned_mirror, given_own))
    part = swapped(combine(mix_mirror, returned_mirror, [], tile), "expert", half)
    arrived = (take_own, take_mirror, arrived_mirror, arrived_own)
    grads_spare = take(*arrived, main, slots - main, tile)
    returned_own = to_half(touched(given_own, part, grads_spare))
    grads_main = take(*arrived, 0, main, tile, grads_spare)
    other_main = swapped(grads_main, "dp", 1)
    grads_spare = swapped(grads_spare, "expert", half)
    other_spare = swapped(grads_spare, "dp", 1)
    layer_out = combine(mix_own, returned_own, [part], tile)
    back, back_spare = project_back(grads_main, grads_spare, near, far, tile)
    back_spare = swapped(back_spare, "expert", half)
    grad_weight = weight_grad(
        turned, other_turned, (grads_main, grads_spare), (other_main, other_spare), tile, back
    )
    grad_hidden = with_spare(back, back_spare, grad_weight)
    return (layer_out, grad_hidden[None, None], grad_weight[None])


def solution(mesh):
    in_specs = (
        P("dp", "expert", None, None),
        P("expert", "dp", None),
        P(("dp", "expert"), None),
        P(("dp", "expert"), None),
        P(("dp", "expert"), None),
        P(("dp", "expert"), None),
    )
    out_specs = (P(("dp", "expert"), None), P("dp", "expert", None, None), P("expert", "dp", None))
    return jax.shard_map(local, mesh=mesh, in_specs=in_specs, out_specs=out_specs, check_vma=False)
```

```python
import functools
import jax
import jax.numpy as jnp
from jax import lax
from jax.experimental import pallas as pl
from jax.experimental.pallas import tpu as pltpu
from jax.sharding import PartitionSpec as P

F32, BF16, I32 = jnp.float32, jnp.bfloat16, jnp.int32
LANES = 128
LONG = 4_000_000_000_000
GIVE_COST = 5_000_000_000
BACK_COST = 40_000_000_000
VMEM_LIMIT = 64 * 1024 * 1024 - 65536


def swapped(value, axis, distance):
    count = lax.axis_size(axis)
    pairs = [(source, (source + distance) % count) for source in range(count)]
    return lax.ppermute(value, axis, pairs)


def dot(left, right, left_dim=1, right_dim=0):
    contract = (((left_dim,), (right_dim,)), ((), ()))
    return lax.dot_general(left, right, contract, preferred_element_type=F32)


def iota(shape, dim):
    return lax.broadcasted_iota(I32, shape, dim).astype(F32)


def row_of(rows, cap, lanes):
    row = iota((rows, lanes), 0)
    group = jnp.floor((row + 0.5) * (1.0 / cap))
    return group, row - group * cap


def before_mask(size):
    return (iota((size, size), 0) < iota((size, size), 1)).astype(BF16)


def bf16(*shape):
    return jax.ShapeDtypeStruct(shape, BF16)


def f32(*shape):
    return jax.ShapeDtypeStruct(shape, F32)


def call(body, grid, ins, outs, scratch=(), after=(), alias=None, cost=0):
    single = not isinstance(outs, list)
    pairs = [outs] if single else outs
    specs = [spec for _, spec in pairs]
    shapes = [shape for shape, _ in pairs]
    count = len(ins)

    def kernel(*refs):
        body(*refs[:count], *refs[count + len(after) :])

    return pl.pallas_call(
        kernel,
        grid=(grid,),
        in_specs=[spec for _, spec in ins] + [anywhere()] * len(after),
        out_specs=specs[0] if single else specs,
        out_shape=shapes[0] if single else shapes,
        scratch_shapes=list(scratch),
        input_output_aliases=alias or {},
        compiler_params=pltpu.CompilerParams(vmem_limit_bytes=VMEM_LIMIT),
        cost_estimate=pl.CostEstimate(flops=cost, bytes_accessed=0, transcendentals=0),
    )(*[array for array, _ in ins], *after)


def anywhere():
    return pl.BlockSpec(memory_space=pl.ANY)


def whole(array):
    return pl.BlockSpec(array.shape, lambda step: (0,) * len(array.shape))


def columns(array, tile):
    return pl.BlockSpec((array.shape[0], tile), lambda step: (0, step))


def entire(*arrays):
    return [(array, whole(array)) for array in arrays]


def by_columns(tile, *arrays):
    return [(array, columns(array, tile)) for array in arrays]


def head_kernel(device_ref, flag_ref, gate_ref, hidden_ref, meta_ref, spare_ref):
    top = device_ref.shape[0]
    codes = (device_ref[...] * 2 + flag_ref[...]).astype(F32)
    count = meta_ref.shape[0]
    meta_ref[:, :top, :] = jnp.broadcast_to(codes[None], (count, *codes.shape))
    meta_ref[:, top:, :] = jnp.broadcast_to(gate_ref[...][None], (count, *codes.shape))
    spare_ref[...] = hidden_ref[...]


def head(devices, flags, gates, hidden, spare, count):
    top, tok = devices.shape
    slots, hid = hidden.shape
    last = pl.BlockSpec((spare, hid), lambda step: (slots // spare - 1, 0))
    outs = entire(f32(count, 2 * top, tok), bf16(spare, hid))
    return call(head_kernel, 1, entire(devices, flags, gates) + [(hidden, last)], outs)


def copy_kernel(source_ref, target_ref):
    target_ref[...] = source_ref[...]


def copied(array, tile, *after):
    ins, outs = by_columns(tile, array), by_columns(tile, bf16(*array.shape))[0]
    return call(copy_kernel, array.shape[1] // tile, ins, outs, (), after)


def touch_kernel(source_ref, target_ref):
    pass


def touched(array, *after):
    shape = jax.ShapeDtypeStruct(array.shape, array.dtype)
    return call(touch_kernel, 1, [(array, anywhere())], (shape, anywhere()), (), after, {0: 0})


def plan_rows(meta, cap, half, sel_ref, gate_ref, mix_ref):
    rows, tok = sel_ref.shape
    top = meta.shape[0] // 2
    me = lax.axis_index("expert")
    first = (lax.div(me, half) * half).astype(F32)
    dest = iota((LANES, tok), 0)
    inside = dest < half
    dest = dest + first
    hit = jnp.zeros((LANES, tok), F32)
    gate = jnp.zeros((LANES, tok), F32)
    for k in range(top):
        device = jnp.floor(meta[k : k + 1] * 0.5)
        named = (dest == device) & inside
        hit = jnp.where(named, 1.0, hit)
        gate = jnp.where(named, meta[top + k : top + k + 1], gate)
    place = dot(hit.astype(BF16), before_mask(tok))
    place = jnp.where(hit > 0.5, place, -1.0)
    group, at = row_of(rows, cap, LANES)
    spread = (iota((rows, LANES), 1) == group).astype(BF16)
    to_rows = lambda table: dot(spread, table.astype(BF16))
    chosen = jnp.where(to_rows(place) == at, 1.0, jnp.zeros((rows, tok), F32))
    high = gate.astype(BF16).astype(F32)
    mid = (gate - high).astype(BF16).astype(F32)
    low = gate - high - mid
    high, mid, low = to_rows(high), to_rows(mid), to_rows(low)
    scale = jnp.sum(chosen * (high + mid + low), axis=1, keepdims=True)
    sel_ref[...] = chosen.astype(BF16)
    gate_ref[...] = jnp.broadcast_to(scale, (rows, LANES))
    mix_ref[:tok] = (chosen * high).T.astype(BF16)
    mix_ref[tok:] = (chosen * mid).T.astype(BF16)


def packed_rows(sel_ref, gate_ref, tokens_ref, packed_ref):
    packed_ref[...] = (dot(sel_ref[...], tokens_ref[...]) * gate_ref[:, :1]).astype(BF16)


def pack(sel, gate, tokens, tile, *after):
    rows, width = sel.shape[0], tokens.shape[1]
    return call(
        packed_rows,
        width // tile,
        entire(sel, gate) + by_columns(tile, tokens),
        by_columns(tile, bf16(rows, width))[0],
        after=after,
        cost=LONG,
    )


def plan_plane(metas_ref, cap, turned, sel_ref, gate_ref):
    count, tops, tok = metas_ref.shape
    rows = sel_ref.shape[0]
    top = tops // 2
    size = count // 4
    me = lax.axis_index("expert")
    plane, mine = lax.div(me, size), lax.rem(me, size)
    index = lax.broadcasted_iota(I32, (LANES, tok), 0)
    inside = index < size
    dest = ((index ^ mine if turned else index) + plane * size).astype(F32)
    group, at = row_of(rows, cap, LANES)
    block = jnp.floor(group * 0.5)
    side = group - 2.0 * block
    scale = jnp.zeros((rows, 1), F32)
    for which, source in enumerate((me, (plane ^ 1) * size + mine)):
        meta = metas_ref[source]
        hit = jnp.zeros((LANES, tok), F32)
        gate = jnp.zeros((LANES, tok), F32)
        for k in range(top):
            named = (dest == jnp.floor(meta[k : k + 1] * 0.5)) & inside
            hit = jnp.where(named, 1.0, hit)
            gate = jnp.where(named, meta[top + k : top + k + 1], gate)
        place = dot(hit.astype(BF16), before_mask(tok))
        place = jnp.where(hit > 0.5, place + 1.0, 0.0)
        spread = ((iota((rows, LANES), 1) == block) & (side == 1.0 * which)).astype(BF16)
        to_rows = lambda table: dot(spread, table.astype(BF16))
        chosen = jnp.where(to_rows(place) == at + 1.0, 1.0, jnp.zeros((rows, tok), F32))
        high = gate.astype(BF16).astype(F32)
        mid = (gate - high).astype(BF16).astype(F32)
        low = gate - high - mid
        total = to_rows(high) + to_rows(mid) + to_rows(low)
        scale = scale + jnp.sum(chosen * total, axis=1, keepdims=True)
        sel_ref[:, which * tok : (which + 1) * tok] = chosen.astype(BF16)
    gate_ref[...] = jnp.broadcast_to(scale, (rows, LANES))


def plan_kernel(cap, half, main, turned, metas_ref, *refs):
    sel_ref, gate_ref, mix_ref, plane_sel, plane_gate, mix_own = refs[:6]
    give_own, take_plane, give_mirror, take_mirror = refs[6:10]
    spare_sel, spare_gate = refs[10:]
    count, tops, tok = metas_ref.shape
    top = tops // 2
    rows, slots = give_own.shape
    spare = slots - main
    size = count // 4
    me = lax.axis_index("expert")
    mirror = lax.rem(me + half, count)
    plan_plane(metas_ref, cap, turned, plane_sel, plane_gate)
    plan_rows(metas_ref[me], cap, half, spare_sel, spare_gate, mix_own)
    plan_rows(metas_ref[mirror], cap, half, sel_ref, gate_ref, mix_ref)

    mine, other = me.astype(F32), mirror.astype(F32)
    none = jnp.zeros((count, tok), F32)
    here, flag, clash = none, none, none
    for k in range(top):
        code = metas_ref[:, k, :]
        device = jnp.floor(code * 0.5)
        here = jnp.where(device == mine, 1.0, here)
        flag = jnp.where(device == mine, code - 2.0 * device, flag)
        clash = jnp.where(device == other, 1.0, clash)
    at_spare = here * flag * (1.0 - clash)
    at_main = here - at_spare
    before = before_mask(tok)
    ones = jnp.ones((tok, LANES), BF16)
    lower = (iota((count, count), 1) < iota((count, count), 0)).astype(BF16)

    def rank(flags):
        flags = flags.astype(BF16)
        return dot(flags, before) + dot(lower, dot(flags, ones).astype(BF16))

    rank_main, rank_spare = rank(at_main), rank(at_spare)
    slot = jnp.where((at_main > 0.5) & (rank_main < main), rank_main + 1.0, none)
    slot = jnp.where((at_spare > 0.5) & (rank_spare < spare), rank_spare + (main + 1.0), slot)
    place = jnp.where(here > 0.5, dot(here.astype(BF16), before), -1.0).astype(BF16)
    tens = jnp.floor(slot * (1.0 / 32.0))
    units = (slot - tens * 32.0).astype(BF16)
    tens = tens.astype(BF16)
    group, _ = row_of(rows, cap, count)
    _, at = row_of(rows, cap, tok)

    def numbers(sources):
        spread = (iota((rows, count), 1) == sources).astype(BF16)
        chosen = dot(spread, place) == at
        number = dot(spread, tens) * 32.0 + dot(spread, units)
        return jnp.sum(jnp.where(chosen, number, 0.0), axis=1, keepdims=True)

    def give_to(ref, number):
        ref[...] = (iota((rows, slots), 1) + 1.0 == number).astype(BF16)

    def take_to(ref, number):
        number = jnp.broadcast_to(number, (rows, LANES)).T[0:1]
        ref[...] = (iota((slots, rows), 0) + 1.0 == number).astype(BF16)

    start = lax.div(me, half) * half
    give_to(give_own, numbers(group + start.astype(F32)))
    number = numbers(group + lax.rem(start + half, count).astype(F32))
    give_to(give_mirror, number)
    take_to(take_mirror, number)
    block = jnp.floor(group * 0.5)
    side = group - 2.0 * block
    plane = lax.div(me, size)
    holder = block.astype(I32)
    holder = (holder ^ lax.rem(me, size) if turned else holder).astype(F32)
    start = jnp.where(side == 0.0, (plane * size).astype(F32), ((plane ^ 1) * size).astype(F32))
    take_to(take_plane, numbers(holder + start))


def plan(metas, cap, half, main, slots, turned):
    tok = metas.shape[2]
    rows = half * cap
    outs = [bf16(rows, tok), f32(rows, LANES), bf16(2 * tok, rows)]
    outs += [bf16(rows, 2 * tok), f32(rows, LANES), bf16(2 * tok, rows)]
    outs += [bf16(rows, slots), bf16(slots, rows)] * 2
    scratch = [pltpu.VMEM((rows, tok), BF16), pltpu.VMEM((rows, LANES), F32)]
    body = functools.partial(plan_kernel, cap, half, main, turned)
    return call(body, 1, entire(metas), entire(*outs), scratch)


def pack_plane_kernel(sel_ref, gate_ref, own_ref, neighbour_ref, *outs):
    tok = own_ref.shape[0]
    packed = dot(sel_ref[:, :tok], own_ref[...]) + dot(sel_ref[:, tok:], neighbour_ref[...])
    packed = (packed * gate_ref[:, :1]).astype(BF16)
    rows = outs[0].shape[0]
    for index, out_ref in enumerate(outs):
        out_ref[...] = packed[index * rows : (index + 1) * rows]


def pack_plane(sel, gate, own, neighbour, blocks, tile, *after):
    width = own.shape[1]
    shapes = [bf16(sel.shape[0] // blocks, width)] * blocks
    ins = entire(sel, gate) + by_columns(tile, own, neighbour)
    return call(pack_plane_kernel, width // tile, ins, by_columns(tile, *shapes), (), after)


def side_by_side(source, target_ref):
    half = target_ref.shape[1] // 2
    core = lax.axis_index("dp")
    for at, which in ((0, core), (half, 1 - core)):
        start = pl.multiple_of(which * half, LANES)
        target_ref[:, at : at + half] = source[: target_ref.shape[0], pl.ds(start, half)]


def projected(stack_ref, near_ref, far_ref, out_ref):
    half = near_ref.shape[0]
    total = dot(stack_ref[:, :half], near_ref[...]) + dot(stack_ref[:, half:], far_ref[...])
    out_ref[...] = total.astype(BF16)


def project_spare_kernel(spare_ref, near_ref, far_ref, out_ref, stack_ref):
    @pl.when(pl.program_id(0) == 0)
    def _():
        side_by_side(spare_ref, stack_ref)

    projected(stack_ref, near_ref, far_ref, out_ref)


def project_spare(spare_hidden, near, far, tile, *after):
    width = near.shape[1]
    return call(
        project_spare_kernel,
        width // tile,
        entire(spare_hidden) + by_columns(tile, near, far),
        by_columns(tile, bf16(spare_hidden.shape[0], width))[0],
        [pltpu.VMEM(spare_hidden.shape, BF16)],
        after,
    )


def project_kernel(hidden_ref, spare_ref, near_ref, far_ref, out_ref, near_turned, far_turned, stack_ref, side_ref):
    main, half = out_ref.shape[0], near_ref.shape[0]

    @pl.when(pl.program_id(0) == 0)
    def _():
        side_by_side(hidden_ref, stack_ref)
        side_by_side(spare_ref, side_ref)
        for at, turned_ref in ((0, near_turned), (half, far_turned)):
            turned_ref[:, :main] = stack_ref[:, at : at + half].T
            turned_ref[:, main:] = side_ref[:, at : at + half].T

    projected(stack_ref, near_ref, far_ref, out_ref)


def project(hidden, spare_hidden, near, far, tile, *after):
    half, width = near.shape
    spare = spare_hidden.shape[0]
    slots, hid = hidden.shape
    turned = [bf16(half, slots), bf16(half, slots)]
    return call(
        project_kernel,
        width // tile,
        entire(hidden, spare_hidden) + by_columns(tile, near, far),
        by_columns(tile, bf16(slots - spare, width)) + entire(*turned),
        [pltpu.VMEM((slots - spare, hid), BF16), pltpu.VMEM((spare, hid), BF16)],
        after,
    )


def give_kernel(slot_ref, main_ref, spare_ref, out_ref):
    main = main_ref.shape[0]
    packed = dot(slot_ref[:, :main], main_ref[...]) + dot(slot_ref[:, main:], spare_ref[...])
    out_ref[...] = packed.astype(BF16)


def give(slot, out_main, out_spare, tile, cost, *after):
    rows, width = slot.shape[0], out_main.shape[1]
    return call(
        give_kernel,
        width // tile,
        entire(slot) + by_columns(tile, out_main, out_spare),
        by_columns(tile, bf16(rows, width))[0],
        after=after,
        cost=cost,
    )


def give_main_kernel(slot_ref, main_ref, out_ref):
    out_ref[...] = dot(slot_ref[:, : main_ref.shape[0]], main_ref[...]).astype(BF16)


def give_main(slot, out_main, tile):
    rows, width = slot.shape[0], out_main.shape[1]
    return call(
        give_main_kernel,
        width // tile,
        entire(slot) + by_columns(tile, out_main),
        by_columns(tile, bf16(rows, width))[0],
    )


def give_rest_kernel(slot_ref, given_ref, spare_ref, out_ref):
    rest = dot(slot_ref[:, slot_ref.shape[1] - spare_ref.shape[0] :], spare_ref[...])
    out_ref[...] = given_ref[...] + rest.astype(BF16)


def give_rest(slot, given, out_spare, tile, cost):
    return call(
        give_rest_kernel,
        given.shape[1] // tile,
        entire(slot) + by_columns(tile, given, out_spare),
        by_columns(tile, bf16(*given.shape))[0],
        cost=cost,
    )


def take_kernel(first, own_slot, mirror_slot, mirror_ref, *rest):
    blocks, (out_ref, stack_ref) = rest[:-2], rest[-2:]
    size = blocks[0].shape[0]
    for index, block_ref in enumerate(blocks):
        stack_ref[index * size : (index + 1) * size] = block_ref[...]
    rows = pl.ds(first, out_ref.shape[0])
    total = dot(own_slot[rows, :], stack_ref[...]) + dot(mirror_slot[rows, :], mirror_ref[...])
    out_ref[...] = total.astype(BF16)


def take(own_slot, mirror_slot, mirror, own, first, count, tile, *after):
    rows, width = mirror.shape
    return call(
        functools.partial(take_kernel, first),
        width // tile,
        entire(own_slot, mirror_slot) + by_columns(tile, mirror, *own),
        by_columns(tile, bf16(count, width))[0],
        [pltpu.VMEM((rows, tile), BF16)],
        after,
    )


def mixed(mix_ref, rows_ref):
    both = dot(mix_ref[...], rows_ref[...])
    tok = both.shape[0] // 2
    return both[:tok] + both[tok:]


def part_kernel(mix_ref, rows_ref, part_ref):
    part_ref[...] = mixed(mix_ref, rows_ref).astype(BF16)


def total_kernel(mix_ref, rows_ref, other_ref, total_ref):
    total_ref[...] = (mixed(mix_ref, rows_ref) + other_ref[...].astype(F32)).astype(BF16)


def combine(mix, rows, others, tile, *after):
    width = rows.shape[1]
    return call(
        total_kernel if others else part_kernel,
        width // tile,
        entire(mix) + by_columns(tile, rows, *others),
        by_columns(tile, bf16(mix.shape[0] // 2, width))[0],
        after=after,
    )


def stack_grads(main_ref, spare_ref, grads_ref):
    main = main_ref.shape[0]
    grads_ref[:main] = main_ref[...]
    grads_ref[main:] = spare_ref[...]


def weight_kernel(turned, other_turned, main_ref, spare_ref, other_main, other_spare, out_ref, grads_ref):
    stack_grads(main_ref, spare_ref, grads_ref)
    total = dot(turned[...], grads_ref[...])
    stack_grads(other_main, other_spare, grads_ref)
    out_ref[...] = (total + dot(other_turned[...], grads_ref[...])).astype(BF16)


def weight_grad(turned, other_turned, grads, other_grads, tile, *after):
    half, slots = turned.shape
    width = grads[0].shape[1]
    return call(
        weight_kernel,
        width // tile,
        entire(turned, other_turned) + by_columns(tile, *grads, *other_grads),
        by_columns(tile, bf16(half, width))[0],
        [pltpu.VMEM((slots, tile), BF16)],
        after,
    )


def back_kernel(main_ref, grad_ref, near_ref, far_ref, back_ref, spare_ref, sum_ref, grads_ref):
    step = pl.program_id(0)
    half = near_ref.shape[0]
    main = main_ref.shape[0]

    @pl.when(step == 0)
    def _():
        sum_ref[...] = jnp.zeros_like(sum_ref)

    stack_grads(main_ref, grad_ref, grads_ref)
    sum_ref[:, :half] += dot(grads_ref[...], near_ref[...], 1, 1)
    sum_ref[:, half:] += dot(grads_ref[...], far_ref[...], 1, 1)

    @pl.when(step == pl.num_programs(0) - 1)
    def _():
        core = lax.axis_index("dp")
        for at, which in ((0, core), (half, 1 - core)):
            start = pl.multiple_of(which * half, LANES)
            total = sum_ref[:, at : at + half].astype(BF16)
            back_ref[:, pl.ds(start, half)] = total
            spare_ref[:, pl.ds(start, half)] = total[main:]


def project_back(grads_main, grads_spare, near, far, tile, *after):
    main, width = grads_main.shape
    spare = grads_spare.shape[0]
    half = near.shape[0]
    slots = main + spare
    return call(
        back_kernel,
        width // tile,
        by_columns(tile, grads_main, grads_spare, near, far),
        entire(bf16(slots, 2 * half), bf16(spare, 2 * half)),
        [pltpu.VMEM((slots, 2 * half), F32), pltpu.VMEM((slots, tile), BF16)],
        after,
        cost=BACK_COST,
    )


def place_kernel(back_ref, spare_ref, out_ref):
    out_ref[...] = spare_ref[...]


def with_spare(back, back_spare, *after):
    slots, hid = back.shape
    spare = back_spare.shape[0]
    last = pl.BlockSpec((spare, hid), lambda step: (slots // spare - 1, 0))
    ins = [(back, anywhere())] + entire(back_spare)
    return call(place_kernel, 1, ins, (bf16(slots, hid), last), (), after, {0: 0})


def local(hidden_saved, down_weight, route_device, replica_flag, gate_values, grad_out):
    count = lax.axis_size("expert")
    half = count // 2
    tok, top = route_device.shape
    width = grad_out.shape[1]
    cap = 5 * tok * top // (4 * count)
    main = 3 * tok * top // 4
    hidden = hidden_saved[0, 0]
    near = down_weight[0]
    slots = hidden.shape[0]
    tile = width // 2
    groups = [list(range(half)), list(range(half, count))]

    def to_half(rows):
        return lax.all_to_all(
            rows.reshape(half, cap, width), "expert", 0, 0, axis_index_groups=groups, tiled=True
        ).reshape(half * cap, width)

    far = swapped(near, "dp", 1)
    meta, spare_hidden = head(
        route_device.T, replica_flag.T, gate_values.T, hidden, slots - main, count
    )
    spare_hidden = swapped(spare_hidden, "expert", half)
    metas = lax.all_to_all(meta, "expert", 0, 0, tiled=True)
    size = count // 4
    turned_blocks = size == 4
    place_of = lambda plane, index: plane * size + index
    across = [(d, place_of(d // size ^ 1, d % size)) for d in range(count)]
    neighbour = lax.ppermute(touched(copied(grad_out, tile), spare_hidden, metas), "expert", across)
    out_spare = project_spare(spare_hidden, near, far, tile)
    plans = plan(metas, cap, half, main, slots, turned_blocks)
    sel, gate, mix_mirror, plane_sel, plane_gate, mix_own = plans[:6]
    give_own, take_own, give_mirror, take_mirror = plans[6:]
    blocks = 4 if turned_blocks else 1
    out_main, turned, far_turned = project(hidden, spare_hidden, near, far, tile, out_spare)
    given_main = give_main(give_mirror, out_main, tile)
    packed_own = pack_plane(plane_sel, plane_gate, grad_out, neighbour, blocks, tile, given_main)
    if turned_blocks:
        ways = [[(d, d // size * size + (d % size ^ way)) for d in range(count)] for way in range(blocks)]
        arrived_own = [packed_own[0]]
        arrived_own += [lax.ppermute(packed_own[way], "expert", ways[way]) for way in range(1, blocks)]
    else:
        planes = [[place_of(plane, index) for index in range(size)] for plane in range(4)]
        rows = packed_own[0].reshape(size, 2 * cap, width)
        rows = lax.all_to_all(rows, "expert", 0, 0, axis_index_groups=planes, tiled=True)
        arrived_own = [rows.reshape(half * cap, width)]
    out_spare = swapped(out_spare, "expert", half)
    mirror = swapped(touched(copied(grad_out, tile, meta), out_main, packed_own[0]), "expert", half)
    other_turned = swapped(far_turned, "dp", 1)
    given_mirror = give_rest(give_mirror, given_main, out_spare, tile, GIVE_COST)
    returned_mirror = to_half(given_mirror)
    packed_mirror = pack(sel, gate, mirror, tile, *arrived_own[1:])
    given_own = give(give_own, out_main, out_spare, tile, 0, packed_mirror)
    arrived_mirror = to_half(touched(packed_mirror, returned_mirror, given_own))
    part = swapped(combine(mix_mirror, returned_mirror, [], tile), "expert", half)
    arrived = (take_own, take_mirror, arrived_mirror, arrived_own)
    grads_spare = take(*arrived, main, slots - main, tile)
    returned_own = to_half(touched(given_own, part, grads_spare))
    grads_main = take(*arrived, 0, main, tile, grads_spare)
    other_main = swapped(grads_main, "dp", 1)
    grads_spare = swapped(grads_spare, "expert", half)
    other_spare = swapped(grads_spare, "dp", 1)
    layer_out = combine(mix_own, returned_own, [part], tile)
    back, back_spare = project_back(grads_main, grads_spare, near, far, tile)
    back_spare = swapped(back_spare, "expert", half)
    grad_weight = weight_grad(
        turned, other_turned, (grads_main, grads_spare), (other_main, other_spare), tile, back
    )
    grad_hidden = with_spare(back, back_spare, grad_weight)
    return (layer_out, grad_hidden[None, None], grad_weight[None])


def solution(mesh):
    in_specs = (
        P("dp", "expert", None, None),
        P("expert", "dp", None),
        P(("dp", "expert"), None),
        P(("dp", "expert"), None),
        P(("dp", "expert"), None),
        P(("dp", "expert"), None),
    )
    out_specs = (P(("dp", "expert"), None), P("dp", "expert", None, None), P("expert", "dp", None))
    return jax.shard_map(local, mesh=mesh, in_specs=in_specs, out_specs=out_specs, check_vma=False)
```

```python
import functools
import jax
import jax.numpy as jnp
from jax import lax
from jax.experimental import pallas as pl
from jax.experimental.pallas import tpu as pltpu
from jax.sharding import PartitionSpec as P

F32, BF16, I32 = jnp.float32, jnp.bfloat16, jnp.int32
LANES = 128
LONG = 4_000_000_000_000
GIVE_COST = 5_000_000_000
BACK_COST = 40_000_000_000
VMEM_LIMIT = 64 * 1024 * 1024 - 65536


def swapped(value, axis, distance):
    count = lax.axis_size(axis)
    pairs = [(source, (source + distance) % count) for source in range(count)]
    return lax.ppermute(value, axis, pairs)


def dot(left, right, left_dim=1, right_dim=0):
    contract = (((left_dim,), (right_dim,)), ((), ()))
    return lax.dot_general(left, right, contract, preferred_element_type=F32)


def iota(shape, dim):
    return lax.broadcasted_iota(I32, shape, dim).astype(F32)


def row_of(rows, cap, lanes):
    row = iota((rows, lanes), 0)
    group = jnp.floor((row + 0.5) * (1.0 / cap))
    return group, row - group * cap


def before_mask(size):
    return (iota((size, size), 0) < iota((size, size), 1)).astype(BF16)


def bf16(*shape):
    return jax.ShapeDtypeStruct(shape, BF16)


def f32(*shape):
    return jax.ShapeDtypeStruct(shape, F32)


def call(body, grid, ins, outs, scratch=(), after=(), alias=None, cost=0):
    single = not isinstance(outs, list)
    pairs = [outs] if single else outs
    specs = [spec for _, spec in pairs]
    shapes = [shape for shape, _ in pairs]
    count = len(ins)

    def kernel(*refs):
        body(*refs[:count], *refs[count + len(after) :])

    return pl.pallas_call(
        kernel,
        grid=(grid,),
        in_specs=[spec for _, spec in ins] + [anywhere()] * len(after),
        out_specs=specs[0] if single else specs,
        out_shape=shapes[0] if single else shapes,
        scratch_shapes=list(scratch),
        input_output_aliases=alias or {},
        compiler_params=pltpu.CompilerParams(vmem_limit_bytes=VMEM_LIMIT),
        cost_estimate=pl.CostEstimate(flops=cost, bytes_accessed=0, transcendentals=0),
    )(*[array for array, _ in ins], *after)


def anywhere():
    return pl.BlockSpec(memory_space=pl.ANY)


def whole(array):
    return pl.BlockSpec(array.shape, lambda step: (0,) * len(array.shape))


def columns(array, tile):
    return pl.BlockSpec((array.shape[0], tile), lambda step: (0, step))


def entire(*arrays):
    return [(array, whole(array)) for array in arrays]


def by_columns(tile, *arrays):
    return [(array, columns(array, tile)) for array in arrays]


def head_kernel(device_ref, flag_ref, gate_ref, hidden_ref, meta_ref, spare_ref):
    top = device_ref.shape[0]
    codes = (device_ref[...] * 2 + flag_ref[...]).astype(F32)
    count = meta_ref.shape[0]
    meta_ref[:, :top, :] = jnp.broadcast_to(codes[None], (count, *codes.shape))
    meta_ref[:, top:, :] = jnp.broadcast_to(gate_ref[...][None], (count, *codes.shape))
    spare_ref[...] = hidden_ref[...]


def head(devices, flags, gates, hidden, spare, count):
    top, tok = devices.shape
    slots, hid = hidden.shape
    last = pl.BlockSpec((spare, hid), lambda step: (slots // spare - 1, 0))
    outs = entire(f32(count, 2 * top, tok), bf16(spare, hid))
    return call(head_kernel, 1, entire(devices, flags, gates) + [(hidden, last)], outs)


def copy_kernel(source_ref, target_ref):
    target_ref[...] = source_ref[...]


def copied(array, tile, *after):
    ins, outs = by_columns(tile, array), by_columns(tile, bf16(*array.shape))[0]
    return call(copy_kernel, array.shape[1] // tile, ins, outs, (), after)


def touch_kernel(source_ref, target_ref):
    pass


def touched(array, *after):
    shape = jax.ShapeDtypeStruct(array.shape, array.dtype)
    return call(touch_kernel, 1, [(array, anywhere())], (shape, anywhere()), (), after, {0: 0})


def plan_rows(meta, cap, half, sel_ref, gate_ref, mix_ref):
    rows, tok = sel_ref.shape
    top = meta.shape[0] // 2
    me = lax.axis_index("expert")
    first = (lax.div(me, half) * half).astype(F32)
    dest = iota((LANES, tok), 0)
    inside = dest < half
    dest = dest + first
    hit = jnp.zeros((LANES, tok), F32)
    gate = jnp.zeros((LANES, tok), F32)
    for k in range(top):
        device = jnp.floor(meta[k : k + 1] * 0.5)
        named = (dest == device) & inside
        hit = jnp.where(named, 1.0, hit)
        gate = jnp.where(named, meta[top + k : top + k + 1], gate)
    place = dot(hit.astype(BF16), before_mask(tok))
    place = jnp.where(hit > 0.5, place, -1.0)
    group, at = row_of(rows, cap, LANES)
    spread = (iota((rows, LANES), 1) == group).astype(BF16)
    to_rows = lambda table: dot(spread, table.astype(BF16))
    chosen = jnp.where(to_rows(place) == at, 1.0, jnp.zeros((rows, tok), F32))
    high = gate.astype(BF16).astype(F32)
    mid = (gate - high).astype(BF16).astype(F32)
    low = gate - high - mid
    high, mid, low = to_rows(high), to_rows(mid), to_rows(low)
    scale = jnp.sum(chosen * (high + mid + low), axis=1, keepdims=True)
    sel_ref[...] = chosen.astype(BF16)
    gate_ref[...] = jnp.broadcast_to(scale, (rows, LANES))
    mix_ref[:tok] = (chosen * high).T.astype(BF16)
    mix_ref[tok:] = (chosen * mid).T.astype(BF16)


def packed_rows(sel_ref, gate_ref, tokens_ref, packed_ref):
    packed_ref[...] = (dot(sel_ref[...], tokens_ref[...]) * gate_ref[:, :1]).astype(BF16)


def pack(sel, gate, tokens, tile, *after):
    rows, width = sel.shape[0], tokens.shape[1]
    return call(
        packed_rows,
        width // tile,
        entire(sel, gate) + by_columns(tile, tokens),
        by_columns(tile, bf16(rows, width))[0],
        after=after,
        cost=LONG,
    )


def plan_plane(metas_ref, cap, turned, sel_ref, gate_ref):
    count, tops, tok = metas_ref.shape
    rows = sel_ref.shape[0]
    top = tops // 2
    size = count // 4
    me = lax.axis_index("expert")
    plane, mine = lax.div(me, size), lax.rem(me, size)
    index = lax.broadcasted_iota(I32, (LANES, tok), 0)
    inside = index < size
    dest = ((index ^ mine if turned else index) + plane * size).astype(F32)
    group, at = row_of(rows, cap, LANES)
    block = jnp.floor(group * 0.5)
    side = group - 2.0 * block
    scale = jnp.zeros((rows, 1), F32)
    for which, source in enumerate((me, (plane ^ 1) * size + mine)):
        meta = metas_ref[source]
        hit = jnp.zeros((LANES, tok), F32)
        gate = jnp.zeros((LANES, tok), F32)
        for k in range(top):
            named = (dest == jnp.floor(meta[k : k + 1] * 0.5)) & inside
            hit = jnp.where(named, 1.0, hit)
            gate = jnp.where(named, meta[top + k : top + k + 1], gate)
        place = dot(hit.astype(BF16), before_mask(tok))
        place = jnp.where(hit > 0.5, place + 1.0, 0.0)
        spread = ((iota((rows, LANES), 1) == block) & (side == 1.0 * which)).astype(BF16)
        to_rows = lambda table: dot(spread, table.astype(BF16))
        chosen = jnp.where(to_rows(place) == at + 1.0, 1.0, jnp.zeros((rows, tok), F32))
        high = gate.astype(BF16).astype(F32)
        mid = (gate - high).astype(BF16).astype(F32)
        low = gate - high - mid
        total = to_rows(high) + to_rows(mid) + to_rows(low)
        scale = scale + jnp.sum(chosen * total, axis=1, keepdims=True)
        sel_ref[:, which * tok : (which + 1) * tok] = chosen.astype(BF16)
    gate_ref[...] = jnp.broadcast_to(scale, (rows, LANES))


def plan_kernel(cap, half, main, turned, metas_ref, *refs):
    sel_ref, gate_ref, mix_ref, plane_sel, plane_gate, mix_own = refs[:6]
    give_own, take_plane, give_mirror, take_mirror = refs[6:10]
    spare_sel, spare_gate = refs[10:]
    count, tops, tok = metas_ref.shape
    top = tops // 2
    rows, slots = give_own.shape
    spare = slots - main
    size = count // 4
    me = lax.axis_index("expert")
    mirror = lax.rem(me + half, count)
    plan_plane(metas_ref, cap, turned, plane_sel, plane_gate)
    plan_rows(metas_ref[me], cap, half, spare_sel, spare_gate, mix_own)
    plan_rows(metas_ref[mirror], cap, half, sel_ref, gate_ref, mix_ref)

    mine, other = me.astype(F32), mirror.astype(F32)
    none = jnp.zeros((count, tok), F32)
    here, flag, clash = none, none, none
    for k in range(top):
        code = metas_ref[:, k, :]
        device = jnp.floor(code * 0.5)
        here = jnp.where(device == mine, 1.0, here)
        flag = jnp.where(device == mine, code - 2.0 * device, flag)
        clash = jnp.where(device == other, 1.0, clash)
    at_spare = here * flag * (1.0 - clash)
    at_main = here - at_spare
    before = before_mask(tok)
    ones = jnp.ones((tok, LANES), BF16)
    lower = (iota((count, count), 1) < iota((count, count), 0)).astype(BF16)

    def rank(flags):
        flags = flags.astype(BF16)
        return dot(flags, before) + dot(lower, dot(flags, ones).astype(BF16))

    rank_main, rank_spare = rank(at_main), rank(at_spare)
    slot = jnp.where((at_main > 0.5) & (rank_main < main), rank_main + 1.0, none)
    slot = jnp.where((at_spare > 0.5) & (rank_spare < spare), rank_spare + (main + 1.0), slot)
    place = jnp.where(here > 0.5, dot(here.astype(BF16), before), -1.0).astype(BF16)
    tens = jnp.floor(slot * (1.0 / 32.0))
    units = (slot - tens * 32.0).astype(BF16)
    tens = tens.astype(BF16)
    group, _ = row_of(rows, cap, count)
    _, at = row_of(rows, cap, tok)

    def numbers(sources):
        spread = (iota((rows, count), 1) == sources).astype(BF16)
        chosen = dot(spread, place) == at
        number = dot(spread, tens) * 32.0 + dot(spread, units)
        return jnp.sum(jnp.where(chosen, number, 0.0), axis=1, keepdims=True)

    def give_to(ref, number):
        ref[...] = (iota((rows, slots), 1) + 1.0 == number).astype(BF16)

    def take_to(ref, number):
        number = jnp.broadcast_to(number, (rows, LANES)).T[0:1]
        ref[...] = (iota((slots, rows), 0) + 1.0 == number).astype(BF16)

    start = lax.div(me, half) * half
    give_to(give_own, numbers(group + start.astype(F32)))
    number = numbers(group + lax.rem(start + half, count).astype(F32))
    give_to(give_mirror, number)
    take_to(take_mirror, number)
    block = jnp.floor(group * 0.5)
    side = group - 2.0 * block
    plane = lax.div(me, size)
    holder = block.astype(I32)
    holder = (holder ^ lax.rem(me, size) if turned else holder).astype(F32)
    start = jnp.where(side == 0.0, (plane * size).astype(F32), ((plane ^ 1) * size).astype(F32))
    take_to(take_plane, numbers(holder + start))


def plan(metas, cap, half, main, slots, turned):
    tok = metas.shape[2]
    rows = half * cap
    outs = [bf16(rows, tok), f32(rows, LANES), bf16(2 * tok, rows)]
    outs += [bf16(rows, 2 * tok), f32(rows, LANES), bf16(2 * tok, rows)]
    outs += [bf16(rows, slots), bf16(slots, rows)] * 2
    scratch = [pltpu.VMEM((rows, tok), BF16), pltpu.VMEM((rows, LANES), F32)]
    body = functools.partial(plan_kernel, cap, half, main, turned)
    return call(body, 1, entire(metas), entire(*outs), scratch)


def pack_plane_kernel(sel_ref, gate_ref, own_ref, neighbour_ref, *outs):
    tok = own_ref.shape[0]
    packed = dot(sel_ref[:, :tok], own_ref[...]) + dot(sel_ref[:, tok:], neighbour_ref[...])
    packed = (packed * gate_ref[:, :1]).astype(BF16)
    rows = outs[0].shape[0]
    for index, out_ref in enumerate(outs):
        out_ref[...] = packed[index * rows : (index + 1) * rows]


def pack_plane(sel, gate, own, neighbour, blocks, tile, *after):
    width = own.shape[1]
    shapes = [bf16(sel.shape[0] // blocks, width)] * blocks
    ins = entire(sel, gate) + by_columns(tile, own, neighbour)
    return call(pack_plane_kernel, width // tile, ins, by_columns(tile, *shapes), (), after)


def side_by_side(source, target_ref):
    half = target_ref.shape[1] // 2
    core = lax.axis_index("dp")
    for at, which in ((0, core), (half, 1 - core)):
        start = pl.multiple_of(which * half, LANES)
        target_ref[:, at : at + half] = source[: target_ref.shape[0], pl.ds(start, half)]


def projected(stack_ref, near_ref, far_ref, out_ref):
    half = near_ref.shape[0]
    total = dot(stack_ref[:, :half], near_ref[...]) + dot(stack_ref[:, half:], far_ref[...])
    out_ref[...] = total.astype(BF16)


def project_spare_kernel(spare_ref, near_ref, far_ref, out_ref, stack_ref):
    @pl.when(pl.program_id(0) == 0)
    def _():
        side_by_side(spare_ref, stack_ref)

    projected(stack_ref, near_ref, far_ref, out_ref)


def project_spare(spare_hidden, near, far, tile, *after):
    width = near.shape[1]
    return call(
        project_spare_kernel,
        width // tile,
        entire(spare_hidden) + by_columns(tile, near, far),
        by_columns(tile, bf16(spare_hidden.shape[0], width))[0],
        [pltpu.VMEM(spare_hidden.shape, BF16)],
        after,
    )


def project_kernel(hidden_ref, spare_ref, near_ref, far_ref, out_ref, near_turned, far_turned, stack_ref, side_ref):
    main, half = out_ref.shape[0], near_ref.shape[0]

    @pl.when(pl.program_id(0) == 0)
    def _():
        side_by_side(hidden_ref, stack_ref)
        side_by_side(spare_ref, side_ref)
        for at, turned_ref in ((0, near_turned), (half, far_turned)):
            turned_ref[:, :main] = stack_ref[:, at : at + half].T
            turned_ref[:, main:] = side_ref[:, at : at + half].T

    projected(stack_ref, near_ref, far_ref, out_ref)


def project(hidden, spare_hidden, near, far, tile, *after):
    half, width = near.shape
    spare = spare_hidden.shape[0]
    slots, hid = hidden.shape
    turned = [bf16(half, slots), bf16(half, slots)]
    return call(
        project_kernel,
        width // tile,
        entire(hidden, spare_hidden) + by_columns(tile, near, far),
        by_columns(tile, bf16(slots - spare, width)) + entire(*turned),
        [pltpu.VMEM((slots - spare, hid), BF16), pltpu.VMEM((spare, hid), BF16)],
        after,
    )


def give_kernel(slot_ref, main_ref, spare_ref, out_ref):
    main = main_ref.shape[0]
    packed = dot(slot_ref[:, :main], main_ref[...]) + dot(slot_ref[:, main:], spare_ref[...])
    out_ref[...] = packed.astype(BF16)


def give(slot, out_main, out_spare, tile, cost, *after):
    rows, width = slot.shape[0], out_main.shape[1]
    return call(
        give_kernel,
        width // tile,
        entire(slot) + by_columns(tile, out_main, out_spare),
        by_columns(tile, bf16(rows, width))[0],
        after=after,
        cost=cost,
    )


def give_main_kernel(slot_ref, main_ref, out_ref):
    out_ref[...] = dot(slot_ref[:, : main_ref.shape[0]], main_ref[...]).astype(BF16)


def give_main(slot, out_main, tile):
    rows, width = slot.shape[0], out_main.shape[1]
    return call(
        give_main_kernel,
        width // tile,
        entire(slot) + by_columns(tile, out_main),
        by_columns(tile, bf16(rows, width))[0],
    )


def give_rest_kernel(slot_ref, given_ref, spare_ref, out_ref):
    rest = dot(slot_ref[:, slot_ref.shape[1] - spare_ref.shape[0] :], spare_ref[...])
    out_ref[...] = given_ref[...] + rest.astype(BF16)


def give_rest(slot, given, out_spare, tile, cost):
    return call(
        give_rest_kernel,
        given.shape[1] // tile,
        entire(slot) + by_columns(tile, given, out_spare),
        by_columns(tile, bf16(*given.shape))[0],
        cost=cost,
    )


def take_kernel(first, own_slot, mirror_slot, mirror_ref, *rest):
    blocks, (out_ref, stack_ref) = rest[:-2], rest[-2:]
    size = blocks[0].shape[0]
    for index, block_ref in enumerate(blocks):
        stack_ref[index * size : (index + 1) * size] = block_ref[...]
    rows = pl.ds(first, out_ref.shape[0])
    total = dot(own_slot[rows, :], stack_ref[...]) + dot(mirror_slot[rows, :], mirror_ref[...])
    out_ref[...] = total.astype(BF16)


def take(own_slot, mirror_slot, mirror, own, first, count, tile, *after):
    rows, width = mirror.shape
    return call(
        functools.partial(take_kernel, first),
        width // tile,
        entire(own_slot, mirror_slot) + by_columns(tile, mirror, *own),
        by_columns(tile, bf16(count, width))[0],
        [pltpu.VMEM((rows, tile), BF16)],
        after,
    )


def mixed(mix_ref, rows_ref):
    both = dot(mix_ref[...], rows_ref[...])
    tok = both.shape[0] // 2
    return both[:tok] + both[tok:]


def part_kernel(mix_ref, rows_ref, part_ref):
    part_ref[...] = mixed(mix_ref, rows_ref).astype(BF16)


def total_kernel(mix_ref, rows_ref, other_ref, total_ref):
    total_ref[...] = (mixed(mix_ref, rows_ref) + other_ref[...].astype(F32)).astype(BF16)


def combine(mix, rows, others, tile, *after):
    width = rows.shape[1]
    return call(
        total_kernel if others else part_kernel,
        width // tile,
        entire(mix) + by_columns(tile, rows, *others),
        by_columns(tile, bf16(mix.shape[0] // 2, width))[0],
        after=after,
    )


def stack_grads(main_ref, spare_ref, grads_ref):
    main = main_ref.shape[0]
    grads_ref[:main] = main_ref[...]
    grads_ref[main:] = spare_ref[...]


def weight_kernel(turned, other_turned, main_ref, spare_ref, other_main, other_spare, out_ref, grads_ref):
    stack_grads(main_ref, spare_ref, grads_ref)
    total = dot(turned[...], grads_ref[...])
    stack_grads(other_main, other_spare, grads_ref)
    out_ref[...] = (total + dot(other_turned[...], grads_ref[...])).astype(BF16)


def weight_grad(turned, other_turned, grads, other_grads, tile, *after):
    half, slots = turned.shape
    width = grads[0].shape[1]
    return call(
        weight_kernel,
        width // tile,
        entire(turned, other_turned) + by_columns(tile, *grads, *other_grads),
        by_columns(tile, bf16(half, width))[0],
        [pltpu.VMEM((slots, tile), BF16)],
        after,
    )


def back_kernel(main_ref, grad_ref, near_ref, far_ref, back_ref, spare_ref, sum_ref, grads_ref):
    step = pl.program_id(0)
    half = near_ref.shape[0]
    main = main_ref.shape[0]

    @pl.when(step == 0)
    def _():
        sum_ref[...] = jnp.zeros_like(sum_ref)

    stack_grads(main_ref, grad_ref, grads_ref)
    sum_ref[:, :half] += dot(grads_ref[...], near_ref[...], 1, 1)
    sum_ref[:, half:] += dot(grads_ref[...], far_ref[...], 1, 1)

    @pl.when(step == pl.num_programs(0) - 1)
    def _():
        core = lax.axis_index("dp")
        for at, which in ((0, core), (half, 1 - core)):
            start = pl.multiple_of(which * half, LANES)
            total = sum_ref[:, at : at + half].astype(BF16)
            back_ref[:, pl.ds(start, half)] = total
            spare_ref[:, pl.ds(start, half)] = total[main:]


def project_back(grads_main, grads_spare, near, far, tile, *after):
    main, width = grads_main.shape
    spare = grads_spare.shape[0]
    half = near.shape[0]
    slots = main + spare
    return call(
        back_kernel,
        width // tile,
        by_columns(tile, grads_main, grads_spare, near, far),
        entire(bf16(slots, 2 * half), bf16(spare, 2 * half)),
        [pltpu.VMEM((slots, 2 * half), F32), pltpu.VMEM((slots, tile), BF16)],
        after,
        cost=BACK_COST,
    )


def place_kernel(back_ref, spare_ref, out_ref):
    out_ref[...] = spare_ref[...]


def with_spare(back, back_spare, *after):
    slots, hid = back.shape
    spare = back_spare.shape[0]
    last = pl.BlockSpec((spare, hid), lambda step: (slots // spare - 1, 0))
    ins = [(back, anywhere())] + entire(back_spare)
    return call(place_kernel, 1, ins, (bf16(slots, hid), last), (), after, {0: 0})


def local(hidden_saved, down_weight, route_device, replica_flag, gate_values, grad_out):
    count = lax.axis_size("expert")
    half = count // 2
    tok, top = route_device.shape
    width = grad_out.shape[1]
    cap = 5 * tok * top // (4 * count)
    main = 3 * tok * top // 4
    hidden = hidden_saved[0, 0]
    near = down_weight[0]
    slots = hidden.shape[0]
    tile = width // 2
    groups = [list(range(half)), list(range(half, count))]

    def to_half(rows):
        return lax.all_to_all(
            rows.reshape(half, cap, width), "expert", 0, 0, axis_index_groups=groups, tiled=True
        ).reshape(half * cap, width)

    far = swapped(near, "dp", 1)
    meta, spare_hidden = head(
        route_device.T, replica_flag.T, gate_values.T, hidden, slots - main, count
    )
    spare_hidden = swapped(spare_hidden, "expert", half)
    metas = lax.all_to_all(meta, "expert", 0, 0, tiled=True)
    size = count // 4
    turned_blocks = size == 4
    place_of = lambda plane, index: plane * size + index
    across = [(d, place_of(d // size ^ 1, d % size)) for d in range(count)]
    neighbour = lax.ppermute(touched(copied(grad_out, tile), spare_hidden, metas), "expert", across)
    out_spare = project_spare(spare_hidden, near, far, tile)
    plans = plan(metas, cap, half, main, slots, turned_blocks)
    sel, gate, mix_mirror, plane_sel, plane_gate, mix_own = plans[:6]
    give_own, take_own, give_mirror, take_mirror = plans[6:]
    blocks = 4 if turned_blocks else 1
    out_main, turned, far_turned = project(hidden, spare_hidden, near, far, tile, out_spare)
    given_main = give_main(give_mirror, out_main, tile)
    packed_own = pack_plane(plane_sel, plane_gate, grad_out, neighbour, blocks, tile, given_main)
    if turned_blocks:
        ways = [[(d, d // size * size + (d % size ^ way)) for d in range(count)] for way in range(blocks)]
        arrived_own = [packed_own[0]]
        arrived_own += [lax.ppermute(packed_own[way], "expert", ways[way]) for way in range(1, blocks)]
    else:
        planes = [[place_of(plane, index) for index in range(size)] for plane in range(4)]
        rows = packed_own[0].reshape(size, 2 * cap, width)
        rows = lax.all_to_all(rows, "expert", 0, 0, axis_index_groups=planes, tiled=True)
        arrived_own = [rows.reshape(half * cap, width)]
    out_spare = swapped(out_spare, "expert", half)
    mirror = swapped(touched(copied(grad_out, tile, meta), out_main, packed_own[0]), "expert", half)
    other_turned = swapped(far_turned, "dp", 1)
    given_mirror = give_rest(give_mirror, given_main, out_spare, tile, GIVE_COST)
    returned_mirror = to_half(given_mirror)
    packed_mirror = pack(sel, gate, mirror, tile, *arrived_own[1:2])
    given_own = give(give_own, out_main, out_spare, tile, 0, packed_mirror)
    arrived_mirror = to_half(touched(packed_mirror, returned_mirror, given_own))
    part = swapped(combine(mix_mirror, returned_mirror, [], tile), "expert", half)
    arrived = (take_own, take_mirror, arrived_mirror, arrived_own)
    grads_spare = take(*arrived, main, slots - main, tile)
    returned_own = to_half(touched(given_own, part, grads_spare))
    grads_main = take(*arrived, 0, main, tile, grads_spare)
    other_main = swapped(grads_main, "dp", 1)
    grads_spare = swapped(grads_spare, "expert", half)
    other_spare = swapped(grads_spare, "dp", 1)
    layer_out = combine(mix_own, returned_own, [part], tile)
    back, back_spare = project_back(grads_main, grads_spare, near, far, tile)
    back_spare = swapped(back_spare, "expert", half)
    grad_weight = weight_grad(
        turned, other_turned, (grads_main, grads_spare), (other_main, other_spare), tile, back
    )
    grad_hidden = with_spare(back, back_spare, grad_weight)
    return (layer_out, grad_hidden[None, None], grad_weight[None])


def solution(mesh):
    in_specs = (
        P("dp", "expert", None, None),
        P("expert", "dp", None),
        P(("dp", "expert"), None),
        P(("dp", "expert"), None),
        P(("dp", "expert"), None),
        P(("dp", "expert"), None),
    )
    out_specs = (P(("dp", "expert"), None), P("dp", "expert", None, None), P("expert", "dp", None))
    return jax.shard_map(local, mesh=mesh, in_specs=in_specs, out_specs=out_specs, check_vma=False)
```

```python
import functools
import jax
import jax.numpy as jnp
from jax import lax
from jax.experimental import pallas as pl
from jax.experimental.pallas import tpu as pltpu
from jax.sharding import PartitionSpec as P

F32, BF16, I32 = jnp.float32, jnp.bfloat16, jnp.int32
LANES = 128
LONG = 4_000_000_000_000
GIVE_COST = 10_000_000_000
BACK_COST = 40_000_000_000
VMEM_LIMIT = 64 * 1024 * 1024 - 65536


def swapped(value, axis, distance):
    count = lax.axis_size(axis)
    pairs = [(source, (source + distance) % count) for source in range(count)]
    return lax.ppermute(value, axis, pairs)


def dot(left, right, left_dim=1, right_dim=0):
    contract = (((left_dim,), (right_dim,)), ((), ()))
    return lax.dot_general(left, right, contract, preferred_element_type=F32)


def iota(shape, dim):
    return lax.broadcasted_iota(I32, shape, dim).astype(F32)


def row_of(rows, cap, lanes):
    row = iota((rows, lanes), 0)
    group = jnp.floor((row + 0.5) * (1.0 / cap))
    return group, row - group * cap


def before_mask(size):
    return (iota((size, size), 0) < iota((size, size), 1)).astype(BF16)


def bf16(*shape):
    return jax.ShapeDtypeStruct(shape, BF16)


def f32(*shape):
    return jax.ShapeDtypeStruct(shape, F32)


def call(body, grid, ins, outs, scratch=(), after=(), alias=None, cost=0):
    single = not isinstance(outs, list)
    pairs = [outs] if single else outs
    specs = [spec for _, spec in pairs]
    shapes = [shape for shape, _ in pairs]
    count = len(ins)

    def kernel(*refs):
        body(*refs[:count], *refs[count + len(after) :])

    return pl.pallas_call(
        kernel,
        grid=(grid,),
        in_specs=[spec for _, spec in ins] + [anywhere()] * len(after),
        out_specs=specs[0] if single else specs,
        out_shape=shapes[0] if single else shapes,
        scratch_shapes=list(scratch),
        input_output_aliases=alias or {},
        compiler_params=pltpu.CompilerParams(vmem_limit_bytes=VMEM_LIMIT),
        cost_estimate=pl.CostEstimate(flops=cost, bytes_accessed=0, transcendentals=0),
    )(*[array for array, _ in ins], *after)


def anywhere():
    return pl.BlockSpec(memory_space=pl.ANY)


def whole(array):
    return pl.BlockSpec(array.shape, lambda step: (0,) * len(array.shape))


def columns(array, tile):
    return pl.BlockSpec((array.shape[0], tile), lambda step: (0, step))


def entire(*arrays):
    return [(array, whole(array)) for array in arrays]


def by_columns(tile, *arrays):
    return [(array, columns(array, tile)) for array in arrays]


def head_kernel(device_ref, flag_ref, gate_ref, hidden_ref, meta_ref, spare_ref):
    top = device_ref.shape[0]
    codes = (device_ref[...] * 2 + flag_ref[...]).astype(F32)
    count = meta_ref.shape[0]
    meta_ref[:, :top, :] = jnp.broadcast_to(codes[None], (count, *codes.shape))
    meta_ref[:, top:, :] = jnp.broadcast_to(gate_ref[...][None], (count, *codes.shape))
    spare_ref[...] = hidden_ref[...]


def head(devices, flags, gates, hidden, spare, count):
    top, tok = devices.shape
    slots, hid = hidden.shape
    last = pl.BlockSpec((spare, hid), lambda step: (slots // spare - 1, 0))
    outs = entire(f32(count, 2 * top, tok), bf16(spare, hid))
    return call(head_kernel, 1, entire(devices, flags, gates) + [(hidden, last)], outs)


def copy_kernel(source_ref, target_ref):
    target_ref[...] = source_ref[...]


def copied(array, tile, *after):
    ins, outs = by_columns(tile, array), by_columns(tile, bf16(*array.shape))[0]
    return call(copy_kernel, array.shape[1] // tile, ins, outs, (), after)


def touch_kernel(source_ref, target_ref):
    pass


def touched(array, *after):
    shape = jax.ShapeDtypeStruct(array.shape, array.dtype)
    return call(touch_kernel, 1, [(array, anywhere())], (shape, anywhere()), (), after, {0: 0})


def plan_rows(meta, cap, half, sel_ref, gate_ref, mix_ref):
    rows, tok = sel_ref.shape
    top = meta.shape[0] // 2
    me = lax.axis_index("expert")
    first = (lax.div(me, half) * half).astype(F32)
    dest = iota((LANES, tok), 0)
    inside = dest < half
    dest = dest + first
    hit = jnp.zeros((LANES, tok), F32)
    gate = jnp.zeros((LANES, tok), F32)
    for k in range(top):
        device = jnp.floor(meta[k : k + 1] * 0.5)
        named = (dest == device) & inside
        hit = jnp.where(named, 1.0, hit)
        gate = jnp.where(named, meta[top + k : top + k + 1], gate)
    place = dot(hit.astype(BF16), before_mask(tok))
    place = jnp.where(hit > 0.5, place, -1.0)
    group, at = row_of(rows, cap, LANES)
    spread = (iota((rows, LANES), 1) == group).astype(BF16)
    to_rows = lambda table: dot(spread, table.astype(BF16))
    chosen = jnp.where(to_rows(place) == at, 1.0, jnp.zeros((rows, tok), F32))
    high = gate.astype(BF16).astype(F32)
    mid = (gate - high).astype(BF16).astype(F32)
    low = gate - high - mid
    high, mid, low = to_rows(high), to_rows(mid), to_rows(low)
    scale = jnp.sum(chosen * (high + mid + low), axis=1, keepdims=True)
    sel_ref[...] = chosen.astype(BF16)
    gate_ref[...] = jnp.broadcast_to(scale, (rows, LANES))
    mix_ref[:tok] = (chosen * high).T.astype(BF16)
    mix_ref[tok:] = (chosen * mid).T.astype(BF16)


def packed_rows(sel_ref, gate_ref, tokens_ref, packed_ref):
    packed_ref[...] = (dot(sel_ref[...], tokens_ref[...]) * gate_ref[:, :1]).astype(BF16)


def pack_own_kernel(cap, half, meta_ref, tokens_ref, packed_ref, mix_ref, sel_ref, gate_ref):
    @pl.when(pl.program_id(0) == 0)
    def _():
        plan_rows(meta_ref[0], cap, half, sel_ref, gate_ref, mix_ref)

    packed_rows(sel_ref, gate_ref, tokens_ref, packed_ref)


def pack_own(meta, tokens, cap, half, tile, *after):
    tok, width = tokens.shape
    rows = half * cap
    first = pl.BlockSpec((1, *meta.shape[1:]), lambda step: (0, 0, 0))
    return call(
        functools.partial(pack_own_kernel, cap, half),
        width // tile,
        [(meta, first)] + by_columns(tile, tokens),
        by_columns(tile, bf16(rows, width)) + entire(bf16(2 * tok, rows)),
        [pltpu.VMEM((rows, tok), BF16), pltpu.VMEM((rows, LANES), F32)],
        after,
    )


def pack(sel, gate, tokens, tile, *after):
    rows, width = sel.shape[0], tokens.shape[1]
    return call(
        packed_rows,
        width // tile,
        entire(sel, gate) + by_columns(tile, tokens),
        by_columns(tile, bf16(rows, width))[0],
        after=after,
        cost=LONG,
    )


def plan_kernel(cap, half, main, metas_ref, sel_ref, gate_ref, mix_ref, *slot_refs):
    count, tops, tok = metas_ref.shape
    top = tops // 2
    rows, slots = slot_refs[0].shape
    spare = slots - main
    me = lax.axis_index("expert")
    mirror = lax.rem(me + half, count)
    plan_rows(metas_ref[mirror], cap, half, sel_ref, gate_ref, mix_ref)

    mine, other = me.astype(F32), mirror.astype(F32)
    none = jnp.zeros((count, tok), F32)
    here, flag, clash = none, none, none
    for k in range(top):
        code = metas_ref[:, k, :]
        device = jnp.floor(code * 0.5)
        here = jnp.where(device == mine, 1.0, here)
        flag = jnp.where(device == mine, code - 2.0 * device, flag)
        clash = jnp.where(device == other, 1.0, clash)
    at_spare = here * flag * (1.0 - clash)
    at_main = here - at_spare
    before = before_mask(tok)
    ones = jnp.ones((tok, LANES), BF16)
    lower = (iota((count, count), 1) < iota((count, count), 0)).astype(BF16)

    def rank(flags):
        flags = flags.astype(BF16)
        return dot(flags, before) + dot(lower, dot(flags, ones).astype(BF16))

    rank_main, rank_spare = rank(at_main), rank(at_spare)
    slot = jnp.where((at_main > 0.5) & (rank_main < main), rank_main + 1.0, none)
    slot = jnp.where((at_spare > 0.5) & (rank_spare < spare), rank_spare + (main + 1.0), slot)
    place = jnp.where(here > 0.5, dot(here.astype(BF16), before), -1.0).astype(BF16)
    tens = jnp.floor(slot * (1.0 / 32.0))
    units = (slot - tens * 32.0).astype(BF16)
    tens = tens.astype(BF16)
    group, _ = row_of(rows, cap, count)
    _, at = row_of(rows, cap, tok)
    start = lax.div(me, half) * half
    for side, base in enumerate((start, lax.rem(start + half, count))):
        spread = (iota((rows, count), 1) == group + base.astype(F32)).astype(BF16)
        chosen = dot(spread, place) == at
        number = dot(spread, tens) * 32.0 + dot(spread, units)
        number = jnp.sum(jnp.where(chosen, number, 0.0), axis=1, keepdims=True)
        give_ref, take_ref = slot_refs[2 * side : 2 * side + 2]
        give_ref[...] = (iota((rows, slots), 1) + 1.0 == number).astype(BF16)
        number = jnp.broadcast_to(number, (rows, LANES)).T[0:1]
        take_ref[...] = (iota((slots, rows), 0) + 1.0 == number).astype(BF16)


def plan(metas, cap, half, main, slots):
    tok = metas.shape[2]
    rows = half * cap
    sides = [bf16(rows, slots), bf16(slots, rows)] * 2
    outs = entire(bf16(rows, tok), f32(rows, LANES), bf16(2 * tok, rows), *sides)
    return call(functools.partial(plan_kernel, cap, half, main), 1, entire(metas), outs)


def side_by_side(source, target_ref):
    half = target_ref.shape[1] // 2
    core = lax.axis_index("dp")
    for at, which in ((0, core), (half, 1 - core)):
        start = pl.multiple_of(which * half, LANES)
        target_ref[:, at : at + half] = source[: target_ref.shape[0], pl.ds(start, half)]


def projected(stack_ref, near_ref, far_ref, out_ref):
    half = near_ref.shape[0]
    total = dot(stack_ref[:, :half], near_ref[...]) + dot(stack_ref[:, half:], far_ref[...])
    out_ref[...] = total.astype(BF16)


def project_spare_kernel(spare_ref, near_ref, far_ref, out_ref, stack_ref):
    @pl.when(pl.program_id(0) == 0)
    def _():
        side_by_side(spare_ref, stack_ref)

    projected(stack_ref, near_ref, far_ref, out_ref)


def project_spare(spare_hidden, near, far, tile, *after):
    width = near.shape[1]
    return call(
        project_spare_kernel,
        width // tile,
        entire(spare_hidden) + by_columns(tile, near, far),
        by_columns(tile, bf16(spare_hidden.shape[0], width))[0],
        [pltpu.VMEM(spare_hidden.shape, BF16)],
        after,
    )


def project_kernel(hidden_ref, spare_ref, near_ref, far_ref, out_ref, near_turned, far_turned, stack_ref, side_ref):
    main, half = out_ref.shape[0], near_ref.shape[0]

    @pl.when(pl.program_id(0) == 0)
    def _():
        side_by_side(hidden_ref, stack_ref)
        side_by_side(spare_ref, side_ref)
        for at, turned_ref in ((0, near_turned), (half, far_turned)):
            turned_ref[:, :main] = stack_ref[:, at : at + half].T
            turned_ref[:, main:] = side_ref[:, at : at + half].T

    projected(stack_ref, near_ref, far_ref, out_ref)


def project(hidden, spare_hidden, near, far, tile, *after):
    half, width = near.shape
    spare = spare_hidden.shape[0]
    slots, hid = hidden.shape
    turned = [bf16(half, slots), bf16(half, slots)]
    return call(
        project_kernel,
        width // tile,
        entire(hidden, spare_hidden) + by_columns(tile, near, far),
        by_columns(tile, bf16(slots - spare, width)) + entire(*turned),
        [pltpu.VMEM((slots - spare, hid), BF16), pltpu.VMEM((spare, hid), BF16)],
        after,
    )


def give_kernel(slot_ref, main_ref, spare_ref, out_ref):
    main = main_ref.shape[0]
    packed = dot(slot_ref[:, :main], main_ref[...]) + dot(slot_ref[:, main:], spare_ref[...])
    out_ref[...] = packed.astype(BF16)


def give(slot, out_main, out_spare, tile, cost, *after):
    rows, width = slot.shape[0], out_main.shape[1]
    return call(
        give_kernel,
        width // tile,
        entire(slot) + by_columns(tile, out_main, out_spare),
        by_columns(tile, bf16(rows, width))[0],
        after=after,
        cost=cost,
    )


def give_main_kernel(slot_ref, main_ref, out_ref):
    out_ref[...] = dot(slot_ref[:, : main_ref.shape[0]], main_ref[...]).astype(BF16)


def give_main(slot, out_main, tile):
    rows, width = slot.shape[0], out_main.shape[1]
    return call(
        give_main_kernel,
        width // tile,
        entire(slot) + by_columns(tile, out_main),
        by_columns(tile, bf16(rows, width))[0],
    )


def give_rest_kernel(slot_ref, given_ref, spare_ref, out_ref):
    rest = dot(slot_ref[:, slot_ref.shape[1] - spare_ref.shape[0] :], spare_ref[...])
    out_ref[...] = given_ref[...] + rest.astype(BF16)


def give_rest(slot, given, out_spare, tile, cost):
    return call(
        give_rest_kernel,
        given.shape[1] // tile,
        entire(slot) + by_columns(tile, given, out_spare),
        by_columns(tile, bf16(*given.shape))[0],
        cost=cost,
    )


def take_kernel(first, own_slot, mirror_slot, own_ref, mirror_ref, out_ref):
    rows = pl.ds(first, out_ref.shape[0])
    total = dot(own_slot[rows, :], own_ref[...]) + dot(mirror_slot[rows, :], mirror_ref[...])
    out_ref[...] = total.astype(BF16)


def take(own_slot, mirror_slot, own, mirror, first, count, tile, *after):
    return call(
        functools.partial(take_kernel, first),
        own.shape[1] // tile,
        entire(own_slot, mirror_slot) + by_columns(tile, own, mirror),
        by_columns(tile, bf16(count, own.shape[1]))[0],
        after=after,
    )


def mixed(mix_ref, rows_ref):
    both = dot(mix_ref[...], rows_ref[...])
    tok = both.shape[0] // 2
    return both[:tok] + both[tok:]


def part_kernel(mix_ref, rows_ref, part_ref):
    part_ref[...] = mixed(mix_ref, rows_ref).astype(BF16)


def total_kernel(mix_ref, rows_ref, other_ref, total_ref):
    total_ref[...] = (mixed(mix_ref, rows_ref) + other_ref[...].astype(F32)).astype(BF16)


def combine(mix, rows, others, tile, *after):
    width = rows.shape[1]
    return call(
        total_kernel if others else part_kernel,
        width // tile,
        entire(mix) + by_columns(tile, rows, *others),
        by_columns(tile, bf16(mix.shape[0] // 2, width))[0],
        after=after,
    )


def stack_grads(main_ref, spare_ref, grads_ref):
    main = main_ref.shape[0]
    grads_ref[:main] = main_ref[...]
    grads_ref[main:] = spare_ref[...]


def weight_kernel(turned, other_turned, main_ref, spare_ref, other_main, other_spare, out_ref, grads_ref):
    stack_grads(main_ref, spare_ref, grads_ref)
    total = dot(turned[...], grads_ref[...])
    stack_grads(other_main, other_spare, grads_ref)
    out_ref[...] = (total + dot(other_turned[...], grads_ref[...])).astype(BF16)


def weight_grad(turned, other_turned, grads, other_grads, tile, *after):
    half, slots = turned.shape
    width = grads[0].shape[1]
    return call(
        weight_kernel,
        width // tile,
        entire(turned, other_turned) + by_columns(tile, *grads, *other_grads),
        by_columns(tile, bf16(half, width))[0],
        [pltpu.VMEM((slots, tile), BF16)],
        after,
    )


def back_kernel(main_ref, grad_ref, near_ref, far_ref, back_ref, spare_ref, sum_ref, grads_ref):
    step = pl.program_id(0)
    half = near_ref.shape[0]
    main = main_ref.shape[0]

    @pl.when(step == 0)
    def _():
        sum_ref[...] = jnp.zeros_like(sum_ref)

    stack_grads(main_ref, grad_ref, grads_ref)
    sum_ref[:, :half] += dot(grads_ref[...], near_ref[...], 1, 1)
    sum_ref[:, half:] += dot(grads_ref[...], far_ref[...], 1, 1)

    @pl.when(step == pl.num_programs(0) - 1)
    def _():
        core = lax.axis_index("dp")
        for at, which in ((0, core), (half, 1 - core)):
            start = pl.multiple_of(which * half, LANES)
            total = sum_ref[:, at : at + half].astype(BF16)
            back_ref[:, pl.ds(start, half)] = total
            spare_ref[:, pl.ds(start, half)] = total[main:]


def project_back(grads_main, grads_spare, near, far, tile, *after):
    main, width = grads_main.shape
    spare = grads_spare.shape[0]
    half = near.shape[0]
    slots = main + spare
    return call(
        back_kernel,
        width // tile,
        by_columns(tile, grads_main, grads_spare, near, far),
        entire(bf16(slots, 2 * half), bf16(spare, 2 * half)),
        [pltpu.VMEM((slots, 2 * half), F32), pltpu.VMEM((slots, tile), BF16)],
        after,
        cost=BACK_COST,
    )


def place_kernel(back_ref, spare_ref, out_ref):
    out_ref[...] = spare_ref[...]


def with_spare(back, back_spare, *after):
    slots, hid = back.shape
    spare = back_spare.shape[0]
    last = pl.BlockSpec((spare, hid), lambda step: (slots // spare - 1, 0))
    ins = [(back, anywhere())] + entire(back_spare)
    return call(place_kernel, 1, ins, (bf16(slots, hid), last), (), after, {0: 0})


def local(hidden_saved, down_weight, route_device, replica_flag, gate_values, grad_out):
    count = lax.axis_size("expert")
    half = count // 2
    tok, top = route_device.shape
    width = grad_out.shape[1]
    cap = 5 * tok * top // (4 * count)
    main = 3 * tok * top // 4
    hidden = hidden_saved[0, 0]
    near = down_weight[0]
    slots = hidden.shape[0]
    tile = width // 2
    groups = [list(range(half)), list(range(half, count))]

    def to_half(rows):
        return lax.all_to_all(
            rows.reshape(half, cap, width), "expert", 0, 0, axis_index_groups=groups, tiled=True
        ).reshape(half * cap, width)

    far = swapped(near, "dp", 1)
    meta, spare_hidden = head(
        route_device.T, replica_flag.T, gate_values.T, hidden, slots - main, count
    )
    spare_hidden = swapped(spare_hidden, "expert", half)
    metas = lax.all_to_all(meta, "expert", 0, 0, tiled=True)
    packed_own, mix_own = pack_own(meta, grad_out, cap, half, tile)
    out_spare = project_spare(spare_hidden, near, far, tile, mix_own)
    arrived_own = to_half(touched(packed_own, metas, out_spare))
    sel, gate, mix_mirror, give_own, take_own, give_mirror, take_mirror = plan(
        metas, cap, half, main, slots
    )
    out_main, turned, far_turned = project(hidden, spare_hidden, near, far, tile, out_spare)
    out_spare = swapped(out_spare, "expert", half)
    given_main = give_main(give_mirror, out_main, tile)
    mirror = swapped(touched(copied(grad_out, tile), out_main, sel), "expert", half)
    other_turned = swapped(far_turned, "dp", 1)
    given_mirror = give_rest(give_mirror, given_main, out_spare, tile, GIVE_COST)
    returned_mirror = to_half(touched(given_mirror, arrived_own))
    packed_mirror = pack(sel, gate, mirror, tile)
    given_own = give(give_own, out_main, out_spare, tile, 0, packed_mirror)
    arrived_mirror = to_half(touched(packed_mirror, returned_mirror, given_own))
    part = swapped(combine(mix_mirror, returned_mirror, [], tile), "expert", half)
    arrived = (take_own, take_mirror, arrived_own, arrived_mirror)
    grads_spare = take(*arrived, main, slots - main, tile)
    returned_own = to_half(touched(given_own, part, grads_spare))
    grads_main = take(*arrived, 0, main, tile, grads_spare)
    other_main = swapped(grads_main, "dp", 1)
    grads_spare = swapped(grads_spare, "expert", half)
    other_spare = swapped(grads_spare, "dp", 1)
    layer_out = combine(mix_own, returned_own, [part], tile)
    back, back_spare = project_back(grads_main, grads_spare, near, far, tile)
    back_spare = swapped(back_spare, "expert", half)
    grad_weight = weight_grad(
        turned, other_turned, (grads_main, grads_spare), (other_main, other_spare), tile, back
    )
    grad_hidden = with_spare(back, back_spare, grad_weight)
    return (layer_out, grad_hidden[None, None], grad_weight[None])


def solution(mesh):
    in_specs = (
        P("dp", "expert", None, None),
        P("expert", "dp", None),
        P(("dp", "expert"), None),
        P(("dp", "expert"), None),
        P(("dp", "expert"), None),
        P(("dp", "expert"), None),
    )
    out_specs = (P(("dp", "expert"), None), P("dp", "expert", None, None), P("expert", "dp", None))
    return jax.shard_map(local, mesh=mesh, in_specs=in_specs, out_specs=out_specs, check_vma=False)
```
